32 devices in a mesh: scan: 16 (over z, y, x), mode: 2 (over core).
Axes of the slice: x: 2, y: 2, z: 4, core: 2. Of those that a mesh axis runs over, the one named last changes fastest.
Arguments:
- object_field: float32 [2, 640, 1152], P(None, 'scan'), may hold values from -4.5 to 4.5
- probe: float32 [8, 2, 512, 512], P('mode'), may hold values from -1.5 to 1.5
- amplitude: float32 [16, 512, 512], P('scan'), may hold values from 0.2 to 1.8
- pos_row: int32 [16], P('scan'), may hold values from 0 to 128, as said below
- pos_col: int32 [16], P('scan'), may hold values from 0 to 640, as said below
- strip_of: int32 [16], P('scan'), may hold values from 0 to 15, each once
Outputs:
- object_grad: float32 [2, 640, 1152], P(None, 'scan')
- probe_grad: float32 [8, 2, 512, 512], P('mode')
The draws below stay inside these ranges and needn't reach their ends.
Inputs may be any that keep to these rules, and one draw needn't show every extreme that they name: Pattern p covers object rows pos_row[p] to pos_row[p] + 511; the smallest and the largest allowed value both occur. Pattern p covers object columns pos_col[p] to pos_col[p] + 511; the smallest and the largest allowed value both occur.
All inputs are finite; a program needn't handle non-finite values.
Results may differ from the reference program's by a relative error of at most 0.0055.
The reference program's roundings to bfloat16 on the way count: a program that leaves them out, or rounds other values in their place, can miss the bound.
Values may be sent and summed in bfloat16 or wider, within the bound.
A program may use at most 128 MiB of HBM per device.

```python
import math
import jax
import jax.numpy as jnp
from jax import lax

PROBE = 512
MODES = 8
COLS = 1152
STRIP = 40
PATTERNS = 16
TILES = 16
OBJ_ROWS = 640


def pinned_offsets(key, count_all, upper_bound):
    first_key, second_key, third_key = jax.random.split(key, 3)
    values = jax.random.randint(first_key, (count_all,), 0, upper_bound + 1, dtype=jnp.int32)
    low_slot = jax.random.randint(second_key, (), 0, count_all, dtype=jnp.int32)
    shift_by = jax.random.randint(third_key, (), 1, count_all, dtype=jnp.int32)
    high_slot = (low_slot + shift_by) % count_all
    slots = jnp.arange(count_all, dtype=jnp.int32)
    values = jnp.where(slots == low_slot, 0, values)
    return jnp.where(slots == high_slot, upper_bound, values).astype(jnp.int32)


def draw_pos_row(key, part):
    return pinned_offsets(jax.random.fold_in(key, 11), PATTERNS, OBJ_ROWS - PROBE)


def draw_pos_col(key, part):
    return pinned_offsets(jax.random.fold_in(key, 23), PATTERNS, COLS - PROBE)


def shard_levels(key, shape, cuts, low, largest):
    level = 1.0
    for position, shards_of in cuts:
        draws = jax.random.uniform(jax.random.fold_in(jax.random.fold_in(key, 6), position), (shards_of,), jnp.float32, low / len(cuts), largest / len(cuts))
        level = level * jnp.repeat(jnp.exp(draws), shape[position] // shards_of).reshape((-1,) + (1,) * (len(shape) - 1 - position))
    return level


def centred(own_key, extent, spread, reach, cuts=(), kind=jnp.bfloat16):
    loudness = shard_levels(own_key, extent, cuts, -0.22, 0.18) if cuts else 1.0
    values = jax.random.normal(own_key, extent, jnp.float32) * spread * loudness
    return jnp.minimum(jnp.maximum(values, -reach), reach).astype(kind)


def setup_inputs(seed: int = 0) -> dict:
    keys = jax.random.split(jax.random.key(seed), 7)
    object_field = centred(keys[0], (2, OBJ_ROWS, COLS), 0.7, 4.5, ((1, 16),), jnp.float32)
    probe = centred(keys[1], (MODES, 2, PROBE, PROBE), 0.25, 1.5, ((0, 2),), jnp.float32)
    amplitude = jnp.clip(0.2 + 1.5999999 * jax.random.uniform(keys[2], (PATTERNS, PROBE, PROBE), jnp.float32) ** shard_levels(keys[2], (PATTERNS, PROBE, PROBE), ((0, 16),), -0.2, 0.2), 0.2, 1.8)
    pos_row = draw_pos_row(jax.random.fold_in(keys[6], 71), 0)
    pos_col = draw_pos_col(jax.random.fold_in(keys[6], 71), 0)
    strip_of = jax.random.permutation(keys[5], TILES).astype(jnp.int32)
    return {"object_field": object_field, "probe": probe, "amplitude": amplitude, "pos_row": pos_row, "pos_col": pos_col, "strip_of": strip_of}


def dft_table(sign_factor):
    positions = jnp.arange(PROBE, dtype=jnp.int32)
    products = positions[:, None] * positions[None, :] % PROBE
    angle_table = products.astype(jnp.float32) * (2.0 * math.pi / PROBE)
    norm_scale = 1.0 / math.sqrt(PROBE)
    cosine = jnp.cos(angle_table) * norm_scale
    sine_part = jnp.sin(angle_table) * (sign_factor * norm_scale)
    table_half = jnp.stack([jnp.stack([cosine, sine_part]), jnp.stack([-sine_part, cosine])]).astype(jnp.bfloat16)
    return lax.optimization_barrier(table_half)

def transform(field_wave, matrix_table):
    table_wide = matrix_table.astype(jnp.float32)
    half_wave = jnp.einsum('oiab,mibx->moax', table_wide, field_wave.astype(jnp.float32))
    half_wave = lax.optimization_barrier(half_wave.astype(jnp.bfloat16))
    return jnp.einsum('miax,oixy->moay', half_wave.astype(jnp.float32), table_wide)

def reference(object_field, probe, amplitude, pos_row, pos_col, strip_of):
    forward = dft_table(1.0)
    inverse = dft_table(-1.0)
    held_strips = object_field.reshape(2, TILES, STRIP, COLS)
    window_field = jnp.zeros_like(held_strips).at[:, strip_of].set(held_strips).reshape(2, OBJ_ROWS, COLS)
    probe_re = probe[:, 0]
    probe_im = probe[:, 1]
    zero_index = jnp.zeros((), jnp.int32)

    def one_pattern(carry, inputs):
        window_grad, probe_grad = carry
        row_start, col_start, measured = inputs
        start = (zero_index, row_start.astype(jnp.int32), col_start.astype(jnp.int32))
        patch_half = lax.optimization_barrier(lax.dynamic_slice(window_field, start, (2, PROBE, PROBE)).astype(jnp.bfloat16))
        patch_wide = patch_half.astype(jnp.float32)
        patch_re = patch_wide[0]
        patch_im = patch_wide[1]
        exit_re = probe_re * patch_re - probe_im * patch_im
        exit_im = probe_re * patch_im + probe_im * patch_re
        exit_wave = lax.optimization_barrier(jnp.stack([exit_re, exit_im], axis=1).astype(jnp.bfloat16))
        far_field = transform(exit_wave, forward)
        intensity = lax.optimization_barrier(jnp.sum(far_field[:, 0] * far_field[:, 0] + far_field[:, 1] * far_field[:, 1], axis=0))
        scale_factor = 1.0 - measured / jnp.sqrt(jnp.maximum(intensity, 0.25))
        residual_wave = lax.optimization_barrier((far_field * scale_factor).astype(jnp.bfloat16))
        back_wave = transform(residual_wave, inverse)
        back_re = back_wave[:, 0]
        back_im = back_wave[:, 1]
        grad_re = lax.optimization_barrier(jnp.sum(probe_re * back_re + probe_im * back_im, axis=0))
        grad_im = lax.optimization_barrier(jnp.sum(probe_re * back_im - probe_im * back_re, axis=0))
        current = lax.dynamic_slice(window_grad, start, (2, PROBE, PROBE))
        window_grad = lax.dynamic_update_slice(window_grad, current + jnp.stack([grad_re, grad_im]), start)
        term_re = patch_re * back_re + patch_im * back_im
        term_im = patch_re * back_im - patch_im * back_re
        probe_grad = probe_grad + jnp.stack([term_re, term_im], axis=1)
        return ((window_grad, probe_grad), None)
    initial = (jnp.zeros((2, OBJ_ROWS, COLS), jnp.float32), jnp.zeros((MODES, 2, PROBE, PROBE), jnp.float32))
    (window_grad, probe_grad), _ = lax.scan(one_pattern, initial, (pos_row, pos_col, amplitude))
    object_grad = window_grad.reshape(2, TILES, STRIP, COLS)[:, strip_of].reshape(2, OBJ_ROWS, COLS)
    return (object_grad, probe_grad)
```

```python
import math

import jax
import jax.numpy as jnp
import numpy as np
from jax import lax
from jax.experimental import pallas as pl
from jax.experimental.pallas import tpu as pltpu
from jax.sharding import PartitionSpec as P

F32 = jnp.float32
BF16 = jnp.bfloat16
LANES = 128
META = 8
PLANE = 4
TILE = 256
PARAMS = pltpu.CompilerParams(vmem_limit_bytes=56 * 1024 * 1024)
VMEM = pl.BlockSpec(memory_space=pltpu.VMEM)
SMEM = pl.BlockSpec(memory_space=pltpu.SMEM)
MESH = pl.DeviceIdType.MESH


def dft_tables(size):
    positions = np.arange(size, dtype=np.int32)
    angles = (positions[:, None] * positions[None, :] % size).astype(np.float32)
    angles = angles * np.float32(2.0 * math.pi / size)
    norm = np.float32(1.0 / math.sqrt(size))
    cosine, sine = np.cos(angles) * norm, np.sin(angles) * norm
    forward = np.block([[cosine, sine], [-sine, cosine]])
    inverse = np.block([[cosine, -sine], [sine, cosine]])
    return jnp.asarray(forward, BF16), jnp.asarray(inverse, BF16)


def gather_kernel(mine, out, line_send, line_recv, plane_send, plane_recv, swap_send, swap_recv):
    count = out.shape[1]
    lines = count // PLANE
    scan, mode = lax.axis_index("scan"), lax.axis_index("mode")
    line, place = scan // PLANE, lax.rem(scan, PLANE)
    in_line = [(lax.rem(line + k, lines) * PLANE + place, mode) for k in range(1, lines)]
    in_plane = [(line * PLANE + lax.rem(place + t, PLANE), mode) for t in range(1, PLANE)]
    partner = (scan, 1 - mode)

    barrier = pltpu.get_barrier_semaphore()
    for peer in in_line + in_plane + [partner]:
        pl.semaphore_signal(barrier, inc=1, device_id=peer, device_id_type=pl.DeviceIdType.MESH)
    pl.semaphore_wait(barrier, len(in_line) + len(in_plane) + 1)

    def push(src, dst, send, recv, peer):
        copy = pltpu.make_async_remote_copy(
            src_ref=src,
            dst_ref=dst,
            send_sem=send,
            recv_sem=recv,
            device_id=peer,
            device_id_type=pl.DeviceIdType.MESH,
        )
        copy.start()
        return copy

    own = out.at[mode, scan]
    line_copies = [
        push(mine, own, line_send.at[k], line_recv.at[k], peer) for k, peer in enumerate(in_line)
    ]
    plane_copies = [
        push(mine, own, plane_send.at[0, t], plane_recv.at[0, t], peer) for t, peer in enumerate(in_plane)
    ]
    out[mode, scan] = mine[...]
    for k, arriving in enumerate(line_copies):
        arriving.wait_recv()
        piece = out.at[mode, lax.rem(line + lines - k - 1, lines) * PLANE + place]
        plane_copies += [
            push(piece, piece, plane_send.at[k + 1, t], plane_recv.at[k + 1, t], peer)
            for t, peer in enumerate(in_plane)
        ]
    for copy in plane_copies:
        copy.wait_recv()
    last = push(out.at[mode], out.at[mode], swap_send, swap_recv, partner)
    for copy in line_copies + plane_copies:
        copy.wait_send()
    last.wait()


def cut_kernel(strips, row, col, held, patch, window):
    count, rows = held.shape[1], held.shape[2] - META
    size, cols = patch.shape[-1], held.shape[-1]
    wide = size + LANES

    def place(j, carry):
        at = pl.ds(pl.multiple_of(strips[j] * rows, 8), rows)
        for c in range(2):
            window[c, at, :cols] = held[c, j].astype(F32)[:rows]
        return carry

    lax.fori_loop(0, count, place, 0)
    across = pl.ds(pl.multiple_of(col[0] // LANES * LANES, LANES), wide)
    back = lax.rem(wide - lax.rem(col[0], LANES), wide)
    up = lax.rem(72 - lax.rem(row[0], 8), 72)
    for c in range(2):

        def cut(i, carry, c=c):
            block = window[c, pl.ds(pl.multiple_of(row[0] // 8 * 8 + i * 64, 8), 72), across]
            block = pltpu.roll(block, up, 0)[:64]
            patch[c, pl.ds(pl.multiple_of(i * 64, 64), 64), :] = pltpu.roll(block, back, 1)[:, :size]
            return carry

        lax.fori_loop(0, size // 64, cut, 0)


def forward_kernel(probe, patch, left, right, far, power, wave, half):
    size = patch.shape[-1]

    def leave(i, carry):
        at = pl.ds(pl.multiple_of(i * 64, 64), 64)
        low = pl.ds(pl.multiple_of(size + i * 64, 64), 64)
        pr, pi, xr, xi = probe[0, 0, at], probe[0, 1, at], patch[0, at], patch[1, at]
        wave[at] = (pr * xr - pi * xi).astype(BF16)
        wave[low] = (pr * xi + pi * xr).astype(BF16)
        return carry

    lax.fori_loop(0, size // 64, leave, 0)
    rows_product(left, wave, half)
    first = pl.program_id(0) == 0

    def across(i, carry):
        at = pl.ds(pl.multiple_of(i * TILE, TILE), TILE)
        both = jnp.dot(half[at], right[...], preferred_element_type=F32)
        re, im = both[:, :size], both[:, size:]
        far[0, 0, at] = re
        far[0, 1, at] = im
        here = re * re + im * im
        power[at] = jnp.where(first, here, power[at] + here)
        return carry

    lax.fori_loop(0, size // TILE, across, 0)


def rows_product(left, wave, half):
    size = wave.shape[-1]
    for c in range(2):

        def down(i, carry, c=c):
            at = pl.ds(pl.multiple_of(c * size + i * TILE, TILE), TILE)
            to = pl.ds(pl.multiple_of(i * TILE, TILE), TILE)
            product = jnp.dot(left[at], wave[...], preferred_element_type=F32)
            half[to, c * size : (c + 1) * size] = product.astype(BF16)
            return carry

        lax.fori_loop(0, size // TILE, down, 0)


def backward_kernel(far, probe, patch, measured, power, left, right, term, grad, scale, wave, half):
    size = patch.shape[-1]
    first = pl.program_id(0) == 0

    @pl.when(first)
    def _():
        total = jnp.maximum(power[...], 0.25)
        scale[...] = 1.0 - measured[...] / jnp.sqrt(total)

    def residual(i, carry):
        at = pl.ds(pl.multiple_of(i * 64, 64), 64)
        low = pl.ds(pl.multiple_of(size + i * 64, 64), 64)
        wave[at] = (far[0, 0, at] * scale[at]).astype(BF16)
        wave[low] = (far[0, 1, at] * scale[at]).astype(BF16)
        return carry

    lax.fori_loop(0, size // 64, residual, 0)
    rows_product(left, wave, half)

    def across(i, carry):
        at = pl.ds(pl.multiple_of(i * TILE, TILE), TILE)
        both = jnp.dot(half[at], right[...], preferred_element_type=F32)
        br, bi = both[:, :size], both[:, size:]
        pr, pi, xr, xi = probe[0, 0, at], probe[0, 1, at], patch[0, at], patch[1, at]
        term[0, 0, at] = (xr * br + xi * bi).astype(BF16)
        term[0, 1, at] = (xr * bi - xi * br).astype(BF16)
        re, im = pr * br + pi * bi, pr * bi - pi * br
        grad[0, at] = jnp.where(first, re, grad[0, at] + re)
        grad[1, at] = jnp.where(first, im, grad[1, at] + im)
        return carry

    lax.fori_loop(0, size // TILE, across, 0)


def mesh_peer(scan, mode, planes, dx, dy, dz):
    z, y, x = scan // 4, lax.rem(scan // 2, 2), lax.rem(scan, 2)
    x, y = lax.rem(x + dx, 2), lax.rem(y + dy, 2)
    return (lax.rem(z + dz, planes) * 4 + y * 2 + x, mode)


def core_kernel(
    probe, patch, measured, left, right, result, grad,
    far, power, power_in, scale, wave, half, term, got1, sum1, got2, sum2, got3,
    swap_send, swap_recv, send, recv, send_z, recv_z, ship_z, land_z,
):
    modes, size = probe.shape[0], patch.shape[-1]
    planes = got3.shape[2] + 1
    scan, mode = lax.axis_index("scan"), lax.axis_index("mode")
    z, y, x = scan // 4, lax.rem(scan // 2, 2), lax.rem(scan, 2)
    partner = (scan, 1 - mode)
    peer_x = mesh_peer(scan, mode, planes, 1, 0, 0)
    peer_y = mesh_peer(scan, mode, planes, 0, 1, 0)
    peers_z = [mesh_peer(scan, mode, planes, 0, 0, k) for k in range(1, planes)]
    first_peer, second_peer = (peer_x, peer_y), (peer_y, peer_x)
    first_at, second_at = (x, y), (y, x)
    h, q, e = size // 2, size // 4, size // 4 // planes

    barrier = pltpu.get_barrier_semaphore()
    everyone = [partner, peer_x, peer_y] + peers_z
    for peer in everyone:
        pl.semaphore_signal(barrier, inc=1, device_id=peer, device_id_type=MESH)
    pl.semaphore_wait(barrier, len(everyone))

    def remote(src, dst, send_sem, recv_sem, peer):
        return pltpu.make_async_remote_copy(
            src_ref=src, dst_ref=dst, send_sem=send_sem, recv_sem=recv_sem, device_id=peer, device_id_type=MESH
        )

    def rows(start, count, step):
        return pl.ds(pl.multiple_of(start, step), count)

    def copy1(m, c):
        away = rows((1 - first_at[c]) * h, h, h)
        return remote(term.at[m, c, away], got1.at[m, c], send.at[0, m, c], recv.at[0, m, c], first_peer[c])

    def copy2(m, c):
        away = rows((1 - second_at[c]) * q, q, q)
        return remote(sum1.at[m, c, away], got2.at[m, c], send.at[1, m, c], recv.at[1, m, c], second_peer[c])

    def copy3(m, c, k):
        away = rows(lax.rem(z + k, planes) * e, e, e)
        return remote(
            sum2.at[m, c, away], got3.at[m, c, k - 1], send_z.at[m, c, k - 1], recv_z.at[m, c, k - 1], peers_z[k - 1]
        )

    def base(c):
        return first_at[c] * h + second_at[c] * q

    def copy4(m, c, k):
        own = result.at[m, c, rows(base(c) + z * e, e, e)]
        return remote(own, own, ship_z.at[m, c, k - 1], land_z.at[m, c, k - 1], peers_z[k - 1])

    def copy5(m, c):
        own = result.at[m, c, rows(base(c), q, q)]
        return remote(own, own, send.at[2, m, c], recv.at[2, m, c], second_peer[c])

    def copy6(m, c):
        own = result.at[m, c, rows(first_at[c] * h, h, h)]
        return remote(own, own, send.at[3, m, c], recv.at[3, m, c], first_peer[c])

    def start(stage, m):
        for c in range(2):
            if stage in (3, 4):
                for k in range(1, planes):
                    (copy3, copy4)[stage - 3](m, c, k).start()
            else:
                {1: copy1, 2: copy2, 5: copy5, 6: copy6}[stage](m, c).start()

    def finish(stage, m):
        for c in range(2):
            if stage == 1:
                copy1(m, c).wait_recv()
                mine = term[m, c, rows(first_at[c] * h, h, h)].astype(F32)
                sum1[m, c] = (mine + got1[m, c].astype(F32)).astype(BF16)
            if stage == 2:
                copy2(m, c).wait_recv()
                mine = sum1[m, c, rows(second_at[c] * q, q, q)].astype(F32)
                sum2[m, c] = (mine + got2[m, c].astype(F32)).astype(BF16)
            if stage == 3:
                total = sum2[m, c, rows(z * e, e, e)].astype(F32)
                for k in range(1, planes):
                    copy3(m, c, k).wait_recv()
                    total = total + got3[m, c, k - 1].astype(F32)
                result[m, c, rows(base(c) + z * e, e, e)] = total.astype(BF16)
            if stage == 4:
                for k in range(1, planes):
                    copy4(m, c, k).wait_recv()
            if stage == 5:
                copy5(m, c).wait_recv()
            if stage == 6:
                copy6(m, c).wait_recv()

    def swap(i):
        at = rows(i * TILE, TILE, TILE)
        return remote(power.at[at], power_in.at[at], swap_send.at[i], swap_recv.at[i], partner)

    def product(table, source):
        for c in range(2):

            def down(i, carry, c=c):
                at = rows(c * size + i * TILE, TILE, TILE)
                out = jnp.dot(table[at], source[...], preferred_element_type=F32)
                half[rows(i * TILE, TILE, TILE), c * size : (c + 1) * size] = out.astype(BF16)
                return carry

            lax.fori_loop(0, size // TILE, down, 0)

    def forward(m, carry):
        def leave(i, carry):
            at, low = rows(i * 64, 64, 64), rows(size + i * 64, 64, 64)
            pr, pi, xr, xi = probe[m, 0, at], probe[m, 1, at], patch[0, at], patch[1, at]
            wave[at] = (pr * xr - pi * xi).astype(BF16)
            wave[low] = (pr * xi + pi * xr).astype(BF16)
            return carry

        lax.fori_loop(0, size // 64, leave, 0)
        product(left, wave)

        def across(i, carry):
            at = rows(i * TILE, TILE, TILE)
            both = jnp.dot(half[at], right[...], preferred_element_type=F32)
            re, im = both[:, :size], both[:, size:]
            far[m, 0, at] = re
            far[m, 1, at] = im
            here = re * re + im * im
            power[at] = jnp.where(m == 0, here, power[at] + here)

            @pl.when(m == modes - 1)
            def _():
                swap(i).start()

            return carry

        lax.fori_loop(0, size // TILE, across, 0)
        return carry

    lax.fori_loop(0, modes, forward, 0)
    for i in range(size // TILE):
        at = pl.ds(i * TILE, TILE)
        swap(i).wait_recv()
        total = jnp.maximum(power[at] + power_in[at], 0.25)
        scale[at] = 1.0 - measured[at] / jnp.sqrt(total)

    def backward(m, carry):
        def residual(i, carry):
            at, low = rows(i * 64, 64, 64), rows(size + i * 64, 64, 64)
            wave[at] = (far[m, 0, at] * scale[at]).astype(BF16)
            wave[low] = (far[m, 1, at] * scale[at]).astype(BF16)
            return carry

        lax.fori_loop(0, size // 64, residual, 0)
        product(right, wave)

        def across(i, carry):
            at = rows(i * TILE, TILE, TILE)
            both = jnp.dot(half[at], left[...], preferred_element_type=F32)
            br, bi = both[:, :size], both[:, size:]
            pr, pi, xr, xi = probe[m, 0, at], probe[m, 1, at], patch[0, at], patch[1, at]
            term[m, 0, at] = (xr * br + xi * bi).astype(BF16)
            term[m, 1, at] = (xr * bi - xi * br).astype(BF16)
            re, im = pr * br + pi * bi, pr * bi - pi * br
            grad[0, at] = jnp.where(m == 0, re, grad[0, at] + re)
            grad[1, at] = jnp.where(m == 0, im, grad[1, at] + im)
            return carry

        lax.fori_loop(0, size // TILE, across, 0)
        start(1, m)

        @pl.when(m >= 2)
        def _():
            finish(1, m - 2)
            start(2, m - 2)

        return carry

    lax.fori_loop(0, modes, backward, 0)
    steps = sorted((m + s, -s, m, s) for m in range(modes) for s in range(1, 7) if s > 1 or m >= modes - 2)
    for _, _, m, s in steps:
        finish(s, m)
        if s < 6:
            start(s + 1, m)

    def drain(m, carry):
        for c in range(2):
            for copy in (copy1, copy2, copy5, copy6):
                copy(m, c).wait_send()
            for k in range(1, planes):
                copy3(m, c, k).wait_send()
                copy4(m, c, k).wait_send()
        return carry

    lax.fori_loop(0, modes, drain, 0)
    for i in range(size // TILE):
        swap(i).wait_send()


def place_kernel(strips, row, grad, out, padded):
    count, parts, rows, size = out.shape
    padded[...] = jnp.zeros_like(padded)
    padded[:, rows : rows + size, :] = grad[...]

    def one(j, carry):
        start = jnp.clip(strips[j] * rows - row[0], -rows, size) + rows
        base = pl.ds(pl.multiple_of(start // 8 * 8, 8), rows + 8)
        up = lax.rem(rows + 8 - lax.rem(start, 8), rows + 8)
        for k in range(parts):
            out[j, k] = pltpu.roll(padded[k, base, :], up, 0)[:rows]
        return carry

    lax.fori_loop(0, count, one, 0)


def add_kernel(cols, received, out, total):
    count, parts, rows, size = received.shape
    total[...] = jnp.zeros_like(total)
    edge = jnp.zeros((rows, LANES), F32)

    def one(j, carry):
        across = pl.ds(pl.multiple_of(cols[j] // LANES * LANES, LANES), size + LANES)
        shift = lax.rem(cols[j], LANES)
        for k in range(parts):
            piece = jnp.concatenate([received[j, k], edge], axis=1)
            total[k, :, across] += pltpu.roll(piece, shift, 1)
        return carry

    lax.fori_loop(0, count, one, 0)
    out[...] = total[:, :, : out.shape[-1]]


def shards(object_field, probe, amplitude, pos_row, pos_col, strip_of):
    size = probe.shape[-1]
    modes = probe.shape[0]
    rows, cols = object_field.shape[1], object_field.shape[2]
    devices, groups = lax.axis_size("scan"), lax.axis_size("mode")
    padded_cols = cols + LANES
    forward, inverse = dft_tables(size)

    def swap(x):
        return lax.ppermute(x, "mode", [(0, 1), (1, 0)])

    lane = lax.broadcasted_iota(jnp.int32, (2, META, cols), 2)
    numbers = jnp.where(lane == 0, strip_of[0], jnp.where(lane == 1, pos_col[0] // LANES, pos_col[0] % LANES))
    packed = jnp.concatenate([object_field.astype(BF16), numbers.astype(BF16)], axis=1)
    me = lax.axis_index("mode")
    if groups == 2 and devices % PLANE == 0:
        dma, lines = pltpu.SemaphoreType.DMA, devices // PLANE
        held = pl.pallas_call(
            gather_kernel,
            out_shape=jax.ShapeDtypeStruct((2, devices, rows + META, cols), BF16),
            in_specs=[VMEM],
            out_specs=VMEM,
            scratch_shapes=[
                dma((max(lines - 1, 1),)),
                dma((max(lines - 1, 1),)),
                dma((lines, PLANE - 1)),
                dma((lines, PLANE - 1)),
                dma,
                dma,
            ],
            compiler_params=pltpu.CompilerParams(
                vmem_limit_bytes=56 * 1024 * 1024, collective_id=0, has_side_effects=True
            ),
        )(lax.dynamic_index_in_dim(packed, me, 0, keepdims=False))
    else:
        held = lax.all_gather(packed, "scan", axis=1)
    numbers = held[0, :, rows, :3].astype(jnp.int32)
    strips = numbers[:, 0]
    all_cols = numbers[:, 1] * LANES + numbers[:, 2]

    wave_shape = jax.ShapeDtypeStruct((2, size, size), F32)
    patch = pl.pallas_call(
        cut_kernel,
        out_shape=wave_shape,
        in_specs=[SMEM, SMEM, SMEM, VMEM],
        out_specs=VMEM,
        scratch_shapes=[pltpu.VMEM((2, devices * rows + 8, padded_cols), F32)],
        compiler_params=PARAMS,
    )(strips, pos_row, pos_col, held)

    def whole(*shape):
        return pl.BlockSpec(shape, lambda m: (0,) * len(shape))

    mode_spec = pl.BlockSpec((1, 2, size, size), lambda m: (m, 0, 0, 0))
    table_spec = whole(2 * size, 2 * size)
    buffers = [pltpu.VMEM((2 * size, size), BF16), pltpu.VMEM((size, 2 * size), BF16)]
    planes = devices // 4
    if groups == 2 and planes >= 2 and size % (64 * planes) == 0:
        dma = pltpu.SemaphoreType.DMA
        h, q, e = size // 2, size // 4, size // 4 // planes
        term, grad = pl.pallas_call(
            core_kernel,
            out_shape=(jax.ShapeDtypeStruct((modes, 2, size, size), BF16), wave_shape),
            in_specs=[VMEM] * 5,
            out_specs=(VMEM, VMEM),
            scratch_shapes=[
                pltpu.VMEM((modes, 2, size, size), F32),
                pltpu.VMEM((size, size), F32),
                pltpu.VMEM((size, size), F32),
                pltpu.VMEM((size, size), F32),
                pltpu.VMEM((2 * size, size), BF16),
                pltpu.VMEM((size, 2 * size), BF16),
                pltpu.VMEM((modes, 2, size, size), BF16),
                pltpu.VMEM((modes, 2, h, size), BF16),
                pltpu.VMEM((modes, 2, h, size), BF16),
                pltpu.VMEM((modes, 2, q, size), BF16),
                pltpu.VMEM((modes, 2, q, size), BF16),
                pltpu.VMEM((modes, 2, planes - 1, e, size), BF16),
                dma((size // TILE,)),
                dma((size // TILE,)),
                dma((4, modes, 2)),
                dma((4, modes, 2)),
                dma((modes, 2, planes - 1)),
                dma((modes, 2, planes - 1)),
                dma((modes, 2, planes - 1)),
                dma((modes, 2, planes - 1)),
            ],
            compiler_params=pltpu.CompilerParams(
                vmem_limit_bytes=56 * 1024 * 1024, collective_id=1, has_side_effects=True
            ),
        )(probe, patch, amplitude[0], forward, inverse)
        probe_grad = term.astype(F32)
    else:
        far, power = pl.pallas_call(
            forward_kernel,
            grid=(modes,),
            out_shape=(
                jax.ShapeDtypeStruct((modes, 2, size, size), F32),
                jax.ShapeDtypeStruct((size, size), F32),
            ),
            in_specs=[mode_spec, whole(2, size, size), table_spec, table_spec],
            out_specs=(mode_spec, whole(size, size)),
            scratch_shapes=buffers,
            compiler_params=PARAMS,
        )(probe, patch, forward, inverse)
        power = power + swap(power) if groups == 2 else lax.psum(power, "mode")
        term, grad = pl.pallas_call(
            backward_kernel,
            grid=(modes,),
            out_shape=(jax.ShapeDtypeStruct((modes, 2, size, size), BF16), wave_shape),
            in_specs=[
                mode_spec,
                mode_spec,
                whole(2, size, size),
                whole(size, size),
                whole(size, size),
                table_spec,
                table_spec,
            ],
            out_specs=(mode_spec, whole(2, size, size)),
            scratch_shapes=[pltpu.VMEM((size, size), F32)] + buffers,
            compiler_params=PARAMS,
        )(far, probe, patch, amplitude[0], power, inverse, forward)
        probe_grad = lax.psum(term, "scan").astype(F32)

    if groups == 2:
        mine = lax.dynamic_index_in_dim(grad, me, 0, keepdims=True)
        other = lax.dynamic_index_in_dim(grad, 1 - me, 0, keepdims=True)
        grad = mine + swap(other)
    else:
        grad = lax.psum(grad, "mode")
    parts = grad.shape[0]
    pieces = pl.pallas_call(
        place_kernel,
        out_shape=jax.ShapeDtypeStruct((devices, parts, rows, size), F32),
        in_specs=[SMEM, SMEM, VMEM],
        out_specs=VMEM,
        scratch_shapes=[pltpu.VMEM((parts, size + 2 * rows + 8, size), F32)],
        compiler_params=PARAMS,
    )(strips, pos_row, grad)
    received = lax.all_to_all(pieces.astype(BF16), "scan", 0, 0, tiled=False).astype(F32)
    strip_grad = pl.pallas_call(
        add_kernel,
        out_shape=jax.ShapeDtypeStruct((parts, rows, cols), F32),
        in_specs=[SMEM, VMEM],
        out_specs=VMEM,
        scratch_shapes=[pltpu.VMEM((parts, rows, padded_cols), F32)],
        compiler_params=PARAMS,
    )(all_cols, received)
    if groups == 2:
        theirs = swap(strip_grad)
        strip_grad = jnp.where(
            me == 0,
            jnp.concatenate([strip_grad, theirs]),
            jnp.concatenate([theirs, strip_grad]),
        )
    return (strip_grad, probe_grad)


def solution(mesh):
    return jax.shard_map(
        shards,
        mesh=mesh,
        in_specs=(
            P(None, "scan", None),
            P("mode", None, None, None),
            P("scan", None, None),
            P("scan"),
            P("scan"),
            P("scan"),
        ),
        out_specs=(P(None, "scan", None), P("mode", None, None, None)),
        check_vma=False,
    )
```

```python
import math

import jax
import jax.numpy as jnp
import numpy as np
from jax import lax
from jax.experimental import pallas as pl
from jax.experimental.pallas import tpu as pltpu
from jax.sharding import PartitionSpec as P

F32 = jnp.float32
BF16 = jnp.bfloat16
LANES = 128
META = 8
PLANE = 4
TILE = 256
PARAMS = pltpu.CompilerParams(vmem_limit_bytes=56 * 1024 * 1024)
VMEM = pl.BlockSpec(memory_space=pltpu.VMEM)
SMEM = pl.BlockSpec(memory_space=pltpu.SMEM)
MESH = pl.DeviceIdType.MESH


def dft_tables(size):
    positions = np.arange(size, dtype=np.int32)
    angles = (positions[:, None] * positions[None, :] % size).astype(np.float32)
    angles = angles * np.float32(2.0 * math.pi / size)
    norm = np.float32(1.0 / math.sqrt(size))
    cosine, sine = np.cos(angles) * norm, np.sin(angles) * norm
    forward = np.block([[cosine, sine], [-sine, cosine]])
    inverse = np.block([[cosine, -sine], [sine, cosine]])
    return jnp.asarray(forward, BF16), jnp.asarray(inverse, BF16)


def gather_kernel(mine, out, line_send, line_recv, plane_send, plane_recv, swap_send, swap_recv):
    count = out.shape[1]
    lines = count // PLANE
    scan, mode = lax.axis_index("scan"), lax.axis_index("mode")
    line, place = scan // PLANE, lax.rem(scan, PLANE)
    in_line = [(lax.rem(line + k, lines) * PLANE + place, mode) for k in range(1, lines)]
    in_plane = [(line * PLANE + lax.rem(place + t, PLANE), mode) for t in range(1, PLANE)]
    partner = (scan, 1 - mode)

    barrier = pltpu.get_barrier_semaphore()
    for peer in in_line + in_plane + [partner]:
        pl.semaphore_signal(barrier, inc=1, device_id=peer, device_id_type=pl.DeviceIdType.MESH)
    pl.semaphore_wait(barrier, len(in_line) + len(in_plane) + 1)

    def push(src, dst, send, recv, peer):
        copy = pltpu.make_async_remote_copy(
            src_ref=src,
            dst_ref=dst,
            send_sem=send,
            recv_sem=recv,
            device_id=peer,
            device_id_type=pl.DeviceIdType.MESH,
        )
        copy.start()
        return copy

    own = out.at[mode, scan]
    line_copies = [
        push(mine, own, line_send.at[k], line_recv.at[k], peer) for k, peer in enumerate(in_line)
    ]
    plane_copies = [
        push(mine, own, plane_send.at[0, t], plane_recv.at[0, t], peer) for t, peer in enumerate(in_plane)
    ]
    out[mode, scan] = mine[...]
    for k, arriving in enumerate(line_copies):
        arriving.wait_recv()
        piece = out.at[mode, lax.rem(line + lines - k - 1, lines) * PLANE + place]
        plane_copies += [
            push(piece, piece, plane_send.at[k + 1, t], plane_recv.at[k + 1, t], peer)
            for t, peer in enumerate(in_plane)
        ]
    for copy in plane_copies:
        copy.wait_recv()
    last = push(out.at[mode], out.at[mode], swap_send, swap_recv, partner)
    for copy in line_copies + plane_copies:
        copy.wait_send()
    last.wait()


def cut_kernel(strips, row, col, held, patch, window):
    count, rows = held.shape[1], held.shape[2] - META
    size, cols = patch.shape[-1], held.shape[-1]
    wide = size + LANES

    def place(j, carry):
        at = pl.ds(pl.multiple_of(strips[j] * rows, 8), rows)
        for c in range(2):
            window[c, at, :cols] = held[c, j].astype(F32)[:rows]
        return carry

    lax.fori_loop(0, count, place, 0)
    across = pl.ds(pl.multiple_of(col[0] // LANES * LANES, LANES), wide)
    back = lax.rem(wide - lax.rem(col[0], LANES), wide)
    up = lax.rem(72 - lax.rem(row[0], 8), 72)
    for c in range(2):

        def cut(i, carry, c=c):
            block = window[c, pl.ds(pl.multiple_of(row[0] // 8 * 8 + i * 64, 8), 72), across]
            block = pltpu.roll(block, up, 0)[:64]
            patch[c, pl.ds(pl.multiple_of(i * 64, 64), 64), :] = pltpu.roll(block, back, 1)[:, :size]
            return carry

        lax.fori_loop(0, size // 64, cut, 0)


def forward_kernel(probe, patch, left, right, far, power, wave, half):
    size = patch.shape[-1]

    def leave(i, carry):
        at = pl.ds(pl.multiple_of(i * 64, 64), 64)
        low = pl.ds(pl.multiple_of(size + i * 64, 64), 64)
        pr, pi, xr, xi = probe[0, 0, at], probe[0, 1, at], patch[0, at], patch[1, at]
        wave[at] = (pr * xr - pi * xi).astype(BF16)
        wave[low] = (pr * xi + pi * xr).astype(BF16)
        return carry

    lax.fori_loop(0, size // 64, leave, 0)
    rows_product(left, wave, half)
    first = pl.program_id(0) == 0

    def across(i, carry):
        at = pl.ds(pl.multiple_of(i * TILE, TILE), TILE)
        both = jnp.dot(half[at], right[...], preferred_element_type=F32)
        re, im = both[:, :size], both[:, size:]
        far[0, 0, at] = re
        far[0, 1, at] = im
        here = re * re + im * im
        power[at] = jnp.where(first, here, power[at] + here)
        return carry

    lax.fori_loop(0, size // TILE, across, 0)


def rows_product(left, wave, half):
    size = wave.shape[-1]
    for c in range(2):

        def down(i, carry, c=c):
            at = pl.ds(pl.multiple_of(c * size + i * TILE, TILE), TILE)
            to = pl.ds(pl.multiple_of(i * TILE, TILE), TILE)
            product = jnp.dot(left[at], wave[...], preferred_element_type=F32)
            half[to, c * size : (c + 1) * size] = product.astype(BF16)
            return carry

        lax.fori_loop(0, size // TILE, down, 0)


def backward_kernel(far, probe, patch, measured, power, left, right, term, grad, scale, wave, half):
    size = patch.shape[-1]
    first = pl.program_id(0) == 0

    @pl.when(first)
    def _():
        total = jnp.maximum(power[...], 0.25)
        scale[...] = 1.0 - measured[...] / jnp.sqrt(total)

    def residual(i, carry):
        at = pl.ds(pl.multiple_of(i * 64, 64), 64)
        low = pl.ds(pl.multiple_of(size + i * 64, 64), 64)
        wave[at] = (far[0, 0, at] * scale[at]).astype(BF16)
        wave[low] = (far[0, 1, at] * scale[at]).astype(BF16)
        return carry

    lax.fori_loop(0, size // 64, residual, 0)
    rows_product(left, wave, half)

    def across(i, carry):
        at = pl.ds(pl.multiple_of(i * TILE, TILE), TILE)
        both = jnp.dot(half[at], right[...], preferred_element_type=F32)
        br, bi = both[:, :size], both[:, size:]
        pr, pi, xr, xi = probe[0, 0, at], probe[0, 1, at], patch[0, at], patch[1, at]
        term[0, 0, at] = (xr * br + xi * bi).astype(BF16)
        term[0, 1, at] = (xr * bi - xi * br).astype(BF16)
        re, im = pr * br + pi * bi, pr * bi - pi * br
        grad[0, at] = jnp.where(first, re, grad[0, at] + re)
        grad[1, at] = jnp.where(first, im, grad[1, at] + im)
        return carry

    lax.fori_loop(0, size // TILE, across, 0)


def mesh_peer(scan, mode, planes, dx, dy, dz):
    z, y, x = scan // 4, lax.rem(scan // 2, 2), lax.rem(scan, 2)
    x, y = lax.rem(x + dx, 2), lax.rem(y + dy, 2)
    return (lax.rem(z + dz, planes) * 4 + y * 2 + x, mode)


def core_kernel(
    strips, row, cols, probe_hbm, patch_hbm, measured_hbm, left_hbm, right_hbm, result, strip_grad,
    probe, patch, measured, left, right,
    far, power, power_in, scale, wave, half, term, got1, sum1, got2, sum2, got3,
    grad, grad_in, summed, pieces, landed,
    load, load_probe, swap_send, swap_recv, send, recv, send_z, recv_z, ship_z, land_z,
    part_send, part_recv, piece_send, piece_recv, strip_send, strip_recv,
):
    modes, size = probe.shape[0], patch.shape[-1]
    devices = lax.axis_size("scan")
    strip, width = strip_grad.shape[1], strip_grad.shape[2]
    planes = got3.shape[2] + 1
    scan, mode = lax.axis_index("scan"), lax.axis_index("mode")
    z, y, x = scan // 4, lax.rem(scan // 2, 2), lax.rem(scan, 2)
    partner = (scan, 1 - mode)
    peer_x = mesh_peer(scan, mode, planes, 1, 0, 0)
    peer_y = mesh_peer(scan, mode, planes, 0, 1, 0)
    peers_z = [mesh_peer(scan, mode, planes, 0, 0, k) for k in range(1, planes)]
    first_peer, second_peer = (peer_x, peer_y), (peer_y, peer_x)
    first_at, second_at = (x, y), (y, x)
    h, q, e = size // 2, size // 4, size // 4 // planes

    barrier = pltpu.get_barrier_semaphore()
    everyone = [partner] + [(lax.rem(scan + k, devices), mode) for k in range(1, devices)]
    for peer in everyone:
        pl.semaphore_signal(barrier, inc=1, device_id=peer, device_id_type=MESH)

    def probe_load(m):
        return pltpu.make_async_copy(probe_hbm.at[m], probe.at[m], load_probe.at[m])

    whole = [(patch_hbm, patch), (left_hbm, left), (right_hbm, right), (measured_hbm, measured)]
    loads = [pltpu.make_async_copy(src, dst, load.at[i]) for i, (src, dst) in enumerate(whole)]
    probe_load(0).start()
    for copy in loads:
        copy.start()
    for m in range(1, modes):
        probe_load(m).start()
    for copy in loads:
        copy.wait()
    pl.semaphore_wait(barrier, len(everyone))

    def remote(src, dst, send_sem, recv_sem, peer):
        return pltpu.make_async_remote_copy(
            src_ref=src, dst_ref=dst, send_sem=send_sem, recv_sem=recv_sem, device_id=peer, device_id_type=MESH
        )

    def rows(start, count, step):
        return pl.ds(pl.multiple_of(start, step), count)

    def copy1(m, c):
        away = rows((1 - first_at[c]) * h, h, h)
        return remote(term.at[m, c, away], got1.at[m, c], send.at[0, m, c], recv.at[0, m, c], first_peer[c])

    def copy2(m, c):
        away = rows((1 - second_at[c]) * q, q, q)
        return remote(sum1.at[m, c, away], got2.at[m, c], send.at[1, m, c], recv.at[1, m, c], second_peer[c])

    def copy3(m, c, k):
        away = rows(lax.rem(z + k, planes) * e, e, e)
        return remote(
            sum2.at[m, c, away], got3.at[m, c, k - 1], send_z.at[m, c, k - 1], recv_z.at[m, c, k - 1], peers_z[k - 1]
        )

    def base(c):
        return first_at[c] * h + second_at[c] * q

    def copy4(m, c, k):
        own = result.at[m, c, rows(base(c) + z * e, e, e)]
        return remote(own, own, ship_z.at[m, c, k - 1], land_z.at[m, c, k - 1], peers_z[k - 1])

    def copy5(m, c):
        own = result.at[m, c, rows(base(c), q, q)]
        return remote(own, own, send.at[2, m, c], recv.at[2, m, c], second_peer[c])

    def copy6(m, c):
        own = result.at[m, c, rows(first_at[c] * h, h, h)]
        return remote(own, own, send.at[3, m, c], recv.at[3, m, c], first_peer[c])

    def start(stage, m):
        for c in range(2):
            if stage in (3, 4):
                for k in range(1, planes):
                    (copy3, copy4)[stage - 3](m, c, k).start()
            else:
                {1: copy1, 2: copy2, 5: copy5, 6: copy6}[stage](m, c).start()

    def finish(stage, m):
        for c in range(2):
            if stage == 1:
                copy1(m, c).wait_recv()
                mine = term[m, c, rows(first_at[c] * h, h, h)].astype(F32)
                sum1[m, c] = (mine + got1[m, c].astype(F32)).astype(BF16)
            if stage == 2:
                copy2(m, c).wait_recv()
                mine = sum1[m, c, rows(second_at[c] * q, q, q)].astype(F32)
                sum2[m, c] = (mine + got2[m, c].astype(F32)).astype(BF16)
            if stage == 3:
                total = sum2[m, c, rows(z * e, e, e)].astype(F32)
                for k in range(1, planes):
                    copy3(m, c, k).wait_recv()
                    total = total + got3[m, c, k - 1].astype(F32)
                result[m, c, rows(base(c) + z * e, e, e)] = total.astype(BF16)
            if stage == 4:
                for k in range(1, planes):
                    copy4(m, c, k).wait_recv()
            if stage == 5:
                copy5(m, c).wait_recv()
            if stage == 6:
                copy6(m, c).wait_recv()

    def swap(i):
        at = rows(i * TILE, TILE, TILE)
        return remote(power.at[at], power_in.at[at], swap_send.at[i], swap_recv.at[i], partner)

    def product(table, source):
        for c in range(2):

            def down(i, carry, c=c):
                at = rows(c * size + i * TILE, TILE, TILE)
                out = jnp.dot(table[at], source[...], preferred_element_type=F32)
                half[rows(i * TILE, TILE, TILE), c * size : (c + 1) * size] = out.astype(BF16)
                return carry

            lax.fori_loop(0, size // TILE, down, 0)

    def part(i):
        at = rows(i * TILE, TILE, TILE)
        return remote(grad.at[1 - mode, at], grad_in.at[at], part_send.at[i], part_recv.at[i], partner)

    deep = pieces.shape[0] // devices
    mine = rows(scan * deep, deep, deep)

    def one_hot(mask):
        return jnp.where(mask, 1.0, 0.0).astype(BF16)

    def piece(k):
        to = lax.rem(scan + k, devices)
        return remote(pieces.at[rows(to * deep, deep, deep)], landed.at[mine], piece_send.at[k - 1], piece_recv.at[k - 1], (to, mode))

    def arrive(k):
        come = lax.rem(scan + devices - k, devices)
        at = rows(come * deep, deep, deep)
        return remote(pieces.at[at], landed.at[at], piece_send.at[k - 1], piece_recv.at[k - 1], (come, mode))

    def strip_swap():
        return remote(strip_grad.at[mode], strip_grad.at[mode], strip_send, strip_recv, partner)

    def cut_pieces():
        for i in range(size // TILE):
            part(i).wait_recv()
            at = pl.ds(i * TILE, TILE)
            summed[at] = (grad[mode, at] + grad_in[at]).astype(BF16)
        ahead = lax.broadcasted_iota(jnp.int32, (deep, size), 1) - lax.broadcasted_iota(jnp.int32, (deep, size), 0)

        def pick(j, carry):
            wave[rows(j * deep, deep, deep)] = one_hot(ahead == strips[j] * strip - row[0])
            return carry

        lax.fori_loop(0, devices, pick, 0)

        def move(i, carry):
            at = rows(i * TILE, TILE, TILE)
            pieces[at] = jnp.dot(wave[at], summed[...], preferred_element_type=F32).astype(BF16)
            return carry

        lax.fori_loop(0, devices * deep // TILE, move, 0)
        for k in range(1, devices):
            piece(k).start()
        landed[mine] = pieces[mine]

    def add_pieces():
        for k in range(1, devices):
            arrive(k).wait_recv()
        strip_grad[mode] = jnp.zeros((strip, width), F32)
        parts = size // LANES
        ahead = lax.broadcasted_iota(jnp.int32, (LANES, 2 * LANES), 1)
        ahead = ahead - lax.broadcasted_iota(jnp.int32, (LANES, 2 * LANES), 0)

        def one(j, carry):
            turn = one_hot(ahead == lax.rem(cols[j], LANES))
            blocks = jnp.concatenate(
                [landed[rows(j * deep, deep, deep), b * LANES : (b + 1) * LANES] for b in range(parts)]
            )
            moved = jnp.dot(blocks, turn, preferred_element_type=F32)
            for b in range(parts + 1):
                here = moved[b * deep : b * deep + strip, :LANES] if b < parts else 0.0
                if b > 0:
                    here = here + moved[(b - 1) * deep : (b - 1) * deep + strip, LANES:]
                for t in range((width - size) // LANES + 1):
                    if b + t < width // LANES:
                        to = slice((b + t) * LANES, (b + t + 1) * LANES)
                        strip_grad[mode, :, to] += jnp.where(cols[j] // LANES == t, here, 0.0)
            return carry

        lax.fori_loop(0, devices, one, 0)
        strip_swap().start()

    def forward(m, carry):
        probe_load(m).wait()

        def leave(i, carry):
            at, low = rows(i * 64, 64, 64), rows(size + i * 64, 64, 64)
            pr, pi, xr, xi = probe[m, 0, at], probe[m, 1, at], patch[0, at], patch[1, at]
            wave[at] = (pr * xr - pi * xi).astype(BF16)
            wave[low] = (pr * xi + pi * xr).astype(BF16)
            return carry

        lax.fori_loop(0, size // 64, leave, 0)
        product(left, wave)

        def across(i, carry):
            at = rows(i * TILE, TILE, TILE)
            both = jnp.dot(half[at], right[...], preferred_element_type=F32)
            re, im = both[:, :size], both[:, size:]
            far[m, 0, at] = re
            far[m, 1, at] = im
            here = re * re + im * im
            power[at] = jnp.where(m == 0, here, power[at] + here)

            @pl.when(m == modes - 1)
            def _():
                swap(i).start()

            return carry

        lax.fori_loop(0, size // TILE, across, 0)
        return carry

    lax.fori_loop(0, modes, forward, 0)
    for i in range(size // TILE):
        at = pl.ds(i * TILE, TILE)
        swap(i).wait_recv()
        total = jnp.maximum(power[at] + power_in[at], 0.25)
        scale[at] = 1.0 - measured[at] / jnp.sqrt(total)

    def backward(m, carry):
        def residual(i, carry):
            at, low = rows(i * 64, 64, 64), rows(size + i * 64, 64, 64)
            wave[at] = (far[m, 0, at] * scale[at]).astype(BF16)
            wave[low] = (far[m, 1, at] * scale[at]).astype(BF16)
            return carry

        lax.fori_loop(0, size // 64, residual, 0)
        product(right, wave)

        def across(i, carry):
            at = rows(i * TILE, TILE, TILE)
            both = jnp.dot(half[at], left[...], preferred_element_type=F32)
            br, bi = both[:, :size], both[:, size:]
            pr, pi, xr, xi = probe[m, 0, at], probe[m, 1, at], patch[0, at], patch[1, at]
            term[m, 0, at] = (xr * br + xi * bi).astype(BF16)
            term[m, 1, at] = (xr * bi - xi * br).astype(BF16)
            re, im = pr * br + pi * bi, pr * bi - pi * br
            grad[0, at] = jnp.where(m == 0, re, grad[0, at] + re)
            grad[1, at] = jnp.where(m == 0, im, grad[1, at] + im)

            @pl.when(m == modes - 1)
            def _():
                part(i).start()

            return carry

        lax.fori_loop(0, size // TILE, across, 0)
        start(1, m)

        @pl.when(m >= 2)
        def _():
            finish(1, m - 2)
            start(2, m - 2)

        return carry

    lax.fori_loop(0, modes, backward, 0)
    steps = sorted((m + s, -s, m, s) for m in range(modes) for s in range(1, 7) if s > 1 or m >= modes - 2)
    cut_pieces()
    for _, _, m, s in steps:
        if (m, s) == (1, 6):
            add_pieces()
        finish(s, m)
        if s < 6:
            start(s + 1, m)

    def drain(m, carry):
        for c in range(2):
            for copy in (copy1, copy2, copy5, copy6):
                copy(m, c).wait_send()
            for k in range(1, planes):
                copy3(m, c, k).wait_send()
                copy4(m, c, k).wait_send()
        return carry

    lax.fori_loop(0, modes, drain, 0)
    for i in range(size // TILE):
        swap(i).wait_send()
        part(i).wait_send()
    for k in range(1, devices):
        piece(k).wait_send()
    strip_swap().wait()


def place_kernel(strips, row, grad, out, padded):
    count, parts, rows, size = out.shape
    padded[...] = jnp.zeros_like(padded)
    padded[:, rows : rows + size, :] = grad[...]

    def one(j, carry):
        start = jnp.clip(strips[j] * rows - row[0], -rows, size) + rows
        base = pl.ds(pl.multiple_of(start // 8 * 8, 8), rows + 8)
        up = lax.rem(rows + 8 - lax.rem(start, 8), rows + 8)
        for k in range(parts):
            out[j, k] = pltpu.roll(padded[k, base, :], up, 0)[:rows]
        return carry

    lax.fori_loop(0, count, one, 0)


def add_kernel(cols, received, out, total):
    count, parts, rows, size = received.shape
    total[...] = jnp.zeros_like(total)
    edge = jnp.zeros((rows, LANES), F32)

    def one(j, carry):
        across = pl.ds(pl.multiple_of(cols[j] // LANES * LANES, LANES), size + LANES)
        shift = lax.rem(cols[j], LANES)
        for k in range(parts):
            piece = jnp.concatenate([received[j, k], edge], axis=1)
            total[k, :, across] += pltpu.roll(piece, shift, 1)
        return carry

    lax.fori_loop(0, count, one, 0)
    out[...] = total[:, :, : out.shape[-1]]


def shards(object_field, probe, amplitude, pos_row, pos_col, strip_of):
    size = probe.shape[-1]
    modes = probe.shape[0]
    rows, cols = object_field.shape[1], object_field.shape[2]
    devices, groups = lax.axis_size("scan"), lax.axis_size("mode")
    padded_cols = cols + LANES
    forward, inverse = dft_tables(size)

    def swap(x):
        return lax.ppermute(x, "mode", [(0, 1), (1, 0)])

    lane = lax.broadcasted_iota(jnp.int32, (2, META, cols), 2)
    numbers = jnp.where(lane == 0, strip_of[0], jnp.where(lane == 1, pos_col[0] // LANES, pos_col[0] % LANES))
    packed = jnp.concatenate([object_field.astype(BF16), numbers.astype(BF16)], axis=1)
    me = lax.axis_index("mode")
    if groups == 2 and devices % PLANE == 0:
        dma, lines = pltpu.SemaphoreType.DMA, devices // PLANE
        held = pl.pallas_call(
            gather_kernel,
            out_shape=jax.ShapeDtypeStruct((2, devices, rows + META, cols), BF16),
            in_specs=[VMEM],
            out_specs=VMEM,
            scratch_shapes=[
                dma((max(lines - 1, 1),)),
                dma((max(lines - 1, 1),)),
                dma((lines, PLANE - 1)),
                dma((lines, PLANE - 1)),
                dma,
                dma,
            ],
            compiler_params=pltpu.CompilerParams(
                vmem_limit_bytes=56 * 1024 * 1024, collective_id=0, has_side_effects=True
            ),
        )(lax.dynamic_index_in_dim(packed, me, 0, keepdims=False))
    else:
        held = lax.all_gather(packed, "scan", axis=1)
    numbers = held[0, :, rows, :3].astype(jnp.int32)
    strips = numbers[:, 0]
    all_cols = numbers[:, 1] * LANES + numbers[:, 2]

    wave_shape = jax.ShapeDtypeStruct((2, size, size), F32)
    patch = pl.pallas_call(
        cut_kernel,
        out_shape=wave_shape,
        in_specs=[SMEM, SMEM, SMEM, VMEM],
        out_specs=VMEM,
        scratch_shapes=[pltpu.VMEM((2, devices * rows + 8, padded_cols), F32)],
        compiler_params=PARAMS,
    )(strips, pos_row, pos_col, held)

    def whole(*shape):
        return pl.BlockSpec(shape, lambda m: (0,) * len(shape))

    mode_spec = pl.BlockSpec((1, 2, size, size), lambda m: (m, 0, 0, 0))
    table_spec = whole(2 * size, 2 * size)
    buffers = [pltpu.VMEM((2 * size, size), BF16), pltpu.VMEM((size, 2 * size), BF16)]
    planes, deep = devices // 4, -(-rows // 16) * 16
    fits = groups == 2 and devices == 4 * planes and planes >= 2 and size % (64 * planes) == 0
    if fits and rows % 8 == 0 and devices * deep % TILE == 0 and devices * deep <= 2 * size:
        dma = pltpu.SemaphoreType.DMA
        h, q, e = size // 2, size // 4, size // 4 // planes
        vmem = pltpu.VMEM
        any_space = pl.BlockSpec(memory_space=pl.ANY)
        term, strip_grad = pl.pallas_call(
            core_kernel,
            out_shape=(
                jax.ShapeDtypeStruct((modes, 2, size, size), BF16),
                jax.ShapeDtypeStruct((2, rows, cols), F32),
            ),
            in_specs=[SMEM] * 3 + [any_space] * 5,
            out_specs=(VMEM, VMEM),
            scratch_shapes=[
                vmem((modes, 2, size, size), F32),
                vmem((2, size, size), F32),
                vmem((size, size), F32),
                vmem((2 * size, 2 * size), BF16),
                vmem((2 * size, 2 * size), BF16),
                vmem((modes, 2, size, size), F32),
                vmem((size, size), F32),
                vmem((size, size), F32),
                vmem((size, size), F32),
                vmem((2 * size, size), BF16),
                vmem((size, 2 * size), BF16),
                vmem((modes, 2, size, size), BF16),
                vmem((modes, 2, h, size), BF16),
                vmem((modes, 2, h, size), BF16),
                vmem((modes, 2, q, size), BF16),
                vmem((modes, 2, q, size), BF16),
                vmem((modes, 2, planes - 1, e, size), BF16),
                vmem((2, size, size), F32),
                vmem((size, size), F32),
                vmem((size, size), BF16),
                vmem((devices * deep, size), BF16),
                vmem((devices * deep, size), BF16),
                dma((4,)),
                dma((modes,)),
                dma((size // TILE,)),
                dma((size // TILE,)),
                dma((4, modes, 2)),
                dma((4, modes, 2)),
                dma((modes, 2, planes - 1)),
                dma((modes, 2, planes - 1)),
                dma((modes, 2, planes - 1)),
                dma((modes, 2, planes - 1)),
                dma((size // TILE,)),
                dma((size // TILE,)),
                dma((devices - 1,)),
                dma((devices - 1,)),
                dma,
                dma,
            ],
            compiler_params=pltpu.CompilerParams(
                vmem_limit_bytes=58 * 1024 * 1024, collective_id=1, has_side_effects=True
            ),
        )(strips, pos_row, all_cols, probe, patch, amplitude[0], forward, inverse)
        return (strip_grad, term.astype(F32))

    far, power = pl.pallas_call(
        forward_kernel,
        grid=(modes,),
        out_shape=(
            jax.ShapeDtypeStruct((modes, 2, size, size), F32),
            jax.ShapeDtypeStruct((size, size), F32),
        ),
        in_specs=[mode_spec, whole(2, size, size), table_spec, table_spec],
        out_specs=(mode_spec, whole(size, size)),
        scratch_shapes=buffers,
        compiler_params=PARAMS,
    )(probe, patch, forward, inverse)
    power = power + swap(power) if groups == 2 else lax.psum(power, "mode")
    term, grad = pl.pallas_call(
        backward_kernel,
        grid=(modes,),
        out_shape=(jax.ShapeDtypeStruct((modes, 2, size, size), BF16), wave_shape),
        in_specs=[
            mode_spec,
            mode_spec,
            whole(2, size, size),
            whole(size, size),
            whole(size, size),
            table_spec,
            table_spec,
        ],
        out_specs=(mode_spec, whole(2, size, size)),
        scratch_shapes=[pltpu.VMEM((size, size), F32)] + buffers,
        compiler_params=PARAMS,
    )(far, probe, patch, amplitude[0], power, inverse, forward)
    probe_grad = lax.psum(term, "scan").astype(F32)

    if groups == 2:
        mine = lax.dynamic_index_in_dim(grad, me, 0, keepdims=True)
        other = lax.dynamic_index_in_dim(grad, 1 - me, 0, keepdims=True)
        grad = mine + swap(other)
    else:
        grad = lax.psum(grad, "mode")
    parts = grad.shape[0]
    pieces = pl.pallas_call(
        place_kernel,
        out_shape=jax.ShapeDtypeStruct((devices, parts, rows, size), F32),
        in_specs=[SMEM, SMEM, VMEM],
        out_specs=VMEM,
        scratch_shapes=[pltpu.VMEM((parts, size + 2 * rows + 8, size), F32)],
        compiler_params=PARAMS,
    )(strips, pos_row, grad)
    received = lax.all_to_all(pieces.astype(BF16), "scan", 0, 0, tiled=False).astype(F32)
    strip_grad = pl.pallas_call(
        add_kernel,
        out_shape=jax.ShapeDtypeStruct((parts, rows, cols), F32),
        in_specs=[SMEM, VMEM],
        out_specs=VMEM,
        scratch_shapes=[pltpu.VMEM((parts, rows, padded_cols), F32)],
        compiler_params=PARAMS,
    )(all_cols, received)
    if groups == 2:
        theirs = swap(strip_grad)
        strip_grad = jnp.where(
            me == 0,
            jnp.concatenate([strip_grad, theirs]),
            jnp.concatenate([theirs, strip_grad]),
        )
    return (strip_grad, probe_grad)


def solution(mesh):
    return jax.shard_map(
        shards,
        mesh=mesh,
        in_specs=(
            P(None, "scan", None),
            P("mode", None, None, None),
            P("scan", None, None),
            P("scan"),
            P("scan"),
            P("scan"),
        ),
        out_specs=(P(None, "scan", None), P("mode", None, None, None)),
        check_vma=False,
    )
```

```python
import math

import jax
import jax.numpy as jnp
import numpy as np
from jax import lax
from jax.experimental import pallas as pl
from jax.experimental.pallas import tpu as pltpu
from jax.sharding import PartitionSpec as P

F32 = jnp.float32
BF16 = jnp.bfloat16
LANES = 128
META = 8
PLANE = 4
TILE = 256
PARAMS = pltpu.CompilerParams(vmem_limit_bytes=56 * 1024 * 1024)
VMEM = pl.BlockSpec(memory_space=pltpu.VMEM)
SMEM = pl.BlockSpec(memory_space=pltpu.SMEM)
MESH = pl.DeviceIdType.MESH


def dft_tables(size):
    positions = np.arange(size, dtype=np.int32)
    angles = (positions[:, None] * positions[None, :] % size).astype(np.float32)
    angles = angles * np.float32(2.0 * math.pi / size)
    norm = np.float32(1.0 / math.sqrt(size))
    cosine, sine = np.cos(angles) * norm, np.sin(angles) * norm
    forward = np.block([[cosine, sine], [-sine, cosine]])
    inverse = np.block([[cosine, -sine], [sine, cosine]])
    return jnp.asarray(forward, BF16), jnp.asarray(inverse, BF16)


def gather_kernel(mine, out, line_send, line_recv, plane_send, plane_recv, swap_send, swap_recv):
    count = out.shape[1]
    lines = count // PLANE
    scan, mode = lax.axis_index("scan"), lax.axis_index("mode")
    line, place = scan // PLANE, lax.rem(scan, PLANE)
    in_line = [(lax.rem(line + k, lines) * PLANE + place, mode) for k in range(1, lines)]
    in_plane = [(line * PLANE + lax.rem(place + t, PLANE), mode) for t in range(1, PLANE)]
    partner = (scan, 1 - mode)

    barrier = pltpu.get_barrier_semaphore()
    for peer in in_line + in_plane + [partner]:
        pl.semaphore_signal(barrier, inc=1, device_id=peer, device_id_type=pl.DeviceIdType.MESH)
    pl.semaphore_wait(barrier, len(in_line) + len(in_plane) + 1)

    def push(src, dst, send, recv, peer):
        copy = pltpu.make_async_remote_copy(
            src_ref=src,
            dst_ref=dst,
            send_sem=send,
            recv_sem=recv,
            device_id=peer,
            device_id_type=pl.DeviceIdType.MESH,
        )
        copy.start()
        return copy

    own = out.at[mode, scan]
    line_copies = [
        push(mine, own, line_send.at[k], line_recv.at[k], peer) for k, peer in enumerate(in_line)
    ]
    plane_copies = [
        push(mine, own, plane_send.at[0, t], plane_recv.at[0, t], peer) for t, peer in enumerate(in_plane)
    ]
    out[mode, scan] = mine[...]
    for k, arriving in enumerate(line_copies):
        arriving.wait_recv()
        piece = out.at[mode, lax.rem(line + lines - k - 1, lines) * PLANE + place]
        plane_copies += [
            push(piece, piece, plane_send.at[k + 1, t], plane_recv.at[k + 1, t], peer)
            for t, peer in enumerate(in_plane)
        ]
    for copy in plane_copies:
        copy.wait_recv()
    last = push(out.at[mode], out.at[mode], swap_send, swap_recv, partner)
    for copy in line_copies + plane_copies:
        copy.wait_send()
    last.wait()


def cut_kernel(strips, row, col, held, patch, window):
    count, rows = held.shape[1], held.shape[2] - META
    size, cols = patch.shape[-1], held.shape[-1]
    wide = size + LANES

    def place(j, carry):
        at = pl.ds(pl.multiple_of(strips[j] * rows, 8), rows)
        for c in range(2):
            window[c, at, :cols] = held[c, j].astype(F32)[:rows]
        return carry

    lax.fori_loop(0, count, place, 0)
    across = pl.ds(pl.multiple_of(col[0] // LANES * LANES, LANES), wide)
    back = lax.rem(wide - lax.rem(col[0], LANES), wide)
    up = lax.rem(72 - lax.rem(row[0], 8), 72)
    for c in range(2):

        def cut(i, carry, c=c):
            block = window[c, pl.ds(pl.multiple_of(row[0] // 8 * 8 + i * 64, 8), 72), across]
            block = pltpu.roll(block, up, 0)[:64]
            patch[c, pl.ds(pl.multiple_of(i * 64, 64), 64), :] = pltpu.roll(block, back, 1)[:, :size]
            return carry

        lax.fori_loop(0, size // 64, cut, 0)


def forward_kernel(probe, patch, left, right, far, power, wave, half):
    size = patch.shape[-1]

    def leave(i, carry):
        at = pl.ds(pl.multiple_of(i * 64, 64), 64)
        low = pl.ds(pl.multiple_of(size + i * 64, 64), 64)
        pr, pi, xr, xi = probe[0, 0, at], probe[0, 1, at], patch[0, at], patch[1, at]
        wave[at] = (pr * xr - pi * xi).astype(BF16)
        wave[low] = (pr * xi + pi * xr).astype(BF16)
        return carry

    lax.fori_loop(0, size // 64, leave, 0)
    rows_product(left, wave, half)
    first = pl.program_id(0) == 0

    def across(i, carry):
        at = pl.ds(pl.multiple_of(i * TILE, TILE), TILE)
        both = jnp.dot(half[at], right[...], preferred_element_type=F32)
        re, im = both[:, :size], both[:, size:]
        far[0, 0, at] = re
        far[0, 1, at] = im
        here = re * re + im * im
        power[at] = jnp.where(first, here, power[at] + here)
        return carry

    lax.fori_loop(0, size // TILE, across, 0)


def rows_product(left, wave, half):
    size = wave.shape[-1]
    for c in range(2):

        def down(i, carry, c=c):
            at = pl.ds(pl.multiple_of(c * size + i * TILE, TILE), TILE)
            to = pl.ds(pl.multiple_of(i * TILE, TILE), TILE)
            product = jnp.dot(left[at], wave[...], preferred_element_type=F32)
            half[to, c * size : (c + 1) * size] = product.astype(BF16)
            return carry

        lax.fori_loop(0, size // TILE, down, 0)


def backward_kernel(far, probe, patch, measured, power, left, right, term, grad, scale, wave, half):
    size = patch.shape[-1]
    first = pl.program_id(0) == 0

    @pl.when(first)
    def _():
        total = jnp.maximum(power[...], 0.25)
        scale[...] = 1.0 - measured[...] / jnp.sqrt(total)

    def residual(i, carry):
        at = pl.ds(pl.multiple_of(i * 64, 64), 64)
        low = pl.ds(pl.multiple_of(size + i * 64, 64), 64)
        wave[at] = (far[0, 0, at] * scale[at]).astype(BF16)
        wave[low] = (far[0, 1, at] * scale[at]).astype(BF16)
        return carry

    lax.fori_loop(0, size // 64, residual, 0)
    rows_product(left, wave, half)

    def across(i, carry):
        at = pl.ds(pl.multiple_of(i * TILE, TILE), TILE)
        both = jnp.dot(half[at], right[...], preferred_element_type=F32)
        br, bi = both[:, :size], both[:, size:]
        pr, pi, xr, xi = probe[0, 0, at], probe[0, 1, at], patch[0, at], patch[1, at]
        term[0, 0, at] = (xr * br + xi * bi).astype(BF16)
        term[0, 1, at] = (xr * bi - xi * br).astype(BF16)
        re, im = pr * br + pi * bi, pr * bi - pi * br
        grad[0, at] = jnp.where(first, re, grad[0, at] + re)
        grad[1, at] = jnp.where(first, im, grad[1, at] + im)
        return carry

    lax.fori_loop(0, size // TILE, across, 0)


def mesh_peer(scan, mode, planes, dx, dy, dz):
    z, y, x = scan // 4, lax.rem(scan // 2, 2), lax.rem(scan, 2)
    x, y = lax.rem(x + dx, 2), lax.rem(y + dy, 2)
    return (lax.rem(z + dz, planes) * 4 + y * 2 + x, mode)


def core_kernel(
    strips, row, cols, probe_hbm, patch_hbm, measured_hbm, left_hbm, right_hbm, result, strip_grad,
    probe, patch, measured, left, right,
    far, power, power_in, scale, wave, half, term, got1, sum1, got2, sum2, got3,
    grad, grad_in, summed, pieces, landed,
    load, load_probe, swap_send, swap_recv, send, recv, send_z, recv_z, ship_z, land_z,
    part_send, part_recv, piece_send, piece_recv, strip_send, strip_recv,
):
    modes, size = probe.shape[0], patch.shape[-1]
    devices = lax.axis_size("scan")
    strip, width = strip_grad.shape[1], strip_grad.shape[2]
    planes = got3.shape[2] + 1
    scan, mode = lax.axis_index("scan"), lax.axis_index("mode")
    z, y, x = scan // 4, lax.rem(scan // 2, 2), lax.rem(scan, 2)
    partner = (scan, 1 - mode)
    peer_x = mesh_peer(scan, mode, planes, 1, 0, 0)
    peer_y = mesh_peer(scan, mode, planes, 0, 1, 0)
    peers_z = [mesh_peer(scan, mode, planes, 0, 0, k) for k in range(1, planes)]
    first_peer, second_peer = (peer_x, peer_y), (peer_y, peer_x)
    first_at, second_at = (x, y), (y, x)
    h, q, e = size // 2, size // 4, size // 4 // planes

    barrier = pltpu.get_barrier_semaphore()
    everyone = [partner] + [(lax.rem(scan + k, devices), mode) for k in range(1, devices)]
    for peer in everyone:
        pl.semaphore_signal(barrier, inc=1, device_id=peer, device_id_type=MESH)

    def probe_load(m):
        return pltpu.make_async_copy(probe_hbm.at[m], probe.at[m], load_probe.at[m])

    whole = [(patch_hbm, patch), (left_hbm, left), (right_hbm, right), (measured_hbm, measured)]
    loads = [pltpu.make_async_copy(src, dst, load.at[i]) for i, (src, dst) in enumerate(whole)]
    probe_load(0).start()
    for copy in loads:
        copy.start()
    for m in range(1, modes):
        probe_load(m).start()
    for copy in loads:
        copy.wait()
    pl.semaphore_wait(barrier, len(everyone))

    def remote(src, dst, send_sem, recv_sem, peer):
        return pltpu.make_async_remote_copy(
            src_ref=src, dst_ref=dst, send_sem=send_sem, recv_sem=recv_sem, device_id=peer, device_id_type=MESH
        )

    def rows(start, count, step):
        return pl.ds(pl.multiple_of(start, step), count)

    def copy1(m, c):
        away = rows((1 - first_at[c]) * h, h, h)
        return remote(term.at[m, c, away], got1.at[m, c], send.at[0, m, c], recv.at[0, m, c], first_peer[c])

    def copy2(m, c):
        away = rows((1 - second_at[c]) * q, q, q)
        return remote(sum1.at[m, c, away], got2.at[m, c], send.at[1, m, c], recv.at[1, m, c], second_peer[c])

    def copy3(m, c, k):
        away = rows(lax.rem(z + k, planes) * e, e, e)
        return remote(
            sum2.at[m, c, away], got3.at[m, c, k - 1], send_z.at[m, c, k - 1], recv_z.at[m, c, k - 1], peers_z[k - 1]
        )

    def base(c):
        return first_at[c] * h + second_at[c] * q

    def copy4(m, c, k):
        own = result.at[m, c, rows(base(c) + z * e, e, e)]
        return remote(own, own, ship_z.at[m, c, k - 1], land_z.at[m, c, k - 1], peers_z[k - 1])

    def copy5(m, c):
        own = result.at[m, c, rows(base(c), q, q)]
        return remote(own, own, send.at[2, m, c], recv.at[2, m, c], second_peer[c])

    def copy6(m, c):
        own = result.at[m, c, rows(first_at[c] * h, h, h)]
        return remote(own, own, send.at[3, m, c], recv.at[3, m, c], first_peer[c])

    def start(stage, m):
        for c in range(2):
            if stage in (3, 4):
                for k in range(1, planes):
                    (copy3, copy4)[stage - 3](m, c, k).start()
            else:
                {1: copy1, 2: copy2, 5: copy5, 6: copy6}[stage](m, c).start()

    def finish(stage, m):
        for c in range(2):
            if stage == 1:
                copy1(m, c).wait_recv()
                mine = term[m, c, rows(first_at[c] * h, h, h)].astype(F32)
                sum1[m, c] = (mine + got1[m, c].astype(F32)).astype(BF16)
            if stage == 2:
                copy2(m, c).wait_recv()
                mine = sum1[m, c, rows(second_at[c] * q, q, q)].astype(F32)
                sum2[m, c] = (mine + got2[m, c].astype(F32)).astype(BF16)
            if stage == 3:
                total = sum2[m, c, rows(z * e, e, e)].astype(F32)
                for k in range(1, planes):
                    copy3(m, c, k).wait_recv()
                    total = total + got3[m, c, k - 1].astype(F32)
                result[m, c, rows(base(c) + z * e, e, e)] = total.astype(BF16)
            if stage == 4:
                for k in range(1, planes):
                    copy4(m, c, k).wait_recv()
            if stage == 5:
                copy5(m, c).wait_recv()
            if stage == 6:
                copy6(m, c).wait_recv()

    def swap(i):
        at = rows(i * TILE, TILE, TILE)
        return remote(power.at[at], power_in.at[at], swap_send.at[i], swap_recv.at[i], partner)

    def product(table, source):
        for c in range(2):

            def down(i, carry, c=c):
                at = rows(c * size + i * TILE, TILE, TILE)
                out = jnp.dot(table[at], source[...], preferred_element_type=F32)
                half[rows(i * TILE, TILE, TILE), c * size : (c + 1) * size] = out.astype(BF16)
                return carry

            lax.fori_loop(0, size // TILE, down, 0)

    def part(i):
        at = rows(i * TILE, TILE, TILE)
        return remote(grad.at[1 - mode, at], grad_in.at[at], part_send.at[i], part_recv.at[i], partner)

    deep = pieces.shape[0] // devices
    mine = rows(scan * deep, deep, deep)

    def one_hot(mask):
        return jnp.where(mask, 1.0, 0.0).astype(BF16)

    def piece(k):
        to = lax.rem(scan + k, devices)
        return remote(pieces.at[rows(to * deep, deep, deep)], landed.at[mine], piece_send.at[k - 1], piece_recv.at[k - 1], (to, mode))

    def arrive(k):
        come = lax.rem(scan + devices - k, devices)
        at = rows(come * deep, deep, deep)
        return remote(pieces.at[at], landed.at[at], piece_send.at[k - 1], piece_recv.at[k - 1], (come, mode))

    def strip_swap():
        return remote(strip_grad.at[mode], strip_grad.at[mode], strip_send, strip_recv, partner)

    def cut_pieces():
        for i in range(size // TILE):
            part(i).wait_recv()
            at = pl.ds(i * TILE, TILE)
            summed[at] = (grad[mode, at] + grad_in[at]).astype(BF16)
        ahead = lax.broadcasted_iota(jnp.int32, (deep, size), 1) - lax.broadcasted_iota(jnp.int32, (deep, size), 0)

        def pick(j, carry):
            wave[rows(j * deep, deep, deep)] = one_hot(ahead == strips[j] * strip - row[0])
            return carry

        lax.fori_loop(0, devices, pick, 0)

        def move(i, carry):
            at = rows(i * TILE, TILE, TILE)
            pieces[at] = jnp.dot(wave[at], summed[...], preferred_element_type=F32).astype(BF16)
            return carry

        lax.fori_loop(0, devices * deep // TILE, move, 0)
        landed[mine] = pieces[mine]

    def add_pieces():
        for k in range(1, devices):
            arrive(k).wait_recv()
        strip_grad[mode] = jnp.zeros((strip, width), F32)
        parts = size // LANES
        ahead = lax.broadcasted_iota(jnp.int32, (LANES, 2 * LANES), 1)
        ahead = ahead - lax.broadcasted_iota(jnp.int32, (LANES, 2 * LANES), 0)

        def one(j, carry):
            turn = one_hot(ahead == lax.rem(cols[j], LANES))
            blocks = jnp.concatenate(
                [landed[rows(j * deep, deep, deep), b * LANES : (b + 1) * LANES] for b in range(parts)]
            )
            moved = jnp.dot(blocks, turn, preferred_element_type=F32)
            for b in range(parts + 1):
                here = moved[b * deep : b * deep + strip, :LANES] if b < parts else 0.0
                if b > 0:
                    here = here + moved[(b - 1) * deep : (b - 1) * deep + strip, LANES:]
                for t in range((width - size) // LANES + 1):
                    if b + t < width // LANES:
                        to = slice((b + t) * LANES, (b + t + 1) * LANES)
                        strip_grad[mode, :, to] += jnp.where(cols[j] // LANES == t, here, 0.0)
            return carry

        lax.fori_loop(0, devices, one, 0)
        strip_swap().start()

    def forward(m, carry):
        probe_load(m).wait()

        def leave(i, carry):
            at, low = rows(i * 64, 64, 64), rows(size + i * 64, 64, 64)
            pr, pi, xr, xi = probe[m, 0, at], probe[m, 1, at], patch[0, at], patch[1, at]
            wave[at] = (pr * xr - pi * xi).astype(BF16)
            wave[low] = (pr * xi + pi * xr).astype(BF16)
            return carry

        lax.fori_loop(0, size // 64, leave, 0)
        product(left, wave)

        def across(i, carry):
            at = rows(i * TILE, TILE, TILE)
            both = jnp.dot(half[at], right[...], preferred_element_type=F32)
            re, im = both[:, :size], both[:, size:]
            far[m, 0, at] = re
            far[m, 1, at] = im
            here = re * re + im * im
            power[at] = jnp.where(m == 0, here, power[at] + here)

            @pl.when(m == modes - 1)
            def _():
                swap(i).start()

            return carry

        lax.fori_loop(0, size // TILE, across, 0)
        return carry

    lax.fori_loop(0, modes, forward, 0)
    for i in range(size // TILE):
        at = pl.ds(i * TILE, TILE)
        swap(i).wait_recv()
        total = jnp.maximum(power[at] + power_in[at], 0.25)
        scale[at] = 1.0 - measured[at] / jnp.sqrt(total)

    def backward(m, carry):
        def residual(i, carry):
            at, low = rows(i * 64, 64, 64), rows(size + i * 64, 64, 64)
            wave[at] = (far[m, 0, at] * scale[at]).astype(BF16)
            wave[low] = (far[m, 1, at] * scale[at]).astype(BF16)
            return carry

        lax.fori_loop(0, size // 64, residual, 0)
        product(right, wave)

        def across(i, carry):
            at = rows(i * TILE, TILE, TILE)
            both = jnp.dot(half[at], left[...], preferred_element_type=F32)
            br, bi = both[:, :size], both[:, size:]
            pr, pi, xr, xi = probe[m, 0, at], probe[m, 1, at], patch[0, at], patch[1, at]
            term[m, 0, at] = (xr * br + xi * bi).astype(BF16)
            term[m, 1, at] = (xr * bi - xi * br).astype(BF16)
            re, im = pr * br + pi * bi, pr * bi - pi * br
            grad[0, at] = jnp.where(m == 0, re, grad[0, at] + re)
            grad[1, at] = jnp.where(m == 0, im, grad[1, at] + im)

            @pl.when(m == modes - 1)
            def _():
                part(i).start()

            return carry

        lax.fori_loop(0, size // TILE, across, 0)
        start(1, m)

        @pl.when(m >= 2)
        def _():
            finish(1, m - 2)
            start(2, m - 2)

        return carry

    lax.fori_loop(0, modes, backward, 0)
    steps = sorted((m + s, -s, m, s) for m in range(modes) for s in range(1, 7) if s > 1 or m >= modes - 2)
    cut_pieces()
    for _, _, m, s in steps:
        if (m, s) == (1, 6):
            add_pieces()
        finish(s, m)
        if s < 6:
            start(s + 1, m)
        if s == 3:
            for k in range(1 + m, devices, modes):
                piece(k).start()

    def drain(m, carry):
        for c in range(2):
            for copy in (copy1, copy2, copy5, copy6):
                copy(m, c).wait_send()
            for k in range(1, planes):
                copy3(m, c, k).wait_send()
                copy4(m, c, k).wait_send()
        return carry

    lax.fori_loop(0, modes, drain, 0)
    for i in range(size // TILE):
        swap(i).wait_send()
        part(i).wait_send()
    for k in range(1, devices):
        piece(k).wait_send()
    strip_swap().wait()


def place_kernel(strips, row, grad, out, padded):
    count, parts, rows, size = out.shape
    padded[...] = jnp.zeros_like(padded)
    padded[:, rows : rows + size, :] = grad[...]

    def one(j, carry):
        start = jnp.clip(strips[j] * rows - row[0], -rows, size) + rows
        base = pl.ds(pl.multiple_of(start // 8 * 8, 8), rows + 8)
        up = lax.rem(rows + 8 - lax.rem(start, 8), rows + 8)
        for k in range(parts):
            out[j, k] = pltpu.roll(padded[k, base, :], up, 0)[:rows]
        return carry

    lax.fori_loop(0, count, one, 0)


def add_kernel(cols, received, out, total):
    count, parts, rows, size = received.shape
    total[...] = jnp.zeros_like(total)
    edge = jnp.zeros((rows, LANES), F32)

    def one(j, carry):
        across = pl.ds(pl.multiple_of(cols[j] // LANES * LANES, LANES), size + LANES)
        shift = lax.rem(cols[j], LANES)
        for k in range(parts):
            piece = jnp.concatenate([received[j, k], edge], axis=1)
            total[k, :, across] += pltpu.roll(piece, shift, 1)
        return carry

    lax.fori_loop(0, count, one, 0)
    out[...] = total[:, :, : out.shape[-1]]


def shards(object_field, probe, amplitude, pos_row, pos_col, strip_of):
    size = probe.shape[-1]
    modes = probe.shape[0]
    rows, cols = object_field.shape[1], object_field.shape[2]
    devices, groups = lax.axis_size("scan"), lax.axis_size("mode")
    padded_cols = cols + LANES
    forward, inverse = dft_tables(size)

    def swap(x):
        return lax.ppermute(x, "mode", [(0, 1), (1, 0)])

    lane = lax.broadcasted_iota(jnp.int32, (2, META, cols), 2)
    numbers = jnp.where(lane == 0, strip_of[0], jnp.where(lane == 1, pos_col[0] // LANES, pos_col[0] % LANES))
    packed = jnp.concatenate([object_field.astype(BF16), numbers.astype(BF16)], axis=1)
    me = lax.axis_index("mode")
    if groups == 2 and devices % PLANE == 0:
        dma, lines = pltpu.SemaphoreType.DMA, devices // PLANE
        held = pl.pallas_call(
            gather_kernel,
            out_shape=jax.ShapeDtypeStruct((2, devices, rows + META, cols), BF16),
            in_specs=[VMEM],
            out_specs=VMEM,
            scratch_shapes=[
                dma((max(lines - 1, 1),)),
                dma((max(lines - 1, 1),)),
                dma((lines, PLANE - 1)),
                dma((lines, PLANE - 1)),
                dma,
                dma,
            ],
            compiler_params=pltpu.CompilerParams(
                vmem_limit_bytes=56 * 1024 * 1024, collective_id=0, has_side_effects=True
            ),
        )(lax.dynamic_index_in_dim(packed, me, 0, keepdims=False))
    else:
        held = lax.all_gather(packed, "scan", axis=1)
    numbers = held[0, :, rows, :3].astype(jnp.int32)
    strips = numbers[:, 0]
    all_cols = numbers[:, 1] * LANES + numbers[:, 2]

    wave_shape = jax.ShapeDtypeStruct((2, size, size), F32)
    patch = pl.pallas_call(
        cut_kernel,
        out_shape=wave_shape,
        in_specs=[SMEM, SMEM, SMEM, VMEM],
        out_specs=VMEM,
        scratch_shapes=[pltpu.VMEM((2, devices * rows + 8, padded_cols), F32)],
        compiler_params=PARAMS,
    )(strips, pos_row, pos_col, held)

    def whole(*shape):
        return pl.BlockSpec(shape, lambda m: (0,) * len(shape))

    mode_spec = pl.BlockSpec((1, 2, size, size), lambda m: (m, 0, 0, 0))
    table_spec = whole(2 * size, 2 * size)
    buffers = [pltpu.VMEM((2 * size, size), BF16), pltpu.VMEM((size, 2 * size), BF16)]
    planes, deep = devices // 4, -(-rows // 16) * 16
    fits = groups == 2 and devices == 4 * planes and planes >= 2 and size % (64 * planes) == 0
    if fits and rows % 8 == 0 and devices * deep % TILE == 0 and devices * deep <= 2 * size:
        dma = pltpu.SemaphoreType.DMA
        h, q, e = size // 2, size // 4, size // 4 // planes
        vmem = pltpu.VMEM
        any_space = pl.BlockSpec(memory_space=pl.ANY)
        term, strip_grad = pl.pallas_call(
            core_kernel,
            out_shape=(
                jax.ShapeDtypeStruct((modes, 2, size, size), BF16),
                jax.ShapeDtypeStruct((2, rows, cols), F32),
            ),
            in_specs=[SMEM] * 3 + [any_space] * 5,
            out_specs=(VMEM, VMEM),
            scratch_shapes=[
                vmem((modes, 2, size, size), F32),
                vmem((2, size, size), F32),
                vmem((size, size), F32),
                vmem((2 * size, 2 * size), BF16),
                vmem((2 * size, 2 * size), BF16),
                vmem((modes, 2, size, size), F32),
                vmem((size, size), F32),
                vmem((size, size), F32),
                vmem((size, size), F32),
                vmem((2 * size, size), BF16),
                vmem((size, 2 * size), BF16),
                vmem((modes, 2, size, size), BF16),
                vmem((modes, 2, h, size), BF16),
                vmem((modes, 2, h, size), BF16),
                vmem((modes, 2, q, size), BF16),
                vmem((modes, 2, q, size), BF16),
                vmem((modes, 2, planes - 1, e, size), BF16),
                vmem((2, size, size), F32),
                vmem((size, size), F32),
                vmem((size, size), BF16),
                vmem((devices * deep, size), BF16),
                vmem((devices * deep, size), BF16),
                dma((4,)),
                dma((modes,)),
                dma((size // TILE,)),
                dma((size // TILE,)),
                dma((4, modes, 2)),
                dma((4, modes, 2)),
                dma((modes, 2, planes - 1)),
                dma((modes, 2, planes - 1)),
                dma((modes, 2, planes - 1)),
                dma((modes, 2, planes - 1)),
                dma((size // TILE,)),
                dma((size // TILE,)),
                dma((devices - 1,)),
                dma((devices - 1,)),
                dma,
                dma,
            ],
            compiler_params=pltpu.CompilerParams(
                vmem_limit_bytes=58 * 1024 * 1024, collective_id=1, has_side_effects=True
            ),
        )(strips, pos_row, all_cols, probe, patch, amplitude[0], forward, inverse)
        return (strip_grad, term.astype(F32))

    far, power = pl.pallas_call(
        forward_kernel,
        grid=(modes,),
        out_shape=(
            jax.ShapeDtypeStruct((modes, 2, size, size), F32),
            jax.ShapeDtypeStruct((size, size), F32),
        ),
        in_specs=[mode_spec, whole(2, size, size), table_spec, table_spec],
        out_specs=(mode_spec, whole(size, size)),
        scratch_shapes=buffers,
        compiler_params=PARAMS,
    )(probe, patch, forward, inverse)
    power = power + swap(power) if groups == 2 else lax.psum(power, "mode")
    term, grad = pl.pallas_call(
        backward_kernel,
        grid=(modes,),
        out_shape=(jax.ShapeDtypeStruct((modes, 2, size, size), BF16), wave_shape),
        in_specs=[
            mode_spec,
            mode_spec,
            whole(2, size, size),
            whole(size, size),
            whole(size, size),
            table_spec,
            table_spec,
        ],
        out_specs=(mode_spec, whole(2, size, size)),
        scratch_shapes=[pltpu.VMEM((size, size), F32)] + buffers,
        compiler_params=PARAMS,
    )(far, probe, patch, amplitude[0], power, inverse, forward)
    probe_grad = lax.psum(term, "scan").astype(F32)

    if groups == 2:
        mine = lax.dynamic_index_in_dim(grad, me, 0, keepdims=True)
        other = lax.dynamic_index_in_dim(grad, 1 - me, 0, keepdims=True)
        grad = mine + swap(other)
    else:
        grad = lax.psum(grad, "mode")
    parts = grad.shape[0]
    pieces = pl.pallas_call(
        place_kernel,
        out_shape=jax.ShapeDtypeStruct((devices, parts, rows, size), F32),
        in_specs=[SMEM, SMEM, VMEM],
        out_specs=VMEM,
        scratch_shapes=[pltpu.VMEM((parts, size + 2 * rows + 8, size), F32)],
        compiler_params=PARAMS,
    )(strips, pos_row, grad)
    received = lax.all_to_all(pieces.astype(BF16), "scan", 0, 0, tiled=False).astype(F32)
    strip_grad = pl.pallas_call(
        add_kernel,
        out_shape=jax.ShapeDtypeStruct((parts, rows, cols), F32),
        in_specs=[SMEM, VMEM],
        out_specs=VMEM,
        scratch_shapes=[pltpu.VMEM((parts, rows, padded_cols), F32)],
        compiler_params=PARAMS,
    )(all_cols, received)
    if groups == 2:
        theirs = swap(strip_grad)
        strip_grad = jnp.where(
            me == 0,
            jnp.concatenate([strip_grad, theirs]),
            jnp.concatenate([theirs, strip_grad]),
        )
    return (strip_grad, probe_grad)


def solution(mesh):
    return jax.shard_map(
        shards,
        mesh=mesh,
        in_specs=(
            P(None, "scan", None),
            P("mode", None, None, None),
            P("scan", None, None),
            P("scan"),
            P("scan"),
            P("scan"),
        ),
        out_specs=(P(None, "scan", None), P("mode", None, None, None)),
        check_vma=False,
    )
```

```python
import math

import jax
import jax.numpy as jnp
import numpy as np
from jax import lax
from jax.experimental import pallas as pl
from jax.experimental.pallas import tpu as pltpu
from jax.sharding import PartitionSpec as P

F32 = jnp.float32
BF16 = jnp.bfloat16
LANES = 128
META = 8
PLANE = 4
TILE = 256
PARAMS = pltpu.CompilerParams(vmem_limit_bytes=56 * 1024 * 1024)
VMEM = pl.BlockSpec(memory_space=pltpu.VMEM)
SMEM = pl.BlockSpec(memory_space=pltpu.SMEM)
MESH = pl.DeviceIdType.MESH


def dft_tables(size):
    positions = np.arange(size, dtype=np.int32)
    angles = (positions[:, None] * positions[None, :] % size).astype(np.float32)
    angles = angles * np.float32(2.0 * math.pi / size)
    norm = np.float32(1.0 / math.sqrt(size))
    cosine, sine = np.cos(angles) * norm, np.sin(angles) * norm
    forward = np.block([[cosine, sine], [-sine, cosine]])
    inverse = np.block([[cosine, -sine], [sine, cosine]])
    return jnp.asarray(forward, BF16), jnp.asarray(inverse, BF16)


def gather_kernel(mine, out, line_send, line_recv, plane_send, plane_recv, swap_send, swap_recv):
    count = out.shape[1]
    lines = count // PLANE
    scan, mode = lax.axis_index("scan"), lax.axis_index("mode")
    line, place = scan // PLANE, lax.rem(scan, PLANE)
    in_line = [(lax.rem(line + k, lines) * PLANE + place, mode) for k in range(1, lines)]
    in_plane = [(line * PLANE + lax.rem(place + t, PLANE), mode) for t in range(1, PLANE)]
    partner = (scan, 1 - mode)

    barrier = pltpu.get_barrier_semaphore()
    for peer in in_line + in_plane + [partner]:
        pl.semaphore_signal(barrier, inc=1, device_id=peer, device_id_type=pl.DeviceIdType.MESH)
    pl.semaphore_wait(barrier, len(in_line) + len(in_plane) + 1)

    def push(src, dst, send, recv, peer):
        copy = pltpu.make_async_remote_copy(
            src_ref=src,
            dst_ref=dst,
            send_sem=send,
            recv_sem=recv,
            device_id=peer,
            device_id_type=pl.DeviceIdType.MESH,
        )
        copy.start()
        return copy

    own = out.at[mode, scan]
    line_copies = [
        push(mine, own, line_send.at[k], line_recv.at[k], peer) for k, peer in enumerate(in_line)
    ]
    plane_copies = [
        push(mine, own, plane_send.at[0, t], plane_recv.at[0, t], peer) for t, peer in enumerate(in_plane)
    ]
    out[mode, scan] = mine[...]
    for k, arriving in enumerate(line_copies):
        arriving.wait_recv()
        piece = out.at[mode, lax.rem(line + lines - k - 1, lines) * PLANE + place]
        plane_copies += [
            push(piece, piece, plane_send.at[k + 1, t], plane_recv.at[k + 1, t], peer)
            for t, peer in enumerate(in_plane)
        ]
    for copy in plane_copies:
        copy.wait_recv()
    last = push(out.at[mode], out.at[mode], swap_send, swap_recv, partner)
    for copy in line_copies + plane_copies:
        copy.wait_send()
    last.wait()


def cut_kernel(strips, row, col, held, patch, window):
    count, rows = held.shape[1], held.shape[2] - META
    size, cols = patch.shape[-1], held.shape[-1]
    wide = size + LANES

    def place(j, carry):
        at = pl.ds(pl.multiple_of(strips[j] * rows, 8), rows)
        for c in range(2):
            window[c, at, :cols] = held[c, j].astype(F32)[:rows]
        return carry

    lax.fori_loop(0, count, place, 0)
    across = pl.ds(pl.multiple_of(col[0] // LANES * LANES, LANES), wide)
    back = lax.rem(wide - lax.rem(col[0], LANES), wide)
    up = lax.rem(72 - lax.rem(row[0], 8), 72)
    for c in range(2):

        def cut(i, carry, c=c):
            block = window[c, pl.ds(pl.multiple_of(row[0] // 8 * 8 + i * 64, 8), 72), across]
            block = pltpu.roll(block, up, 0)[:64]
            patch[c, pl.ds(pl.multiple_of(i * 64, 64), 64), :] = pltpu.roll(block, back, 1)[:, :size]
            return carry

        lax.fori_loop(0, size // 64, cut, 0)


def forward_kernel(probe, patch, left, right, far, power, wave, half):
    size = patch.shape[-1]

    def leave(i, carry):
        at = pl.ds(pl.multiple_of(i * 64, 64), 64)
        low = pl.ds(pl.multiple_of(size + i * 64, 64), 64)
        pr, pi, xr, xi = probe[0, 0, at], probe[0, 1, at], patch[0, at], patch[1, at]
        wave[at] = (pr * xr - pi * xi).astype(BF16)
        wave[low] = (pr * xi + pi * xr).astype(BF16)
        return carry

    lax.fori_loop(0, size // 64, leave, 0)
    rows_product(left, wave, half)
    first = pl.program_id(0) == 0

    def across(i, carry):
        at = pl.ds(pl.multiple_of(i * TILE, TILE), TILE)
        both = jnp.dot(half[at], right[...], preferred_element_type=F32)
        re, im = both[:, :size], both[:, size:]
        far[0, 0, at] = re
        far[0, 1, at] = im
        here = re * re + im * im
        power[at] = jnp.where(first, here, power[at] + here)
        return carry

    lax.fori_loop(0, size // TILE, across, 0)


def rows_product(left, wave, half):
    size = wave.shape[-1]
    for c in range(2):

        def down(i, carry, c=c):
            at = pl.ds(pl.multiple_of(c * size + i * TILE, TILE), TILE)
            to = pl.ds(pl.multiple_of(i * TILE, TILE), TILE)
            product = jnp.dot(left[at], wave[...], preferred_element_type=F32)
            half[to, c * size : (c + 1) * size] = product.astype(BF16)
            return carry

        lax.fori_loop(0, size // TILE, down, 0)


def backward_kernel(far, probe, patch, measured, power, left, right, term, grad, scale, wave, half):
    size = patch.shape[-1]
    first = pl.program_id(0) == 0

    @pl.when(first)
    def _():
        total = jnp.maximum(power[...], 0.25)
        scale[...] = 1.0 - measured[...] / jnp.sqrt(total)

    def residual(i, carry):
        at = pl.ds(pl.multiple_of(i * 64, 64), 64)
        low = pl.ds(pl.multiple_of(size + i * 64, 64), 64)
        wave[at] = (far[0, 0, at] * scale[at]).astype(BF16)
        wave[low] = (far[0, 1, at] * scale[at]).astype(BF16)
        return carry

    lax.fori_loop(0, size // 64, residual, 0)
    rows_product(left, wave, half)

    def across(i, carry):
        at = pl.ds(pl.multiple_of(i * TILE, TILE), TILE)
        both = jnp.dot(half[at], right[...], preferred_element_type=F32)
        br, bi = both[:, :size], both[:, size:]
        pr, pi, xr, xi = probe[0, 0, at], probe[0, 1, at], patch[0, at], patch[1, at]
        term[0, 0, at] = (xr * br + xi * bi).astype(BF16)
        term[0, 1, at] = (xr * bi - xi * br).astype(BF16)
        re, im = pr * br + pi * bi, pr * bi - pi * br
        grad[0, at] = jnp.where(first, re, grad[0, at] + re)
        grad[1, at] = jnp.where(first, im, grad[1, at] + im)
        return carry

    lax.fori_loop(0, size // TILE, across, 0)


def mesh_peer(scan, mode, planes, dx, dy, dz):
    z, y, x = scan // 4, lax.rem(scan // 2, 2), lax.rem(scan, 2)
    x, y = lax.rem(x + dx, 2), lax.rem(y + dy, 2)
    return (lax.rem(z + dz, planes) * 4 + y * 2 + x, mode)


def core_kernel(
    strip_of, row, col, field, probe_hbm, measured_hbm, left_hbm, right_hbm, result, strip_grad,
    metas, held_a, held_b, col_hot, row_hot, cut, probe, patch, measured, left, right,
    far, power, power_in, scale, wave, half, term, got1, sum1, got2, sum2, got3,
    grad, grad_in, summed, pieces, landed,
    load, load_probe, meta_send, meta_recv, hop_send, hop_recv, swap_send, swap_recv, send, recv,
    send_z, recv_z, ship_z, land_z, part_send, part_recv, piece_send, piece_recv, strip_send, strip_recv,
):
    modes, size = probe.shape[0], patch.shape[-1]
    devices = lax.axis_size("scan")
    strip, width = strip_grad.shape[1], strip_grad.shape[2]
    planes = got3.shape[2] + 1
    scan, mode = lax.axis_index("scan"), lax.axis_index("mode")
    z, y, x = scan // 4, lax.rem(scan // 2, 2), lax.rem(scan, 2)
    partner = (scan, 1 - mode)
    peer_x = mesh_peer(scan, mode, planes, 1, 0, 0)
    peer_y = mesh_peer(scan, mode, planes, 0, 1, 0)
    peers_z = [mesh_peer(scan, mode, planes, 0, 0, k) for k in range(1, planes)]
    first_peer, second_peer = (peer_x, peer_y), (peer_y, peer_x)
    first_at, second_at = (x, y), (y, x)
    h, q, e = size // 2, size // 4, size // 4 // planes
    deep = pieces.shape[0] // devices

    barrier = pltpu.get_barrier_semaphore()
    everyone = [partner] + [(lax.rem(scan + k, devices), mode) for k in range(1, devices)]
    for peer in everyone:
        pl.semaphore_signal(barrier, inc=1, device_id=peer, device_id_type=MESH)

    def probe_load(m):
        return pltpu.make_async_copy(probe_hbm.at[m], probe.at[m], load_probe.at[m])

    whole = [(left_hbm, left), (right_hbm, right), (measured_hbm, measured)]
    loads = [pltpu.make_async_copy(src, dst, load.at[i]) for i, (src, dst) in enumerate(whole)]
    probe_load(0).start()
    for copy in loads:
        copy.start()
    for m in range(1, modes):
        probe_load(m).start()

    def rows(start, count, step):
        return pl.ds(pl.multiple_of(start, step), count)

    def one_hot(mask):
        return jnp.where(mask, 1.0, 0.0).astype(BF16)

    held, parts_at = (held_a, held_b), (0, held_a.shape[1], width)
    plane, plane_x, plane_y = y * 2 + x, y * 2 + 1 - x, (1 - y) * 2 + x
    plane_d = (1 - y) * 2 + 1 - x

    levels = (z, z + 1 - 2 * lax.rem(z, 2), z + 2 - 4 * (z // 2), 3 - z)

    def strip_rows(side, k):
        return rows((side * planes + levels[k]) * deep, deep, deep)

    own = jnp.concatenate([field[mode].astype(BF16), jnp.zeros((deep - strip, width), BF16)])
    for i in range(2):
        held[i][strip_rows(plane, 0)] = own[:, parts_at[i] : parts_at[i + 1]]
    which = lax.broadcasted_iota(jnp.int32, (8, LANES), 0)
    numbers = jnp.where(which == 1, lax.rem(col[0], LANES), col[0] // LANES)
    metas[scan] = jnp.where(which == 0, strip_of[0], numbers)
    pl.semaphore_wait(barrier, len(everyone))

    def remote(src, dst, send_sem, recv_sem, peer):
        return pltpu.make_async_remote_copy(
            src_ref=src, dst_ref=dst, send_sem=send_sem, recv_sem=recv_sem, device_id=peer, device_id_type=MESH
        )

    def meta(k, back=0):
        at = lax.rem(scan + devices - back, devices)
        to = (lax.rem(scan + k, devices), mode)
        return remote(metas.at[at], metas.at[at], meta_send.at[k - 1], meta_recv.at[k - 1], to)

    def hop(kind, i, k, side, peer):
        at = held[i].at[strip_rows(side, k)]
        return remote(at, at, hop_send.at[kind, i, k], hop_recv.at[kind, i, k], peer)

    def hop_z(i, k):
        at = held[i].at[strip_rows(plane, 0)]
        return remote(at, at, hop_send.at[0, i, k], hop_recv.at[0, i, k], (levels[k] * 4 + plane, mode))

    def spread(k):
        for i in range(2):
            hop(1, i, k, plane, peer_x).start()
            hop(2, 1 - i, k, plane, peer_y).start()

    def relay(k):
        hop(1, 0, k, plane_x, peer_x).wait_recv()
        hop(3, 0, k, plane_x, peer_y).start()
        hop(2, 1, k, plane_y, peer_y).wait_recv()
        hop(3, 1, k, plane_y, peer_x).start()

    def cut_columns(side):
        at = rows(side * planes * deep, planes * deep, planes * deep)
        got = jnp.dot(held_a[at], col_hot[: held_a.shape[1]], preferred_element_type=F32)
        got = got + jnp.dot(held_b[at], col_hot[held_a.shape[1] :], preferred_element_type=F32)
        cut[at] = got.astype(BF16)

    def patch_swap(i):
        at = rows(i * TILE, TILE, TILE)
        own = patch.at[mode, at]
        return remote(own, own, hop_send.at[4, i, 0], hop_recv.at[4, i, 0], partner)

    def across_lanes(row_values, count):
        return jnp.concatenate([row_values] * (count // LANES), axis=1)

    for k in range(1, devices):
        meta(k).start()
    for k in range(1, planes):
        hop_z(0, k).start()
        hop_z(1, k).start()
    spread(0)

    def column_hot(i, carry):
        at = rows(i * LANES, LANES, LANES)
        lane = lax.broadcasted_iota(jnp.int32, (LANES, size), 1)
        col_hot[at] = one_hot(lax.broadcasted_iota(jnp.int32, (LANES, size), 0) + i * LANES - lane == col[0])
        return carry

    lax.fori_loop(0, width // LANES, column_hot, 0)
    for k in range(1, planes):
        hop(0, 0, k, plane, partner).wait_recv()
        hop(0, 1, k, plane, partner).wait_recv()
        spread(k)
        relay(k - 1)
    cut_columns(plane)
    relay(planes - 1)
    for k in range(1, devices):
        meta(k, k).wait_recv()
    lane = lax.broadcasted_iota(jnp.int32, (8, devices * deep), 1)
    target = jnp.full((8, devices * deep), -1, jnp.int32)
    for j in range(devices):
        ahead = lane - (j % 4 * planes + j // 4) * deep
        target = jnp.where(
            (ahead >= 0) & (ahead < strip), across_lanes(metas[j, :1], devices * deep) * strip + ahead, target
        )
    target = target[:1] - row[0]

    def line_hot(i, carry):
        at = rows(i * 64, 64, 64)
        line = lax.broadcasted_iota(jnp.int32, (64, devices * deep), 0) + i * 64
        row_hot[at] = one_hot(line == target)
        return carry

    lax.fori_loop(0, size // 64, line_hot, 0)
    for k in range(planes):
        hop(1, 1, k, plane_x, peer_x).wait_recv()
    cut_columns(plane_x)
    for k in range(planes):
        hop(2, 0, k, plane_y, peer_y).wait_recv()
    cut_columns(plane_y)
    for k in range(planes):
        hop(3, 0, k, plane_d, peer_y).wait_recv()
        hop(3, 1, k, plane_d, peer_x).wait_recv()
    cut_columns(plane_d)
    for i in range(size // TILE):
        at = pl.ds(i * TILE, TILE)
        patch[mode, at] = jnp.dot(row_hot[at], cut[...], preferred_element_type=F32).astype(BF16)
        patch_swap(i).start()
    for copy in loads:
        copy.wait()
    for i in range(size // TILE):
        patch_swap(i).wait_recv()

    def copy1(m, c):
        away = rows((1 - first_at[c]) * h, h, h)
        return remote(term.at[m, c, away], got1.at[m, c], send.at[0, m, c], recv.at[0, m, c], first_peer[c])

    def copy2(m, c):
        away = rows((1 - second_at[c]) * q, q, q)
        return remote(sum1.at[m, c, away], got2.at[m, c], send.at[1, m, c], recv.at[1, m, c], second_peer[c])

    def copy3(m, c, k):
        away = rows(lax.rem(z + k, planes) * e, e, e)
        return remote(
            sum2.at[m, c, away], got3.at[m, c, k - 1], send_z.at[m, c, k - 1], recv_z.at[m, c, k - 1], peers_z[k - 1]
        )

    def base(c):
        return first_at[c] * h + second_at[c] * q

    def copy4(m, c, k):
        own = result.at[m, c, rows(base(c) + z * e, e, e)]
        return remote(own, own, ship_z.at[m, c, k - 1], land_z.at[m, c, k - 1], peers_z[k - 1])

    def copy5(m, c):
        own = result.at[m, c, rows(base(c), q, q)]
        return remote(own, own, send.at[2, m, c], recv.at[2, m, c], second_peer[c])

    def copy6(m, c):
        own = result.at[m, c, rows(first_at[c] * h, h, h)]
        return remote(own, own, send.at[3, m, c], recv.at[3, m, c], first_peer[c])

    def start(stage, m):
        for c in range(2):
            if stage in (3, 4):
                for k in range(1, planes):
                    (copy3, copy4)[stage - 3](m, c, k).start()
            else:
                {1: copy1, 2: copy2, 5: copy5, 6: copy6}[stage](m, c).start()

    def finish(stage, m):
        for c in range(2):
            if stage == 1:
                copy1(m, c).wait_recv()
                mine = term[m, c, rows(first_at[c] * h, h, h)].astype(F32)
                sum1[m, c] = (mine + got1[m, c].astype(F32)).astype(BF16)
            if stage == 2:
                copy2(m, c).wait_recv()
                mine = sum1[m, c, rows(second_at[c] * q, q, q)].astype(F32)
                sum2[m, c] = (mine + got2[m, c].astype(F32)).astype(BF16)
            if stage == 3:
                total = sum2[m, c, rows(z * e, e, e)].astype(F32)
                for k in range(1, planes):
                    copy3(m, c, k).wait_recv()
                    total = total + got3[m, c, k - 1].astype(F32)
                result[m, c, rows(base(c) + z * e, e, e)] = total.astype(BF16)
            if stage == 4:
                for k in range(1, planes):
                    copy4(m, c, k).wait_recv()
            if stage == 5:
                copy5(m, c).wait_recv()
            if stage == 6:
                copy6(m, c).wait_recv()

    def swap(i):
        at = rows(i * TILE, TILE, TILE)
        return remote(power.at[at], power_in.at[at], swap_send.at[i], swap_recv.at[i], partner)

    def product(table, source):
        for c in range(2):

            def down(i, carry, c=c):
                at = rows(c * size + i * TILE, TILE, TILE)
                out = jnp.dot(table[at], source[...], preferred_element_type=F32)
                half[rows(i * TILE, TILE, TILE), c * size : (c + 1) * size] = out.astype(BF16)
                return carry

            lax.fori_loop(0, size // TILE, down, 0)

    def part(i):
        at = rows(i * TILE, TILE, TILE)
        return remote(grad.at[1 - mode, at], grad_in.at[at], part_send.at[i], part_recv.at[i], partner)

    mine = rows(scan * deep, deep, deep)

    def piece(k):
        to = lax.rem(scan + k, devices)
        return remote(pieces.at[rows(to * deep, deep, deep)], landed.at[mine], piece_send.at[k - 1], piece_recv.at[k - 1], (to, mode))

    def arrive(k):
        come = lax.rem(scan + devices - k, devices)
        at = rows(come * deep, deep, deep)
        return remote(pieces.at[at], landed.at[at], piece_send.at[k - 1], piece_recv.at[k - 1], (come, mode))

    def strip_swap():
        return remote(strip_grad.at[mode], strip_grad.at[mode], strip_send, strip_recv, partner)

    def cut_pieces():
        for i in range(size // TILE):
            part(i).wait_recv()
            at = pl.ds(i * TILE, TILE)
            summed[at] = (grad[mode, at] + grad_in[at]).astype(BF16)
        ahead = lax.broadcasted_iota(jnp.int32, (deep, size), 1) - lax.broadcasted_iota(jnp.int32, (deep, size), 0)

        def pick(j, carry):
            begin = across_lanes(metas[j, :1], size) * strip - row[0]
            wave[rows(j * deep, deep, deep)] = one_hot(ahead == begin)
            return carry

        lax.fori_loop(0, devices, pick, 0)

        def move(i, carry):
            at = rows(i * TILE, TILE, TILE)
            pieces[at] = jnp.dot(wave[at], summed[...], preferred_element_type=F32).astype(BF16)
            return carry

        lax.fori_loop(0, devices * deep // TILE, move, 0)
        for k in range(1, devices):
            piece(k).start()
        landed[mine] = pieces[mine]

    def add_pieces():
        for k in range(1, devices):
            arrive(k).wait_recv()
        strip_grad[mode] = jnp.zeros((strip, width), F32)
        parts = size // LANES
        ahead = lax.broadcasted_iota(jnp.int32, (LANES, 2 * LANES), 1)
        ahead = ahead - lax.broadcasted_iota(jnp.int32, (LANES, 2 * LANES), 0)

        def one(j, carry):
            turn = one_hot(ahead == across_lanes(metas[j, 1:2], 2 * LANES))
            blocks = jnp.concatenate(
                [landed[rows(j * deep, deep, deep), b * LANES : (b + 1) * LANES] for b in range(parts)]
            )
            moved = jnp.dot(blocks, turn, preferred_element_type=F32)
            for b in range(parts + 1):
                here = moved[b * deep : b * deep + strip, :LANES] if b < parts else 0.0
                if b > 0:
                    here = here + moved[(b - 1) * deep : (b - 1) * deep + strip, LANES:]
                for t in range((width - size) // LANES + 1):
                    if b + t < width // LANES:
                        to = slice((b + t) * LANES, (b + t + 1) * LANES)
                        strip_grad[mode, :, to] += jnp.where(metas[j, 2:3] == t, here, 0.0)
            return carry

        lax.fori_loop(0, devices, one, 0)
        strip_swap().start()

    def forward(m, carry):
        probe_load(m).wait()

        def leave(i, carry):
            at, low = rows(i * 64, 64, 64), rows(size + i * 64, 64, 64)
            pr, pi, xr, xi = probe[m, 0, at], probe[m, 1, at], patch[0, at].astype(F32), patch[1, at].astype(F32)
            wave[at] = (pr * xr - pi * xi).astype(BF16)
            wave[low] = (pr * xi + pi * xr).astype(BF16)
            return carry

        lax.fori_loop(0, size // 64, leave, 0)
        product(left, wave)

        def across(i, carry):
            at = rows(i * TILE, TILE, TILE)
            both = jnp.dot(half[at], right[...], preferred_element_type=F32)
            re, im = both[:, :size], both[:, size:]
            far[m, 0, at] = re
            far[m, 1, at] = im
            here = re * re + im * im
            power[at] = jnp.where(m == 0, here, power[at] + here)

            @pl.when(m == modes - 1)
            def _():
                swap(i).start()

            return carry

        lax.fori_loop(0, size // TILE, across, 0)
        return carry

    lax.fori_loop(0, modes, forward, 0)
    for i in range(size // TILE):
        at = pl.ds(i * TILE, TILE)
        swap(i).wait_recv()
        total = jnp.maximum(power[at] + power_in[at], 0.25)
        scale[at] = 1.0 - measured[at] / jnp.sqrt(total)

    def backward(m, carry):
        def residual(i, carry):
            at, low = rows(i * 64, 64, 64), rows(size + i * 64, 64, 64)
            wave[at] = (far[m, 0, at] * scale[at]).astype(BF16)
            wave[low] = (far[m, 1, at] * scale[at]).astype(BF16)
            return carry

        lax.fori_loop(0, size // 64, residual, 0)
        product(right, wave)

        def across(i, carry):
            at = rows(i * TILE, TILE, TILE)
            both = jnp.dot(half[at], left[...], preferred_element_type=F32)
            br, bi = both[:, :size], both[:, size:]
            pr, pi, xr, xi = probe[m, 0, at], probe[m, 1, at], patch[0, at].astype(F32), patch[1, at].astype(F32)
            term[m, 0, at] = (xr * br + xi * bi).astype(BF16)
            term[m, 1, at] = (xr * bi - xi * br).astype(BF16)
            re, im = pr * br + pi * bi, pr * bi - pi * br
            grad[0, at] = jnp.where(m == 0, re, grad[0, at] + re)
            grad[1, at] = jnp.where(m == 0, im, grad[1, at] + im)

            @pl.when(m == modes - 1)
            def _():
                part(i).start()

            return carry

        lax.fori_loop(0, size // TILE, across, 0)
        start(1, m)

        @pl.when(m >= 2)
        def _():
            finish(1, m - 2)
            start(2, m - 2)

        return carry

    lax.fori_loop(0, modes, backward, 0)
    steps = sorted((m + s, -s, m, s) for m in range(modes) for s in range(1, 7) if s > 1 or m >= modes - 2)
    cut_pieces()
    for _, _, m, s in steps:
        if (m, s) == (1, 6):
            add_pieces()
        finish(s, m)
        if s < 6:
            start(s + 1, m)

    def drain(m, carry):
        for c in range(2):
            for copy in (copy1, copy2, copy5, copy6):
                copy(m, c).wait_send()
            for k in range(1, planes):
                copy3(m, c, k).wait_send()
                copy4(m, c, k).wait_send()
        return carry

    lax.fori_loop(0, modes, drain, 0)
    for i in range(size // TILE):
        swap(i).wait_send()
        part(i).wait_send()
    for k in range(1, devices):
        piece(k).wait_send()
    strip_swap().wait()
    for i in range(size // TILE):
        patch_swap(i).wait_send()
    for k in range(1, devices):
        meta(k).wait_send()
    for i in range(2):
        for k in range(planes):
            if k:
                hop_z(i, k).wait_send()
            hop(1, i, k, plane, peer_x).wait_send()
            hop(2, i, k, plane, peer_y).wait_send()
            hop(3, i, k, (plane_x, plane_y)[i], (peer_y, peer_x)[i]).wait_send()


def place_kernel(strips, row, grad, out, padded):
    count, parts, rows, size = out.shape
    padded[...] = jnp.zeros_like(padded)
    padded[:, rows : rows + size, :] = grad[...]

    def one(j, carry):
        start = jnp.clip(strips[j] * rows - row[0], -rows, size) + rows
        base = pl.ds(pl.multiple_of(start // 8 * 8, 8), rows + 8)
        up = lax.rem(rows + 8 - lax.rem(start, 8), rows + 8)
        for k in range(parts):
            out[j, k] = pltpu.roll(padded[k, base, :], up, 0)[:rows]
        return carry

    lax.fori_loop(0, count, one, 0)


def add_kernel(cols, received, out, total):
    count, parts, rows, size = received.shape
    total[...] = jnp.zeros_like(total)
    edge = jnp.zeros((rows, LANES), F32)

    def one(j, carry):
        across = pl.ds(pl.multiple_of(cols[j] // LANES * LANES, LANES), size + LANES)
        shift = lax.rem(cols[j], LANES)
        for k in range(parts):
            piece = jnp.concatenate([received[j, k], edge], axis=1)
            total[k, :, across] += pltpu.roll(piece, shift, 1)
        return carry

    lax.fori_loop(0, count, one, 0)
    out[...] = total[:, :, : out.shape[-1]]


def shards(object_field, probe, amplitude, pos_row, pos_col, strip_of):
    size = probe.shape[-1]
    modes = probe.shape[0]
    rows, cols = object_field.shape[1], object_field.shape[2]
    devices, groups = lax.axis_size("scan"), lax.axis_size("mode")
    padded_cols = cols + LANES
    forward, inverse = dft_tables(size)

    def swap(x):
        return lax.ppermute(x, "mode", [(0, 1), (1, 0)])

    planes, deep = devices // 4, -(-rows // 16) * 16
    fits = groups == 2 and devices == 4 * planes and planes == 4 and size % (64 * planes) == 0
    fits = fits and cols % LANES == 0 and size // TILE == 2
    if fits and rows % 8 == 0 and devices * deep % TILE == 0 and devices * deep <= 2 * size:
        dma = pltpu.SemaphoreType.DMA
        h, q, e = size // 2, size // 4, size // 4 // planes
        vmem, lanes = pltpu.VMEM, (cols // LANES + 1) // 2 * LANES
        any_space = pl.BlockSpec(memory_space=pl.ANY)
        term, strip_grad = pl.pallas_call(
            core_kernel,
            out_shape=(
                jax.ShapeDtypeStruct((modes, 2, size, size), BF16),
                jax.ShapeDtypeStruct((2, rows, cols), F32),
            ),
            in_specs=[SMEM] * 3 + [VMEM] + [any_space] * 4,
            out_specs=(VMEM, VMEM),
            scratch_shapes=[
                vmem((devices, 8, LANES), jnp.int32),
                vmem((devices * deep, lanes), BF16),
                vmem((devices * deep, cols - lanes), BF16),
                vmem((cols, size), BF16),
                vmem((size, devices * deep), BF16),
                vmem((devices * deep, size), BF16),
                vmem((modes, 2, size, size), F32),
                vmem((2, size, size), BF16),
                vmem((size, size), F32),
                vmem((2 * size, 2 * size), BF16),
                vmem((2 * size, 2 * size), BF16),
                vmem((modes, 2, size, size), F32),
                vmem((size, size), F32),
                vmem((size, size), F32),
                vmem((size, size), F32),
                vmem((2 * size, size), BF16),
                vmem((size, 2 * size), BF16),
                vmem((modes, 2, size, size), BF16),
                vmem((modes, 2, h, size), BF16),
                vmem((modes, 2, h, size), BF16),
                vmem((modes, 2, q, size), BF16),
                vmem((modes, 2, q, size), BF16),
                vmem((modes, 2, planes - 1, e, size), BF16),
                vmem((2, size, size), F32),
                vmem((size, size), F32),
                vmem((size, size), BF16),
                vmem((devices * deep, size), BF16),
                vmem((devices * deep, size), BF16),
                dma((3,)),
                dma((modes,)),
                dma((devices - 1,)),
                dma((devices - 1,)),
                dma((5, 2, planes)),
                dma((5, 2, planes)),
                dma((size // TILE,)),
                dma((size // TILE,)),
                dma((4, modes, 2)),
                dma((4, modes, 2)),
                dma((modes, 2, planes - 1)),
                dma((modes, 2, planes - 1)),
                dma((modes, 2, planes - 1)),
                dma((modes, 2, planes - 1)),
                dma((size // TILE,)),
                dma((size // TILE,)),
                dma((devices - 1,)),
                dma((devices - 1,)),
                dma,
                dma,
            ],
            compiler_params=pltpu.CompilerParams(
                vmem_limit_bytes=60 * 1024 * 1024, collective_id=0, has_side_effects=True
            ),
        )(strip_of, pos_row, pos_col, object_field, probe, amplitude[0], forward, inverse)
        return (strip_grad, term.astype(F32))

    lane = lax.broadcasted_iota(jnp.int32, (2, META, cols), 2)
    numbers = jnp.where(lane == 0, strip_of[0], jnp.where(lane == 1, pos_col[0] // LANES, pos_col[0] % LANES))
    packed = jnp.concatenate([object_field.astype(BF16), numbers.astype(BF16)], axis=1)
    me = lax.axis_index("mode")
    if groups == 2 and devices % PLANE == 0:
        dma, lines = pltpu.SemaphoreType.DMA, devices // PLANE
        held = pl.pallas_call(
            gather_kernel,
            out_shape=jax.ShapeDtypeStruct((2, devices, rows + META, cols), BF16),
            in_specs=[VMEM],
            out_specs=VMEM,
            scratch_shapes=[
                dma((max(lines - 1, 1),)),
                dma((max(lines - 1, 1),)),
                dma((lines, PLANE - 1)),
                dma((lines, PLANE - 1)),
                dma,
                dma,
            ],
            compiler_params=pltpu.CompilerParams(
                vmem_limit_bytes=56 * 1024 * 1024, collective_id=0, has_side_effects=True
            ),
        )(lax.dynamic_index_in_dim(packed, me, 0, keepdims=False))
    else:
        held = lax.all_gather(packed, "scan", axis=1)
    numbers = held[0, :, rows, :3].astype(jnp.int32)
    strips = numbers[:, 0]
    all_cols = numbers[:, 1] * LANES + numbers[:, 2]

    wave_shape = jax.ShapeDtypeStruct((2, size, size), F32)
    patch = pl.pallas_call(
        cut_kernel,
        out_shape=wave_shape,
        in_specs=[SMEM, SMEM, SMEM, VMEM],
        out_specs=VMEM,
        scratch_shapes=[pltpu.VMEM((2, devices * rows + 8, padded_cols), F32)],
        compiler_params=PARAMS,
    )(strips, pos_row, pos_col, held)

    def whole(*shape):
        return pl.BlockSpec(shape, lambda m: (0,) * len(shape))

    mode_spec = pl.BlockSpec((1, 2, size, size), lambda m: (m, 0, 0, 0))
    table_spec = whole(2 * size, 2 * size)
    buffers = [pltpu.VMEM((2 * size, size), BF16), pltpu.VMEM((size, 2 * size), BF16)]
    far, power = pl.pallas_call(
        forward_kernel,
        grid=(modes,),
        out_shape=(
            jax.ShapeDtypeStruct((modes, 2, size, size), F32),
            jax.ShapeDtypeStruct((size, size), F32),
        ),
        in_specs=[mode_spec, whole(2, size, size), table_spec, table_spec],
        out_specs=(mode_spec, whole(size, size)),
        scratch_shapes=buffers,
        compiler_params=PARAMS,
    )(probe, patch, forward, inverse)
    power = power + swap(power) if groups == 2 else lax.psum(power, "mode")
    term, grad = pl.pallas_call(
        backward_kernel,
        grid=(modes,),
        out_shape=(jax.ShapeDtypeStruct((modes, 2, size, size), BF16), wave_shape),
        in_specs=[
            mode_spec,
            mode_spec,
            whole(2, size, size),
            whole(size, size),
            whole(size, size),
            table_spec,
            table_spec,
        ],
        out_specs=(mode_spec, whole(2, size, size)),
        scratch_shapes=[pltpu.VMEM((size, size), F32)] + buffers,
        compiler_params=PARAMS,
    )(far, probe, patch, amplitude[0], power, inverse, forward)
    probe_grad = lax.psum(term, "scan").astype(F32)

    if groups == 2:
        mine = lax.dynamic_index_in_dim(grad, me, 0, keepdims=True)
        other = lax.dynamic_index_in_dim(grad, 1 - me, 0, keepdims=True)
        grad = mine + swap(other)
    else:
        grad = lax.psum(grad, "mode")
    parts = grad.shape[0]
    pieces = pl.pallas_call(
        place_kernel,
        out_shape=jax.ShapeDtypeStruct((devices, parts, rows, size), F32),
        in_specs=[SMEM, SMEM, VMEM],
        out_specs=VMEM,
        scratch_shapes=[pltpu.VMEM((parts, size + 2 * rows + 8, size), F32)],
        compiler_params=PARAMS,
    )(strips, pos_row, grad)
    received = lax.all_to_all(pieces.astype(BF16), "scan", 0, 0, tiled=False).astype(F32)
    strip_grad = pl.pallas_call(
        add_kernel,
        out_shape=jax.ShapeDtypeStruct((parts, rows, cols), F32),
        in_specs=[SMEM, VMEM],
        out_specs=VMEM,
        scratch_shapes=[pltpu.VMEM((parts, rows, padded_cols), F32)],
        compiler_params=PARAMS,
    )(all_cols, received)
    if groups == 2:
        theirs = swap(strip_grad)
        strip_grad = jnp.where(
            me == 0,
            jnp.concatenate([strip_grad, theirs]),
            jnp.concatenate([theirs, strip_grad]),
        )
    return (strip_grad, probe_grad)


def solution(mesh):
    return jax.shard_map(
        shards,
        mesh=mesh,
        in_specs=(
            P(None, "scan", None),
            P("mode", None, None, None),
            P("scan", None, None),
            P("scan"),
            P("scan"),
            P("scan"),
        ),
        out_specs=(P(None, "scan", None), P("mode", None, None, None)),
        check_vma=False,
    )
```

```python
import math

import jax
import jax.numpy as jnp
import numpy as np
from jax import lax
from jax.experimental import pallas as pl
from jax.experimental.pallas import tpu as pltpu
from jax.sharding import PartitionSpec as P

F32 = jnp.float32
BF16 = jnp.bfloat16
LANES = 128
HALVES = 2
META = 8
PLANE = 4
TILE = 256
ORDER = (
    (0, 0), (0, 1), (0, 2), (1, 0), (1, 1), (0, 3), (0, 4), (2, 0), (2, 1), (1, 2),
    (1, 3), (0, 5), (3, 0), (1, 4), (2, 2), (3, 1), (0, 6), (4, 0), (3, 2), (4, 1),
    (2, 4), (1, 6), (4, 2), (1, 5), (2, 3), (0, 7), (5, 2), (3, 4), (3, 3), (1, 7),
    (2, 6), (4, 4), (4, 3), (5, 1), (2, 5), (7, 0), (5, 4), (5, 3), (2, 7), (3, 6),
    (3, 7), (3, 5), (5, 0), (4, 6), (8, 0), (5, 6), (4, 5), (4, 7), (8, 1), (8, 2),
    (5, 5), (5, 7), (9, 0),
)
PARAMS = pltpu.CompilerParams(vmem_limit_bytes=56 * 1024 * 1024)
VMEM = pl.BlockSpec(memory_space=pltpu.VMEM)
SMEM = pl.BlockSpec(memory_space=pltpu.SMEM)
MESH = pl.DeviceIdType.MESH


def dft_tables(size):
    positions = np.arange(size, dtype=np.int32)
    angles = (positions[:, None] * positions[None, :] % size).astype(np.float32)
    angles = angles * np.float32(2.0 * math.pi / size)
    norm = np.float32(1.0 / math.sqrt(size))
    cosine, sine = np.cos(angles) * norm, np.sin(angles) * norm
    forward = np.block([[cosine, sine], [-sine, cosine]])
    inverse = np.block([[cosine, -sine], [sine, cosine]])
    return jnp.asarray(forward, BF16), jnp.asarray(inverse, BF16)


def gather_kernel(mine, out, line_send, line_recv, plane_send, plane_recv, swap_send, swap_recv):
    count = out.shape[1]
    lines = count // PLANE
    scan, mode = lax.axis_index("scan"), lax.axis_index("mode")
    line, place = scan // PLANE, lax.rem(scan, PLANE)
    in_line = [(lax.rem(line + k, lines) * PLANE + place, mode) for k in range(1, lines)]
    in_plane = [(line * PLANE + lax.rem(place + t, PLANE), mode) for t in range(1, PLANE)]
    partner = (scan, 1 - mode)

    barrier = pltpu.get_barrier_semaphore()
    for peer in in_line + in_plane + [partner]:
        pl.semaphore_signal(barrier, inc=1, device_id=peer, device_id_type=pl.DeviceIdType.MESH)
    pl.semaphore_wait(barrier, len(in_line) + len(in_plane) + 1)

    def push(src, dst, send, recv, peer):
        copy = pltpu.make_async_remote_copy(
            src_ref=src,
            dst_ref=dst,
            send_sem=send,
            recv_sem=recv,
            device_id=peer,
            device_id_type=pl.DeviceIdType.MESH,
        )
        copy.start()
        return copy

    own = out.at[mode, scan]
    line_copies = [
        push(mine, own, line_send.at[k], line_recv.at[k], peer) for k, peer in enumerate(in_line)
    ]
    plane_copies = [
        push(mine, own, plane_send.at[0, t], plane_recv.at[0, t], peer) for t, peer in enumerate(in_plane)
    ]
    out[mode, scan] = mine[...]
    for k, arriving in enumerate(line_copies):
        arriving.wait_recv()
        piece = out.at[mode, lax.rem(line + lines - k - 1, lines) * PLANE + place]
        plane_copies += [
            push(piece, piece, plane_send.at[k + 1, t], plane_recv.at[k + 1, t], peer)
            for t, peer in enumerate(in_plane)
        ]
    for copy in plane_copies:
        copy.wait_recv()
    last = push(out.at[mode], out.at[mode], swap_send, swap_recv, partner)
    for copy in line_copies + plane_copies:
        copy.wait_send()
    last.wait()


def cut_kernel(strips, row, col, held, patch, window):
    count, rows = held.shape[1], held.shape[2] - META
    size, cols = patch.shape[-1], held.shape[-1]
    wide = size + LANES

    def place(j, carry):
        at = pl.ds(pl.multiple_of(strips[j] * rows, 8), rows)
        for c in range(2):
            window[c, at, :cols] = held[c, j].astype(F32)[:rows]
        return carry

    lax.fori_loop(0, count, place, 0)
    across = pl.ds(pl.multiple_of(col[0] // LANES * LANES, LANES), wide)
    back = lax.rem(wide - lax.rem(col[0], LANES), wide)
    up = lax.rem(72 - lax.rem(row[0], 8), 72)
    for c in range(2):

        def cut(i, carry, c=c):
            block = window[c, pl.ds(pl.multiple_of(row[0] // 8 * 8 + i * 64, 8), 72), across]
            block = pltpu.roll(block, up, 0)[:64]
            patch[c, pl.ds(pl.multiple_of(i * 64, 64), 64), :] = pltpu.roll(block, back, 1)[:, :size]
            return carry

        lax.fori_loop(0, size // 64, cut, 0)


def forward_kernel(probe, patch, left, right, far, power, wave, half):
    size = patch.shape[-1]

    def leave(i, carry):
        at = pl.ds(pl.multiple_of(i * 64, 64), 64)
        low = pl.ds(pl.multiple_of(size + i * 64, 64), 64)
        pr, pi, xr, xi = probe[0, 0, at], probe[0, 1, at], patch[0, at], patch[1, at]
        wave[at] = (pr * xr - pi * xi).astype(BF16)
        wave[low] = (pr * xi + pi * xr).astype(BF16)
        return carry

    lax.fori_loop(0, size // 64, leave, 0)
    rows_product(left, wave, half)
    first = pl.program_id(0) == 0

    def across(i, carry):
        at = pl.ds(pl.multiple_of(i * TILE, TILE), TILE)
        both = jnp.dot(half[at], right[...], preferred_element_type=F32)
        re, im = both[:, :size], both[:, size:]
        far[0, 0, at] = re
        far[0, 1, at] = im
        here = re * re + im * im
        power[at] = jnp.where(first, here, power[at] + here)
        return carry

    lax.fori_loop(0, size // TILE, across, 0)


def rows_product(left, wave, half):
    size = wave.shape[-1]
    for c in range(2):

        def down(i, carry, c=c):
            at = pl.ds(pl.multiple_of(c * size + i * TILE, TILE), TILE)
            to = pl.ds(pl.multiple_of(i * TILE, TILE), TILE)
            product = jnp.dot(left[at], wave[...], preferred_element_type=F32)
            half[to, c * size : (c + 1) * size] = product.astype(BF16)
            return carry

        lax.fori_loop(0, size // TILE, down, 0)


def backward_kernel(far, probe, patch, measured, power, left, right, term, grad, scale, wave, half):
    size = patch.shape[-1]
    first = pl.program_id(0) == 0

    @pl.when(first)
    def _():
        total = jnp.maximum(power[...], 0.25)
        scale[...] = 1.0 - measured[...] / jnp.sqrt(total)

    def residual(i, carry):
        at = pl.ds(pl.multiple_of(i * 64, 64), 64)
        low = pl.ds(pl.multiple_of(size + i * 64, 64), 64)
        wave[at] = (far[0, 0, at] * scale[at]).astype(BF16)
        wave[low] = (far[0, 1, at] * scale[at]).astype(BF16)
        return carry

    lax.fori_loop(0, size // 64, residual, 0)
    rows_product(left, wave, half)

    def across(i, carry):
        at = pl.ds(pl.multiple_of(i * TILE, TILE), TILE)
        both = jnp.dot(half[at], right[...], preferred_element_type=F32)
        br, bi = both[:, :size], both[:, size:]
        pr, pi, xr, xi = probe[0, 0, at], probe[0, 1, at], patch[0, at], patch[1, at]
        term[0, 0, at] = (xr * br + xi * bi).astype(BF16)
        term[0, 1, at] = (xr * bi - xi * br).astype(BF16)
        re, im = pr * br + pi * bi, pr * bi - pi * br
        grad[0, at] = jnp.where(first, re, grad[0, at] + re)
        grad[1, at] = jnp.where(first, im, grad[1, at] + im)
        return carry

    lax.fori_loop(0, size // TILE, across, 0)


def mesh_peer(scan, mode, planes, dx, dy, dz):
    z, y, x = scan // 4, lax.rem(scan // 2, 2), lax.rem(scan, 2)
    x, y = lax.rem(x + dx, 2), lax.rem(y + dy, 2)
    return (lax.rem(z + dz, planes) * 4 + y * 2 + x, mode)


def core_kernel(
    strip_of, row, col, field, probe_hbm, measured_hbm, left_hbm, right_hbm, result, strip_grad,
    metas, held_a, held_b, col_hot, row_hot, cut, probe, patch, measured, left, right,
    far, power, power_in, scale, wave, half, term, got1, sum1, got2, sum2, got3,
    grad, grad_in, summed, pieces, landed,
    load, load_probe, meta_send, meta_recv, hop_send, hop_recv, swap_send, swap_recv, send, recv,
    send_z, recv_z, ship_z, land_z, part_send, part_recv, piece_send, piece_recv, strip_send, strip_recv,
):
    modes, size = probe.shape[0], patch.shape[-1]
    devices = lax.axis_size("scan")
    strip, width = strip_grad.shape[1], strip_grad.shape[2]
    planes = got3.shape[2] + 1
    scan, mode = lax.axis_index("scan"), lax.axis_index("mode")
    z, y, x = scan // 4, lax.rem(scan // 2, 2), lax.rem(scan, 2)
    partner = (scan, 1 - mode)
    peer_x = mesh_peer(scan, mode, planes, 1, 0, 0)
    peer_y = mesh_peer(scan, mode, planes, 0, 1, 0)
    peers_z = [mesh_peer(scan, mode, planes, 0, 0, k) for k in range(1, planes)]
    first_peer, second_peer = (peer_x, peer_y), (peer_y, peer_x)
    first_at, second_at = (x, y), (y, x)
    chunk = size // HALVES
    h, q, e = chunk // 2, chunk // 4, chunk // 4 // planes
    deep = pieces.shape[0] // devices

    barrier = pltpu.get_barrier_semaphore()
    everyone = [partner] + [(lax.rem(scan + k, devices), mode) for k in range(1, devices)]
    for peer in everyone:
        pl.semaphore_signal(barrier, inc=1, device_id=peer, device_id_type=MESH)

    def probe_load(m):
        return pltpu.make_async_copy(probe_hbm.at[m], probe.at[m], load_probe.at[m])

    whole = [(left_hbm, left), (right_hbm, right), (measured_hbm, measured)]
    loads = [pltpu.make_async_copy(src, dst, load.at[i]) for i, (src, dst) in enumerate(whole)]
    probe_load(0).start()
    for copy in loads:
        copy.start()
    for m in range(1, modes):
        probe_load(m).start()

    def rows(start, count, step):
        return pl.ds(pl.multiple_of(start, step), count)

    def one_hot(mask):
        return jnp.where(mask, 1.0, 0.0).astype(BF16)

    held, parts_at = (held_a, held_b), (0, held_a.shape[1], width)
    plane, plane_x, plane_y = y * 2 + x, y * 2 + 1 - x, (1 - y) * 2 + x
    plane_d = (1 - y) * 2 + 1 - x

    levels = (z, z + 1 - 2 * lax.rem(z, 2), z + 2 - 4 * (z // 2), 3 - z)

    def strip_rows(side, k):
        return rows((side * planes + levels[k]) * deep, deep, deep)

    own = jnp.concatenate([field[mode].astype(BF16), jnp.zeros((deep - strip, width), BF16)])
    for i in range(2):
        held[i][strip_rows(plane, 0)] = own[:, parts_at[i] : parts_at[i + 1]]
    which = lax.broadcasted_iota(jnp.int32, (8, LANES), 0)
    numbers = jnp.where(which == 1, lax.rem(col[0], LANES), col[0] // LANES)
    metas[scan] = jnp.where(which == 0, strip_of[0], numbers)
    pl.semaphore_wait(barrier, len(everyone))

    def remote(src, dst, send_sem, recv_sem, peer):
        return pltpu.make_async_remote_copy(
            src_ref=src, dst_ref=dst, send_sem=send_sem, recv_sem=recv_sem, device_id=peer, device_id_type=MESH
        )

    def meta(k, back=0):
        at = lax.rem(scan + devices - back, devices)
        to = (lax.rem(scan + k, devices), mode)
        return remote(metas.at[at], metas.at[at], meta_send.at[k - 1], meta_recv.at[k - 1], to)

    def hop(kind, i, k, side, peer):
        at = held[i].at[strip_rows(side, k)]
        return remote(at, at, hop_send.at[kind, i, k], hop_recv.at[kind, i, k], peer)

    def hop_z(i, k):
        at = held[i].at[strip_rows(plane, 0)]
        return remote(at, at, hop_send.at[0, i, k], hop_recv.at[0, i, k], (levels[k] * 4 + plane, mode))

    def spread(k):
        for i in range(2):
            hop(1, i, k, plane, peer_x).start()
            hop(2, 1 - i, k, plane, peer_y).start()

    def relay(k):
        hop(1, 0, k, plane_x, peer_x).wait_recv()
        hop(3, 0, k, plane_x, peer_y).start()
        hop(2, 1, k, plane_y, peer_y).wait_recv()
        hop(3, 1, k, plane_y, peer_x).start()

    def cut_columns(side):
        at = rows(side * planes * deep, planes * deep, planes * deep)
        got = jnp.dot(held_a[at], col_hot[: held_a.shape[1]], preferred_element_type=F32)
        got = got + jnp.dot(held_b[at], col_hot[held_a.shape[1] :], preferred_element_type=F32)
        cut[at] = got.astype(BF16)

    def patch_swap(i):
        at = rows(i * TILE, TILE, TILE)
        own = patch.at[mode, at]
        return remote(own, own, hop_send.at[4, i, 0], hop_recv.at[4, i, 0], partner)

    def across_lanes(row_values, count):
        return jnp.concatenate([row_values] * (count // LANES), axis=1)

    for k in range(1, devices):
        meta(k).start()
    for k in range(1, planes):
        hop_z(0, k).start()
        hop_z(1, k).start()
    spread(0)

    def column_hot(i, carry):
        at = rows(i * LANES, LANES, LANES)
        lane = lax.broadcasted_iota(jnp.int32, (LANES, size), 1)
        col_hot[at] = one_hot(lax.broadcasted_iota(jnp.int32, (LANES, size), 0) + i * LANES - lane == col[0])
        return carry

    lax.fori_loop(0, width // LANES, column_hot, 0)
    for k in range(1, planes):
        hop(0, 0, k, plane, partner).wait_recv()
        hop(0, 1, k, plane, partner).wait_recv()
        spread(k)
        relay(k - 1)
    cut_columns(plane)
    relay(planes - 1)
    for k in range(1, devices):
        meta(k, k).wait_recv()
    lane = lax.broadcasted_iota(jnp.int32, (8, devices * deep), 1)
    target = jnp.full((8, devices * deep), -1, jnp.int32)
    for j in range(devices):
        ahead = lane - (j % 4 * planes + j // 4) * deep
        target = jnp.where(
            (ahead >= 0) & (ahead < strip), across_lanes(metas[j, :1], devices * deep) * strip + ahead, target
        )
    target = target[:1] - row[0]

    def line_hot(i, carry):
        at = rows(i * 64, 64, 64)
        line = lax.broadcasted_iota(jnp.int32, (64, devices * deep), 0) + i * 64
        row_hot[at] = one_hot(line == target)
        return carry

    lax.fori_loop(0, size // 64, line_hot, 0)
    for k in range(planes):
        hop(1, 1, k, plane_x, peer_x).wait_recv()
    cut_columns(plane_x)
    for k in range(planes):
        hop(2, 0, k, plane_y, peer_y).wait_recv()
    cut_columns(plane_y)
    for k in range(planes):
        hop(3, 0, k, plane_d, peer_y).wait_recv()
        hop(3, 1, k, plane_d, peer_x).wait_recv()
    cut_columns(plane_d)
    for i in range(size // TILE):
        at = pl.ds(i * TILE, TILE)
        patch[mode, at] = jnp.dot(row_hot[at], cut[...], preferred_element_type=F32).astype(BF16)
        patch_swap(i).start()
    for copy in loads:
        copy.wait()
    for i in range(size // TILE):
        patch_swap(i).wait_recv()

    def place(u):
        return u // HALVES, u % HALVES * chunk

    def copy1(u, c):
        m, low = place(u)
        away = rows(low + (1 - first_at[c]) * h, h, h)
        return remote(term.at[m, c, away], got1.at[u, c], send.at[0, u, c], recv.at[0, u, c], first_peer[c])

    def copy2(u, c):
        away = rows((1 - second_at[c]) * q, q, q)
        return remote(sum1.at[u, c, away], got2.at[u, c], send.at[1, u, c], recv.at[1, u, c], second_peer[c])

    def copy3(u, c, k):
        away = rows(lax.rem(z + k, planes) * e, e, e)
        return remote(
            sum2.at[u, c, away], got3.at[u, c, k - 1], send_z.at[u, c, k - 1], recv_z.at[u, c, k - 1], peers_z[k - 1]
        )

    def base(u, c):
        return place(u)[1] + first_at[c] * h + second_at[c] * q

    def copy4(u, c, k):
        own = result.at[place(u)[0], c, rows(base(u, c) + z * e, e, e)]
        return remote(own, own, ship_z.at[u, c, k - 1], land_z.at[u, c, k - 1], peers_z[k - 1])

    def copy5(u, c):
        own = result.at[place(u)[0], c, rows(base(u, c), q, q)]
        return remote(own, own, send.at[2, u, c], recv.at[2, u, c], second_peer[c])

    def copy6(u, c):
        m, low = place(u)
        own = result.at[m, c, rows(low + first_at[c] * h, h, h)]
        return remote(own, own, send.at[3, u, c], recv.at[3, u, c], first_peer[c])

    def start(stage, u):
        for c in range(2):
            if stage in (3, 4):
                for k in range(1, planes):
                    (copy3, copy4)[stage - 3](u, c, k).start()
            else:
                {1: copy1, 2: copy2, 5: copy5, 6: copy6}[stage](u, c).start()

    def finish(stage, u):
        m, low = place(u)
        for c in range(2):
            if stage == 1:
                copy1(u, c).wait_recv()
                mine = term[m, c, rows(low + first_at[c] * h, h, h)].astype(F32)
                sum1[u, c] = (mine + got1[u, c].astype(F32)).astype(BF16)
            if stage == 2:
                copy2(u, c).wait_recv()
                mine = sum1[u, c, rows(second_at[c] * q, q, q)].astype(F32)
                sum2[u, c] = (mine + got2[u, c].astype(F32)).astype(BF16)
            if stage == 3:
                total = sum2[u, c, rows(z * e, e, e)].astype(F32)
                for k in range(1, planes):
                    copy3(u, c, k).wait_recv()
                    total = total + got3[u, c, k - 1].astype(F32)
                result[m, c, rows(base(u, c) + z * e, e, e)] = total.astype(BF16)
            if stage == 4:
                for k in range(1, planes):
                    copy4(u, c, k).wait_recv()
            if stage == 5:
                copy5(u, c).wait_recv()
            if stage == 6:
                copy6(u, c).wait_recv()

    def swap(i):
        at = rows(i * TILE, TILE, TILE)
        return remote(power.at[at], power_in.at[at], swap_send.at[i], swap_recv.at[i], partner)

    def product(table, source):
        out = jnp.dot(table[...], source[...], preferred_element_type=F32)
        half[:, :size] = out[:size].astype(BF16)
        half[:, size:] = out[size:].astype(BF16)

    def part(i):
        at = rows(i * TILE, TILE, TILE)
        return remote(grad.at[1 - mode, at], grad_in.at[at], part_send.at[i], part_recv.at[i], partner)

    mine = rows(scan * deep, deep, deep)

    def piece(k):
        to = lax.rem(scan + k, devices)
        return remote(pieces.at[rows(to * deep, deep, deep)], landed.at[mine], piece_send.at[k - 1], piece_recv.at[k - 1], (to, mode))

    def arrive(k):
        come = lax.rem(scan + devices - k, devices)
        at = rows(come * deep, deep, deep)
        return remote(pieces.at[at], landed.at[at], piece_send.at[k - 1], piece_recv.at[k - 1], (come, mode))

    def strip_swap():
        return remote(strip_grad.at[mode], strip_grad.at[mode], strip_send, strip_recv, partner)

    def cut_pieces():
        for i in range(size // TILE):
            part(i).wait_recv()
            at = pl.ds(i * TILE, TILE)
            summed[at] = (grad[mode, at] + grad_in[at]).astype(BF16)
        ahead = lax.broadcasted_iota(jnp.int32, (deep, size), 1) - lax.broadcasted_iota(jnp.int32, (deep, size), 0)

        def pick(j, carry):
            begin = across_lanes(metas[j, :1], size) * strip - row[0]
            wave[rows(j * deep, deep, deep)] = one_hot(ahead == begin)
            return carry

        lax.fori_loop(0, devices, pick, 0)

        def move(i, carry):
            at = rows(i * TILE, TILE, TILE)
            pieces[at] = jnp.dot(wave[at], summed[...], preferred_element_type=F32).astype(BF16)
            return carry

        lax.fori_loop(0, devices * deep // TILE, move, 0)
        landed[mine] = pieces[mine]

    def add_pieces():
        for k in range(1, devices):
            arrive(k).wait_recv()
        strip_grad[mode] = jnp.zeros((strip, width), F32)
        parts = size // LANES
        ahead = lax.broadcasted_iota(jnp.int32, (LANES, 2 * LANES), 1)
        ahead = ahead - lax.broadcasted_iota(jnp.int32, (LANES, 2 * LANES), 0)

        def one(j, carry):
            turn = one_hot(ahead == across_lanes(metas[j, 1:2], 2 * LANES))
            blocks = jnp.concatenate(
                [landed[rows(j * deep, deep, deep), b * LANES : (b + 1) * LANES] for b in range(parts)]
            )
            moved = jnp.dot(blocks, turn, preferred_element_type=F32)
            for b in range(parts + 1):
                here = moved[b * deep : b * deep + strip, :LANES] if b < parts else 0.0
                if b > 0:
                    here = here + moved[(b - 1) * deep : (b - 1) * deep + strip, LANES:]
                for t in range((width - size) // LANES + 1):
                    if b + t < width // LANES:
                        to = slice((b + t) * LANES, (b + t + 1) * LANES)
                        strip_grad[mode, :, to] += jnp.where(metas[j, 2:3] == t, here, 0.0)
            return carry

        lax.fori_loop(0, devices, one, 0)
        strip_swap().start()

    def forward(m, carry):
        probe_load(m).wait()

        def leave(i, carry):
            at, low = rows(i * 64, 64, 64), rows(size + i * 64, 64, 64)
            pr, pi, xr, xi = probe[m, 0, at], probe[m, 1, at], patch[0, at].astype(F32), patch[1, at].astype(F32)
            wave[at] = (pr * xr - pi * xi).astype(BF16)
            wave[low] = (pr * xi + pi * xr).astype(BF16)
            return carry

        lax.fori_loop(0, size // 64, leave, 0)
        product(left, wave)

        def across(i, carry):
            at = rows(i * TILE, TILE, TILE)
            both = jnp.dot(half[at], right[...], preferred_element_type=F32)
            re, im = both[:, :size], both[:, size:]
            far[m, 0, at] = re
            far[m, 1, at] = im
            here = re * re + im * im
            power[at] = jnp.where(m == 0, here, power[at] + here)

            @pl.when(m == modes - 1)
            def _():
                swap(i).start()

            return carry

        lax.fori_loop(0, size // TILE, across, 0)
        return carry

    lax.fori_loop(0, modes, forward, 0)
    for i in range(size // TILE):
        at = pl.ds(i * TILE, TILE)
        swap(i).wait_recv()
        total = jnp.maximum(power[at] + power_in[at], 0.25)
        scale[at] = 1.0 - measured[at] / jnp.sqrt(total)

    def backward(m):
        def residual(i, carry):
            at, low = rows(i * 64, 64, 64), rows(size + i * 64, 64, 64)
            wave[at] = (far[m, 0, at] * scale[at]).astype(BF16)
            wave[low] = (far[m, 1, at] * scale[at]).astype(BF16)
            return carry

        lax.fori_loop(0, size // 64, residual, 0)
        product(right, wave)

    def across_back(m, i):
        at = pl.ds(i * TILE, TILE)
        both = jnp.dot(half[at], left[...], preferred_element_type=F32)
        br, bi = both[:, :size], both[:, size:]
        pr, pi, xr, xi = probe[m, 0, at], probe[m, 1, at], patch[0, at].astype(F32), patch[1, at].astype(F32)
        term[m, 0, at] = (xr * br + xi * bi).astype(BF16)
        term[m, 1, at] = (xr * bi - xi * br).astype(BF16)
        re, im = pr * br + pi * bi, pr * bi - pi * br
        grad[0, at] = re if m == 0 else grad[0, at] + re
        grad[1, at] = im if m == 0 else grad[1, at] + im
        if m == modes - 1:
            part(i).start()

    for step, u in ORDER:
        if step == 0:
            if u % HALVES == 0:
                backward(u // HALVES)
            across_back(u // HALVES, u % HALVES)
            start(1, u)
        elif step < 6:
            finish(step, u)
            start(step + 1, u)
        elif step == 7:
            cut_pieces()
        elif step == 8:
            for k in range(1 + u, devices, 3):
                piece(k).start()
        else:
            add_pieces()

    def drain(u):
        for c in range(2):
            for copy in (copy1, copy2, copy5, copy6):
                copy(u, c).wait_send()
            for k in range(1, planes):
                copy3(u, c, k).wait_send()
                copy4(u, c, k).wait_send()

    for u in range(modes * HALVES):
        finish(6, u)
        drain(u)
    for i in range(size // TILE):
        swap(i).wait_send()
        part(i).wait_send()
    for k in range(1, devices):
        piece(k).wait_send()
    strip_swap().wait()
    for i in range(size // TILE):
        patch_swap(i).wait_send()
    for k in range(1, devices):
        meta(k).wait_send()
    for i in range(2):
        for k in range(planes):
            if k:
                hop_z(i, k).wait_send()
            hop(1, i, k, plane, peer_x).wait_send()
            hop(2, i, k, plane, peer_y).wait_send()
            hop(3, i, k, (plane_x, plane_y)[i], (peer_y, peer_x)[i]).wait_send()


def place_kernel(strips, row, grad, out, padded):
    count, parts, rows, size = out.shape
    padded[...] = jnp.zeros_like(padded)
    padded[:, rows : rows + size, :] = grad[...]

    def one(j, carry):
        start = jnp.clip(strips[j] * rows - row[0], -rows, size) + rows
        base = pl.ds(pl.multiple_of(start // 8 * 8, 8), rows + 8)
        up = lax.rem(rows + 8 - lax.rem(start, 8), rows + 8)
        for k in range(parts):
            out[j, k] = pltpu.roll(padded[k, base, :], up, 0)[:rows]
        return carry

    lax.fori_loop(0, count, one, 0)


def add_kernel(cols, received, out, total):
    count, parts, rows, size = received.shape
    total[...] = jnp.zeros_like(total)
    edge = jnp.zeros((rows, LANES), F32)

    def one(j, carry):
        across = pl.ds(pl.multiple_of(cols[j] // LANES * LANES, LANES), size + LANES)
        shift = lax.rem(cols[j], LANES)
        for k in range(parts):
            piece = jnp.concatenate([received[j, k], edge], axis=1)
            total[k, :, across] += pltpu.roll(piece, shift, 1)
        return carry

    lax.fori_loop(0, count, one, 0)
    out[...] = total[:, :, : out.shape[-1]]


def shards(object_field, probe, amplitude, pos_row, pos_col, strip_of):
    size = probe.shape[-1]
    modes = probe.shape[0]
    rows, cols = object_field.shape[1], object_field.shape[2]
    devices, groups = lax.axis_size("scan"), lax.axis_size("mode")
    padded_cols = cols + LANES
    forward, inverse = dft_tables(size)

    def swap(x):
        return lax.ppermute(x, "mode", [(0, 1), (1, 0)])

    planes, deep = devices // 4, -(-rows // 16) * 16
    fits = groups == 2 and devices == 4 * planes and planes == 4 and size % (64 * HALVES * planes) == 0 and modes * HALVES == 8
    fits = fits and cols % LANES == 0 and size // TILE == 2
    if fits and rows % 8 == 0 and devices * deep % TILE == 0 and devices * deep <= 2 * size:
        dma = pltpu.SemaphoreType.DMA
        chunks, chunk = modes * HALVES, size // HALVES
        h, q, e = chunk // 2, chunk // 4, chunk // 4 // planes
        vmem, lanes = pltpu.VMEM, (cols // LANES + 1) // 2 * LANES
        any_space = pl.BlockSpec(memory_space=pl.ANY)
        term, strip_grad = pl.pallas_call(
            core_kernel,
            out_shape=(vmem((modes, 2, size, size), BF16), vmem((2, rows, cols), F32)),
            in_specs=[SMEM] * 3 + [VMEM] + [any_space] * 4,
            out_specs=(VMEM, VMEM),
            scratch_shapes=[
                vmem((devices, 8, LANES), jnp.int32),
                vmem((devices * deep, lanes), BF16),
                vmem((devices * deep, cols - lanes), BF16),
                vmem((cols, size), BF16),
                vmem((size, devices * deep), BF16),
                vmem((devices * deep, size), BF16),
                vmem((modes, 2, size, size), F32),
                vmem((2, size, size), BF16),
                vmem((size, size), F32),
                vmem((2 * size, 2 * size), BF16),
                vmem((2 * size, 2 * size), BF16),
                vmem((modes, 2, size, size), F32),
                vmem((size, size), F32),
                vmem((size, size), F32),
                vmem((size, size), F32),
                vmem((2 * size, size), BF16),
                vmem((size, 2 * size), BF16),
                vmem((modes, 2, size, size), BF16),
                vmem((chunks, 2, h, size), BF16),
                vmem((chunks, 2, h, size), BF16),
                vmem((chunks, 2, q, size), BF16),
                vmem((chunks, 2, q, size), BF16),
                vmem((chunks, 2, planes - 1, e, size), BF16),
                vmem((2, size, size), F32),
                vmem((size, size), F32),
                vmem((size, size), BF16),
                vmem((devices * deep, size), BF16),
                vmem((devices * deep, size), BF16),
                dma((3,)),
                dma((modes,)),
                dma((devices - 1,)),
                dma((devices - 1,)),
                dma((5, 2, planes)),
                dma((5, 2, planes)),
                dma((size // TILE,)),
                dma((size // TILE,)),
                dma((4, chunks, 2)),
                dma((4, chunks, 2)),
                dma((chunks, 2, planes - 1)),
                dma((chunks, 2, planes - 1)),
                dma((chunks, 2, planes - 1)),
                dma((chunks, 2, planes - 1)),
                dma((size // TILE,)),
                dma((size // TILE,)),
                dma((devices - 1,)),
                dma((devices - 1,)),
                dma,
                dma,
            ],
            compiler_params=pltpu.CompilerParams(
                vmem_limit_bytes=56 * 1024 * 1024, collective_id=0, has_side_effects=True
            ),
        )(strip_of, pos_row, pos_col, object_field, probe, amplitude[0], forward, inverse)
        return (strip_grad, term.astype(F32))

    lane = lax.broadcasted_iota(jnp.int32, (2, META, cols), 2)
    numbers = jnp.where(lane == 0, strip_of[0], jnp.where(lane == 1, pos_col[0] // LANES, pos_col[0] % LANES))
    packed = jnp.concatenate([object_field.astype(BF16), numbers.astype(BF16)], axis=1)
    me = lax.axis_index("mode")
    if groups == 2 and devices % PLANE == 0:
        dma, lines = pltpu.SemaphoreType.DMA, devices // PLANE
        held = pl.pallas_call(
            gather_kernel,
            out_shape=jax.ShapeDtypeStruct((2, devices, rows + META, cols), BF16),
            in_specs=[VMEM],
            out_specs=VMEM,
            scratch_shapes=[
                dma((max(lines - 1, 1),)),
                dma((max(lines - 1, 1),)),
                dma((lines, PLANE - 1)),
                dma((lines, PLANE - 1)),
                dma,
                dma,
            ],
            compiler_params=pltpu.CompilerParams(
                vmem_limit_bytes=56 * 1024 * 1024, collective_id=0, has_side_effects=True
            ),
        )(lax.dynamic_index_in_dim(packed, me, 0, keepdims=False))
    else:
        held = lax.all_gather(packed, "scan", axis=1)
    numbers = held[0, :, rows, :3].astype(jnp.int32)
    strips = numbers[:, 0]
    all_cols = numbers[:, 1] * LANES + numbers[:, 2]

    wave_shape = jax.ShapeDtypeStruct((2, size, size), F32)
    patch = pl.pallas_call(
        cut_kernel,
        out_shape=wave_shape,
        in_specs=[SMEM, SMEM, SMEM, VMEM],
        out_specs=VMEM,
        scratch_shapes=[pltpu.VMEM((2, devices * rows + 8, padded_cols), F32)],
        compiler_params=PARAMS,
    )(strips, pos_row, pos_col, held)

    def whole(*shape):
        return pl.BlockSpec(shape, lambda m: (0,) * len(shape))

    mode_spec = pl.BlockSpec((1, 2, size, size), lambda m: (m, 0, 0, 0))
    table_spec = whole(2 * size, 2 * size)
    buffers = [pltpu.VMEM((2 * size, size), BF16), pltpu.VMEM((size, 2 * size), BF16)]
    far, power = pl.pallas_call(
        forward_kernel,
        grid=(modes,),
        out_shape=(
            jax.ShapeDtypeStruct((modes, 2, size, size), F32),
            jax.ShapeDtypeStruct((size, size), F32),
        ),
        in_specs=[mode_spec, whole(2, size, size), table_spec, table_spec],
        out_specs=(mode_spec, whole(size, size)),
        scratch_shapes=buffers,
        compiler_params=PARAMS,
    )(probe, patch, forward, inverse)
    power = power + swap(power) if groups == 2 else lax.psum(power, "mode")
    term, grad = pl.pallas_call(
        backward_kernel,
        grid=(modes,),
        out_shape=(jax.ShapeDtypeStruct((modes, 2, size, size), BF16), wave_shape),
        in_specs=[
            mode_spec,
            mode_spec,
            whole(2, size, size),
            whole(size, size),
            whole(size, size),
            table_spec,
            table_spec,
        ],
        out_specs=(mode_spec, whole(2, size, size)),
        scratch_shapes=[pltpu.VMEM((size, size), F32)] + buffers,
        compiler_params=PARAMS,
    )(far, probe, patch, amplitude[0], power, inverse, forward)
    probe_grad = lax.psum(term, "scan").astype(F32)

    if groups == 2:
        mine = lax.dynamic_index_in_dim(grad, me, 0, keepdims=True)
        other = lax.dynamic_index_in_dim(grad, 1 - me, 0, keepdims=True)
        grad = mine + swap(other)
    else:
        grad = lax.psum(grad, "mode")
    parts = grad.shape[0]
    pieces = pl.pallas_call(
        place_kernel,
        out_shape=jax.ShapeDtypeStruct((devices, parts, rows, size), F32),
        in_specs=[SMEM, SMEM, VMEM],
        out_specs=VMEM,
        scratch_shapes=[pltpu.VMEM((parts, size + 2 * rows + 8, size), F32)],
        compiler_params=PARAMS,
    )(strips, pos_row, grad)
    received = lax.all_to_all(pieces.astype(BF16), "scan", 0, 0, tiled=False).astype(F32)
    strip_grad = pl.pallas_call(
        add_kernel,
        out_shape=jax.ShapeDtypeStruct((parts, rows, cols), F32),
        in_specs=[SMEM, VMEM],
        out_specs=VMEM,
        scratch_shapes=[pltpu.VMEM((parts, rows, padded_cols), F32)],
        compiler_params=PARAMS,
    )(all_cols, received)
    if groups == 2:
        theirs = swap(strip_grad)
        strip_grad = jnp.where(
            me == 0,
            jnp.concatenate([strip_grad, theirs]),
            jnp.concatenate([theirs, strip_grad]),
        )
    return (strip_grad, probe_grad)


def solution(mesh):
    return jax.shard_map(
        shards,
        mesh=mesh,
        in_specs=(
            P(None, "scan", None),
            P("mode", None, None, None),
            P("scan", None, None),
            P("scan"),
            P("scan"),
            P("scan"),
        ),
        out_specs=(P(None, "scan", None), P("mode", None, None, None)),
        check_vma=False,
    )
```

```python
import math

import jax
import jax.numpy as jnp
import numpy as np
from jax import lax
from jax.experimental import pallas as pl
from jax.experimental.pallas import tpu as pltpu
from jax.sharding import PartitionSpec as P

F32 = jnp.float32
BF16 = jnp.bfloat16
LANES = 128
HALVES = 2
META = 8
PLANE = 4
TILE = 256
ORDER = (
    (0, 0), (0, 1), (0, 2), (1, 0), (0, 3), (1, 1), (0, 4), (2, 0), (1, 2), (1, 3),
    (0, 5), (0, 6), (3, 0), (2, 1), (1, 4), (0, 7), (2, 3), (9, 0), (10, 0), (2, 2),
    (1, 5), (4, 0), (2, 4), (3, 1), (3, 3), (5, 0), (3, 4), (4, 1), (4, 3), (10, 1),
    (3, 2), (1, 7), (4, 4), (2, 5), (5, 3), (6, 0), (1, 6), (4, 2), (7, 0), (5, 4),
    (5, 1), (6, 3), (3, 5), (2, 7), (6, 4), (2, 6), (6, 1), (5, 2), (4, 5), (7, 3),
    (3, 7), (3, 6), (7, 4), (5, 5), (4, 7), (7, 1), (4, 6), (6, 2), (5, 7), (6, 5),
    (5, 6), (10, 2), (6, 7), (6, 6), (7, 5), (7, 6), (7, 7), (7, 2), (11, 0),
)
PLANES_FIRST = (2,)
PARAMS = pltpu.CompilerParams(vmem_limit_bytes=56 * 1024 * 1024)
VMEM = pl.BlockSpec(memory_space=pltpu.VMEM)
SMEM = pl.BlockSpec(memory_space=pltpu.SMEM)
MESH = pl.DeviceIdType.MESH


def dft_tables(size):
    positions = np.arange(size, dtype=np.int32)
    angles = (positions[:, None] * positions[None, :] % size).astype(np.float32)
    angles = angles * np.float32(2.0 * math.pi / size)
    norm = np.float32(1.0 / math.sqrt(size))
    cosine, sine = np.cos(angles) * norm, np.sin(angles) * norm
    forward = np.block([[cosine, sine], [-sine, cosine]])
    inverse = np.block([[cosine, -sine], [sine, cosine]])
    return jnp.asarray(forward, BF16), jnp.asarray(inverse, BF16)


def gather_kernel(mine, out, line_send, line_recv, plane_send, plane_recv, swap_send, swap_recv):
    count = out.shape[1]
    lines = count // PLANE
    scan, mode = lax.axis_index("scan"), lax.axis_index("mode")
    line, place = scan // PLANE, lax.rem(scan, PLANE)
    in_line = [(lax.rem(line + k, lines) * PLANE + place, mode) for k in range(1, lines)]
    in_plane = [(line * PLANE + lax.rem(place + t, PLANE), mode) for t in range(1, PLANE)]
    partner = (scan, 1 - mode)

    barrier = pltpu.get_barrier_semaphore()
    for peer in in_line + in_plane + [partner]:
        pl.semaphore_signal(barrier, inc=1, device_id=peer, device_id_type=pl.DeviceIdType.MESH)
    pl.semaphore_wait(barrier, len(in_line) + len(in_plane) + 1)

    def push(src, dst, send, recv, peer):
        copy = pltpu.make_async_remote_copy(
            src_ref=src,
            dst_ref=dst,
            send_sem=send,
            recv_sem=recv,
            device_id=peer,
            device_id_type=pl.DeviceIdType.MESH,
        )
        copy.start()
        return copy

    own = out.at[mode, scan]
    line_copies = [
        push(mine, own, line_send.at[k], line_recv.at[k], peer) for k, peer in enumerate(in_line)
    ]
    plane_copies = [
        push(mine, own, plane_send.at[0, t], plane_recv.at[0, t], peer) for t, peer in enumerate(in_plane)
    ]
    out[mode, scan] = mine[...]
    for k, arriving in enumerate(line_copies):
        arriving.wait_recv()
        piece = out.at[mode, lax.rem(line + lines - k - 1, lines) * PLANE + place]
        plane_copies += [
            push(piece, piece, plane_send.at[k + 1, t], plane_recv.at[k + 1, t], peer)
            for t, peer in enumerate(in_plane)
        ]
    for copy in plane_copies:
        copy.wait_recv()
    last = push(out.at[mode], out.at[mode], swap_send, swap_recv, partner)
    for copy in line_copies + plane_copies:
        copy.wait_send()
    last.wait()


def cut_kernel(strips, row, col, held, patch, window):
    count, rows = held.shape[1], held.shape[2] - META
    size, cols = patch.shape[-1], held.shape[-1]
    wide = size + LANES

    def place(j, carry):
        at = pl.ds(pl.multiple_of(strips[j] * rows, 8), rows)
        for c in range(2):
            window[c, at, :cols] = held[c, j].astype(F32)[:rows]
        return carry

    lax.fori_loop(0, count, place, 0)
    across = pl.ds(pl.multiple_of(col[0] // LANES * LANES, LANES), wide)
    back = lax.rem(wide - lax.rem(col[0], LANES), wide)
    up = lax.rem(72 - lax.rem(row[0], 8), 72)
    for c in range(2):

        def cut(i, carry, c=c):
            block = window[c, pl.ds(pl.multiple_of(row[0] // 8 * 8 + i * 64, 8), 72), across]
            block = pltpu.roll(block, up, 0)[:64]
            patch[c, pl.ds(pl.multiple_of(i * 64, 64), 64), :] = pltpu.roll(block, back, 1)[:, :size]
            return carry

        lax.fori_loop(0, size // 64, cut, 0)


def forward_kernel(probe, patch, left, right, far, power, wave, half):
    size = patch.shape[-1]

    def leave(i, carry):
        at = pl.ds(pl.multiple_of(i * 64, 64), 64)
        low = pl.ds(pl.multiple_of(size + i * 64, 64), 64)
        pr, pi, xr, xi = probe[0, 0, at], probe[0, 1, at], patch[0, at], patch[1, at]
        wave[at] = (pr * xr - pi * xi).astype(BF16)
        wave[low] = (pr * xi + pi * xr).astype(BF16)
        return carry

    lax.fori_loop(0, size // 64, leave, 0)
    rows_product(left, wave, half)
    first = pl.program_id(0) == 0

    def across(i, carry):
        at = pl.ds(pl.multiple_of(i * TILE, TILE), TILE)
        both = jnp.dot(half[at], right[...], preferred_element_type=F32)
        re, im = both[:, :size], both[:, size:]
        far[0, 0, at] = re
        far[0, 1, at] = im
        here = re * re + im * im
        power[at] = jnp.where(first, here, power[at] + here)
        return carry

    lax.fori_loop(0, size // TILE, across, 0)


def rows_product(left, wave, half):
    size = wave.shape[-1]
    for c in range(2):

        def down(i, carry, c=c):
            at = pl.ds(pl.multiple_of(c * size + i * TILE, TILE), TILE)
            to = pl.ds(pl.multiple_of(i * TILE, TILE), TILE)
            product = jnp.dot(left[at], wave[...], preferred_element_type=F32)
            half[to, c * size : (c + 1) * size] = product.astype(BF16)
            return carry

        lax.fori_loop(0, size // TILE, down, 0)


def backward_kernel(far, probe, patch, measured, power, left, right, term, grad, scale, wave, half):
    size = patch.shape[-1]
    first = pl.program_id(0) == 0

    @pl.when(first)
    def _():
        total = jnp.maximum(power[...], 0.25)
        scale[...] = 1.0 - measured[...] / jnp.sqrt(total)

    def residual(i, carry):
        at = pl.ds(pl.multiple_of(i * 64, 64), 64)
        low = pl.ds(pl.multiple_of(size + i * 64, 64), 64)
        wave[at] = (far[0, 0, at] * scale[at]).astype(BF16)
        wave[low] = (far[0, 1, at] * scale[at]).astype(BF16)
        return carry

    lax.fori_loop(0, size // 64, residual, 0)
    rows_product(left, wave, half)

    def across(i, carry):
        at = pl.ds(pl.multiple_of(i * TILE, TILE), TILE)
        both = jnp.dot(half[at], right[...], preferred_element_type=F32)
        br, bi = both[:, :size], both[:, size:]
        pr, pi, xr, xi = probe[0, 0, at], probe[0, 1, at], patch[0, at], patch[1, at]
        term[0, 0, at] = (xr * br + xi * bi).astype(BF16)
        term[0, 1, at] = (xr * bi - xi * br).astype(BF16)
        re, im = pr * br + pi * bi, pr * bi - pi * br
        grad[0, at] = jnp.where(first, re, grad[0, at] + re)
        grad[1, at] = jnp.where(first, im, grad[1, at] + im)
        return carry

    lax.fori_loop(0, size // TILE, across, 0)


def mesh_peer(scan, mode, planes, dx, dy, dz):
    z, y, x = scan // 4, lax.rem(scan // 2, 2), lax.rem(scan, 2)
    x, y = lax.rem(x + dx, 2), lax.rem(y + dy, 2)
    return (lax.rem(z + dz, planes) * 4 + y * 2 + x, mode)


def core_kernel(
    strip_of, row, col, field, probe_hbm, measured_hbm, left_hbm, right_hbm, result, strip_grad,
    metas, held_a, held_b, col_hot, row_hot, cut, probe, patch, measured, left, right,
    far, power, power_in, scale, wave, half, term, got1, sum1, got2, sum2, got3, sum3, got4,
    grad, grad_in, summed, pieces, landed,
    load, load_probe, meta_send, meta_recv, hop_send, hop_recv, swap_send, swap_recv, send, recv,
    part_send, part_recv, piece_send, piece_recv, strip_send, strip_recv,
):
    modes, size = probe.shape[0], patch.shape[-1]
    devices = lax.axis_size("scan")
    strip, width = strip_grad.shape[1], strip_grad.shape[2]
    planes = devices // 4
    scan, mode = lax.axis_index("scan"), lax.axis_index("mode")
    z, y, x = scan // 4, lax.rem(scan // 2, 2), lax.rem(scan, 2)
    partner = (scan, 1 - mode)
    peer_x = mesh_peer(scan, mode, planes, 1, 0, 0)
    peer_y = mesh_peer(scan, mode, planes, 0, 1, 0)
    chunk = size // HALVES
    deep = pieces.shape[0] // devices

    barrier = pltpu.get_barrier_semaphore()
    everyone = [partner] + [(lax.rem(scan + k, devices), mode) for k in range(1, devices)]
    for peer in everyone:
        pl.semaphore_signal(barrier, inc=1, device_id=peer, device_id_type=MESH)

    def probe_load(m):
        return pltpu.make_async_copy(probe_hbm.at[m], probe.at[m], load_probe.at[m])

    whole = [(left_hbm, left), (right_hbm, right), (measured_hbm, measured)]
    loads = [pltpu.make_async_copy(src, dst, load.at[i]) for i, (src, dst) in enumerate(whole)]
    probe_load(0).start()
    for copy in loads:
        copy.start()
    for m in range(1, modes):
        probe_load(m).start()

    def rows(start, count, step):
        return pl.ds(pl.multiple_of(start, step), count)

    def one_hot(mask):
        return jnp.where(mask, 1.0, 0.0).astype(BF16)

    held, parts_at = (held_a, held_b), (0, held_a.shape[1], width)
    plane, plane_x, plane_y = y * 2 + x, y * 2 + 1 - x, (1 - y) * 2 + x
    plane_d = (1 - y) * 2 + 1 - x

    levels = (z, z + 1 - 2 * lax.rem(z, 2), z + 2 - 4 * (z // 2), 3 - z)

    def strip_rows(side, k):
        return rows((side * planes + levels[k]) * deep, deep, deep)

    own = jnp.concatenate([field[mode].astype(BF16), jnp.zeros((deep - strip, width), BF16)])
    for i in range(2):
        held[i][strip_rows(plane, 0)] = own[:, parts_at[i] : parts_at[i + 1]]
    which = lax.broadcasted_iota(jnp.int32, (8, LANES), 0)
    numbers = jnp.where(which == 1, lax.rem(col[0], LANES), col[0] // LANES)
    metas[scan] = jnp.where(which == 0, strip_of[0], numbers)
    pl.semaphore_wait(barrier, len(everyone))

    def remote(src, dst, send_sem, recv_sem, peer):
        return pltpu.make_async_remote_copy(
            src_ref=src, dst_ref=dst, send_sem=send_sem, recv_sem=recv_sem, device_id=peer, device_id_type=MESH
        )

    def meta(k, back=0):
        at = lax.rem(scan + devices - back, devices)
        to = (lax.rem(scan + k, devices), mode)
        return remote(metas.at[at], metas.at[at], meta_send.at[k - 1], meta_recv.at[k - 1], to)

    def hop(kind, i, k, side, peer):
        at = held[i].at[strip_rows(side, k)]
        return remote(at, at, hop_send.at[kind, i, k], hop_recv.at[kind, i, k], peer)

    def hop_z(i, k):
        at = held[i].at[strip_rows(plane, 0)]
        return remote(at, at, hop_send.at[0, i, k], hop_recv.at[0, i, k], (levels[k] * 4 + plane, mode))

    def spread(k):
        for i in range(2):
            hop(1, i, k, plane, peer_x).start()
            hop(2, 1 - i, k, plane, peer_y).start()

    def relay(k):
        hop(1, 0, k, plane_x, peer_x).wait_recv()
        hop(3, 0, k, plane_x, peer_y).start()
        hop(2, 1, k, plane_y, peer_y).wait_recv()
        hop(3, 1, k, plane_y, peer_x).start()

    def cut_columns(side):
        at = rows(side * planes * deep, planes * deep, planes * deep)
        got = jnp.dot(held_a[at], col_hot[: held_a.shape[1]], preferred_element_type=F32)
        got = got + jnp.dot(held_b[at], col_hot[held_a.shape[1] :], preferred_element_type=F32)
        cut[at] = got.astype(BF16)

    def patch_swap(i):
        at = rows(i * TILE, TILE, TILE)
        own = patch.at[mode, at]
        return remote(own, own, hop_send.at[4, i, 0], hop_recv.at[4, i, 0], partner)

    def across_lanes(row_values, count):
        return jnp.concatenate([row_values] * (count // LANES), axis=1)

    for k in range(1, devices):
        meta(k).start()
    for k in range(1, planes):
        hop_z(0, k).start()
        hop_z(1, k).start()
    spread(0)

    def column_hot(i, carry):
        at = rows(i * LANES, LANES, LANES)
        lane = lax.broadcasted_iota(jnp.int32, (LANES, size), 1)
        col_hot[at] = one_hot(lax.broadcasted_iota(jnp.int32, (LANES, size), 0) + i * LANES - lane == col[0])
        return carry

    lax.fori_loop(0, width // LANES, column_hot, 0)
    for k in range(1, planes):
        hop(0, 0, k, plane, partner).wait_recv()
        hop(0, 1, k, plane, partner).wait_recv()
        spread(k)
        relay(k - 1)
    cut_columns(plane)
    relay(planes - 1)
    for k in range(1, devices):
        meta(k, k).wait_recv()
    lane = lax.broadcasted_iota(jnp.int32, (8, devices * deep), 1)
    target = jnp.full((8, devices * deep), -1, jnp.int32)
    for j in range(devices):
        ahead = lane - (j % 4 * planes + j // 4) * deep
        target = jnp.where(
            (ahead >= 0) & (ahead < strip), across_lanes(metas[j, :1], devices * deep) * strip + ahead, target
        )
    target = target[:1] - row[0]

    def line_hot(i, carry):
        at = rows(i * 64, 64, 64)
        line = lax.broadcasted_iota(jnp.int32, (64, devices * deep), 0) + i * 64
        row_hot[at] = one_hot(line == target)
        return carry

    lax.fori_loop(0, size // 64, line_hot, 0)
    for k in range(planes):
        hop(1, 1, k, plane_x, peer_x).wait_recv()
    cut_columns(plane_x)
    for k in range(planes):
        hop(2, 0, k, plane_y, peer_y).wait_recv()
    cut_columns(plane_y)
    for k in range(planes):
        hop(3, 0, k, plane_d, peer_y).wait_recv()
        hop(3, 1, k, plane_d, peer_x).wait_recv()
    cut_columns(plane_d)
    for i in range(size // TILE):
        at = pl.ds(i * TILE, TILE)
        patch[mode, at] = jnp.dot(row_hot[at], cut[...], preferred_element_type=F32).astype(BF16)
        patch_swap(i).start()
    for copy in loads:
        copy.wait()
    for i in range(size // TILE):
        patch_swap(i).wait_recv()

    def place(u):
        return u // HALVES, u % HALVES * chunk

    near, far_z = levels[1] * 4 + plane, levels[2] * 4 + plane
    along = {"x": (peer_x, x), "y": (peer_y, y), "n": ((near, mode), lax.rem(z, 2)), "f": ((far_z, mode), z // 2)}
    sums, gots = (None, sum1, sum2, sum3), (None, got1, got2, got3, got4)

    def way(u, c, stage):
        axes = ("nfxy", "nfyx")[c] if u in PLANES_FIRST else ("xynf", "yxnf")[c]
        return along[axes[stage - 1]]

    def base(u, c, stage):
        low = place(u)[1]
        for s in range(1, stage + 1):
            low = low + way(u, c, s)[1] * (chunk >> s)
        return low

    def exchange(u, c, stage):
        m, low = place(u)
        if stage > 4:
            stage = 9 - stage
            count = chunk >> stage
            own = result.at[m, c, rows(base(u, c, stage), count, count)]
            peer, stage = way(u, c, stage)[0], 9 - stage
            return remote(own, own, send.at[stage - 1, u, c], recv.at[stage - 1, u, c], peer)
        peer, bit = way(u, c, stage)
        count = chunk >> stage
        away = (1 - bit) * count
        src = term.at[m, c, rows(low + away, count, count)] if stage == 1 else sums[stage - 1].at[u, c, rows(away, count, count)]
        return remote(src, gots[stage].at[u, c], send.at[stage - 1, u, c], recv.at[stage - 1, u, c], peer)

    def start(stage, u):
        for c in range(2):
            exchange(u, c, stage).start()

    def finish(stage, u):
        m, low = place(u)
        for c in range(2):
            exchange(u, c, stage).wait_recv()
            if stage > 4:
                continue
            count, bit = chunk >> stage, way(u, c, stage)[1]
            if stage == 1:
                mine = term[m, c, rows(low + bit * count, count, count)]
            else:
                mine = sums[stage - 1][u, c, rows(bit * count, count, count)]
            total = (mine.astype(F32) + gots[stage][u, c].astype(F32)).astype(BF16)
            if stage == 4:
                result[m, c, rows(base(u, c, 4), count, count)] = total
            else:
                sums[stage][u, c] = total

    def swap(i):
        at = rows(i * TILE, TILE, TILE)
        return remote(power.at[at], power_in.at[at], swap_send.at[i], swap_recv.at[i], partner)

    def product(table, source):
        out = jnp.dot(table[...], source[...], preferred_element_type=F32)
        half[:, :size] = out[:size].astype(BF16)
        half[:, size:] = out[size:].astype(BF16)

    def part(i):
        at = rows(i * TILE, TILE, TILE)
        return remote(grad.at[1 - mode, at], grad_in.at[at], part_send.at[i], part_recv.at[i], partner)

    mine = rows(scan * deep, deep, deep)

    def piece(k):
        to = lax.rem(scan + k, devices)
        return remote(pieces.at[rows(to * deep, deep, deep)], landed.at[mine], piece_send.at[k - 1], piece_recv.at[k - 1], (to, mode))

    def arrive(k):
        come = lax.rem(scan + devices - k, devices)
        at = rows(come * deep, deep, deep)
        return remote(pieces.at[at], landed.at[at], piece_send.at[k - 1], piece_recv.at[k - 1], (come, mode))

    def strip_swap():
        return remote(strip_grad.at[mode], strip_grad.at[mode], strip_send, strip_recv, partner)

    def cut_pieces():
        for i in range(size // TILE):
            part(i).wait_recv()
            at = pl.ds(i * TILE, TILE)
            summed[at] = (grad[mode, at] + grad_in[at]).astype(BF16)
        ahead = lax.broadcasted_iota(jnp.int32, (deep, size), 1) - lax.broadcasted_iota(jnp.int32, (deep, size), 0)

        def pick(j, carry):
            begin = across_lanes(metas[j, :1], size) * strip - row[0]
            wave[rows(j * deep, deep, deep)] = one_hot(ahead == begin)
            return carry

        lax.fori_loop(0, devices, pick, 0)

        def move(i, carry):
            at = rows(i * TILE, TILE, TILE)
            pieces[at] = jnp.dot(wave[at], summed[...], preferred_element_type=F32).astype(BF16)
            return carry

        lax.fori_loop(0, devices * deep // TILE, move, 0)
        landed[mine] = pieces[mine]

    def add_pieces():
        for k in range(1, devices):
            arrive(k).wait_recv()
        strip_grad[mode] = jnp.zeros((strip, width), F32)
        parts = size // LANES
        ahead = lax.broadcasted_iota(jnp.int32, (LANES, 2 * LANES), 1)
        ahead = ahead - lax.broadcasted_iota(jnp.int32, (LANES, 2 * LANES), 0)

        def one(j, carry):
            turn = one_hot(ahead == across_lanes(metas[j, 1:2], 2 * LANES))
            blocks = jnp.concatenate(
                [landed[rows(j * deep, deep, deep), b * LANES : (b + 1) * LANES] for b in range(parts)]
            )
            moved = jnp.dot(blocks, turn, preferred_element_type=F32)
            for b in range(parts + 1):
                here = moved[b * deep : b * deep + strip, :LANES] if b < parts else 0.0
                if b > 0:
                    here = here + moved[(b - 1) * deep : (b - 1) * deep + strip, LANES:]
                for t in range((width - size) // LANES + 1):
                    if b + t < width // LANES:
                        to = slice((b + t) * LANES, (b + t + 1) * LANES)
                        strip_grad[mode, :, to] += jnp.where(metas[j, 2:3] == t, here, 0.0)
            return carry

        lax.fori_loop(0, devices, one, 0)
        strip_swap().start()

    def forward(m, carry):
        probe_load(m).wait()

        def leave(i, carry):
            at, low = rows(i * 64, 64, 64), rows(size + i * 64, 64, 64)
            pr, pi, xr, xi = probe[m, 0, at], probe[m, 1, at], patch[0, at].astype(F32), patch[1, at].astype(F32)
            wave[at] = (pr * xr - pi * xi).astype(BF16)
            wave[low] = (pr * xi + pi * xr).astype(BF16)
            return carry

        lax.fori_loop(0, size // 64, leave, 0)
        product(left, wave)

        def across(i, carry):
            at = rows(i * TILE, TILE, TILE)
            both = jnp.dot(half[at], right[...], preferred_element_type=F32)
            re, im = both[:, :size], both[:, size:]
            far[m, 0, at] = re
            far[m, 1, at] = im
            here = re * re + im * im
            power[at] = jnp.where(m == 0, here, power[at] + here)

            @pl.when(m == modes - 1)
            def _():
                swap(i).start()

            return carry

        lax.fori_loop(0, size // TILE, across, 0)
        return carry

    lax.fori_loop(0, modes, forward, 0)
    for i in range(size // TILE):
        at = pl.ds(i * TILE, TILE)
        swap(i).wait_recv()
        total = jnp.maximum(power[at] + power_in[at], 0.25)
        scale[at] = 1.0 - measured[at] / jnp.sqrt(total)

    def backward(m):
        def residual(i, carry):
            at, low = rows(i * 64, 64, 64), rows(size + i * 64, 64, 64)
            wave[at] = (far[m, 0, at] * scale[at]).astype(BF16)
            wave[low] = (far[m, 1, at] * scale[at]).astype(BF16)
            return carry

        lax.fori_loop(0, size // 64, residual, 0)
        product(right, wave)

    def across_back(m, i):
        at = pl.ds(i * TILE, TILE)
        both = jnp.dot(half[at], left[...], preferred_element_type=F32)
        br, bi = both[:, :size], both[:, size:]
        pr, pi, xr, xi = probe[m, 0, at], probe[m, 1, at], patch[0, at].astype(F32), patch[1, at].astype(F32)
        term[m, 0, at] = (xr * br + xi * bi).astype(BF16)
        term[m, 1, at] = (xr * bi - xi * br).astype(BF16)
        re, im = pr * br + pi * bi, pr * bi - pi * br
        grad[0, at] = re if m == 0 else grad[0, at] + re
        grad[1, at] = im if m == 0 else grad[1, at] + im
        if m == modes - 1:
            part(i).start()

    for step, u in ORDER:
        if step == 0:
            if u % HALVES == 0:
                backward(u // HALVES)
            across_back(u // HALVES, u % HALVES)
            start(1, u)
        elif step < 8:
            finish(step, u)
            start(step + 1, u)
        elif step == 9:
            cut_pieces()
        elif step == 10:
            for k in range(1 + u, devices, 3):
                piece(k).start()
        else:
            add_pieces()

    for u in range(modes * HALVES):
        finish(8, u)
        for c in range(2):
            for stage in range(1, 9):
                exchange(u, c, stage).wait_send()
    for i in range(size // TILE):
        swap(i).wait_send()
        part(i).wait_send()
    for k in range(1, devices):
        piece(k).wait_send()
    strip_swap().wait()
    for i in range(size // TILE):
        patch_swap(i).wait_send()
    for k in range(1, devices):
        meta(k).wait_send()
    for i in range(2):
        for k in range(planes):
            if k:
                hop_z(i, k).wait_send()
            hop(1, i, k, plane, peer_x).wait_send()
            hop(2, i, k, plane, peer_y).wait_send()
            hop(3, i, k, (plane_x, plane_y)[i], (peer_y, peer_x)[i]).wait_send()


def place_kernel(strips, row, grad, out, padded):
    count, parts, rows, size = out.shape
    padded[...] = jnp.zeros_like(padded)
    padded[:, rows : rows + size, :] = grad[...]

    def one(j, carry):
        start = jnp.clip(strips[j] * rows - row[0], -rows, size) + rows
        base = pl.ds(pl.multiple_of(start // 8 * 8, 8), rows + 8)
        up = lax.rem(rows + 8 - lax.rem(start, 8), rows + 8)
        for k in range(parts):
            out[j, k] = pltpu.roll(padded[k, base, :], up, 0)[:rows]
        return carry

    lax.fori_loop(0, count, one, 0)


def add_kernel(cols, received, out, total):
    count, parts, rows, size = received.shape
    total[...] = jnp.zeros_like(total)
    edge = jnp.zeros((rows, LANES), F32)

    def one(j, carry):
        across = pl.ds(pl.multiple_of(cols[j] // LANES * LANES, LANES), size + LANES)
        shift = lax.rem(cols[j], LANES)
        for k in range(parts):
            piece = jnp.concatenate([received[j, k], edge], axis=1)
            total[k, :, across] += pltpu.roll(piece, shift, 1)
        return carry

    lax.fori_loop(0, count, one, 0)
    out[...] = total[:, :, : out.shape[-1]]


def shards(object_field, probe, amplitude, pos_row, pos_col, strip_of):
    size = probe.shape[-1]
    modes = probe.shape[0]
    rows, cols = object_field.shape[1], object_field.shape[2]
    devices, groups = lax.axis_size("scan"), lax.axis_size("mode")
    padded_cols = cols + LANES
    forward, inverse = dft_tables(size)

    def swap(x):
        return lax.ppermute(x, "mode", [(0, 1), (1, 0)])

    planes, deep = devices // 4, -(-rows // 16) * 16
    fits = groups == 2 and devices == 4 * planes and planes == 4 and size % (64 * HALVES * planes) == 0 and modes * HALVES == 8
    fits = fits and cols % LANES == 0 and size // TILE == 2
    if fits and rows % 8 == 0 and devices * deep % TILE == 0 and devices * deep <= 2 * size:
        dma = pltpu.SemaphoreType.DMA
        chunks, chunk = modes * HALVES, size // HALVES
        vmem, lanes = pltpu.VMEM, (cols // LANES + 1) // 2 * LANES
        any_space = pl.BlockSpec(memory_space=pl.ANY)
        term, strip_grad = pl.pallas_call(
            core_kernel,
            out_shape=(vmem((modes, 2, size, size), BF16), vmem((2, rows, cols), F32)),
            in_specs=[SMEM] * 3 + [VMEM] + [any_space] * 4,
            out_specs=(VMEM, VMEM),
            scratch_shapes=[
                vmem((devices, 8, LANES), jnp.int32),
                vmem((devices * deep, lanes), BF16),
                vmem((devices * deep, cols - lanes), BF16),
                vmem((cols, size), BF16),
                vmem((size, devices * deep), BF16),
                vmem((devices * deep, size), BF16),
                vmem((modes, 2, size, size), F32),
                vmem((2, size, size), BF16),
                vmem((size, size), F32),
                vmem((2 * size, 2 * size), BF16),
                vmem((2 * size, 2 * size), BF16),
                vmem((modes, 2, size, size), F32),
                vmem((size, size), F32),
                vmem((size, size), F32),
                vmem((size, size), F32),
                vmem((2 * size, size), BF16),
                vmem((size, 2 * size), BF16),
                vmem((modes, 2, size, size), BF16),
                vmem((chunks, 2, chunk // 2, size), BF16),
                vmem((chunks, 2, chunk // 2, size), BF16),
                vmem((chunks, 2, chunk // 4, size), BF16),
                vmem((chunks, 2, chunk // 4, size), BF16),
                vmem((chunks, 2, chunk // 8, size), BF16),
                vmem((chunks, 2, chunk // 8, size), BF16),
                vmem((chunks, 2, chunk // 16, size), BF16),
                vmem((2, size, size), F32),
                vmem((size, size), F32),
                vmem((size, size), BF16),
                vmem((devices * deep, size), BF16),
                vmem((devices * deep, size), BF16),
                dma((3,)),
                dma((modes,)),
                dma((devices - 1,)),
                dma((devices - 1,)),
                dma((5, 2, planes)),
                dma((5, 2, planes)),
                dma((size // TILE,)),
                dma((size // TILE,)),
                dma((8, chunks, 2)),
                dma((8, chunks, 2)),
                dma((size // TILE,)),
                dma((size // TILE,)),
                dma((devices - 1,)),
                dma((devices - 1,)),
                dma,
                dma,
            ],
            compiler_params=pltpu.CompilerParams(
                vmem_limit_bytes=56 * 1024 * 1024, collective_id=0, has_side_effects=True
            ),
        )(strip_of, pos_row, pos_col, object_field, probe, amplitude[0], forward, inverse)
        return (strip_grad, term.astype(F32))

    lane = lax.broadcasted_iota(jnp.int32, (2, META, cols), 2)
    numbers = jnp.where(lane == 0, strip_of[0], jnp.where(lane == 1, pos_col[0] // LANES, pos_col[0] % LANES))
    packed = jnp.concatenate([object_field.astype(BF16), numbers.astype(BF16)], axis=1)
    me = lax.axis_index("mode")
    if groups == 2 and devices % PLANE == 0:
        dma, lines = pltpu.SemaphoreType.DMA, devices // PLANE
        held = pl.pallas_call(
            gather_kernel,
            out_shape=jax.ShapeDtypeStruct((2, devices, rows + META, cols), BF16),
            in_specs=[VMEM],
            out_specs=VMEM,
            scratch_shapes=[
                dma((max(lines - 1, 1),)),
                dma((max(lines - 1, 1),)),
                dma((lines, PLANE - 1)),
                dma((lines, PLANE - 1)),
                dma,
                dma,
            ],
            compiler_params=pltpu.CompilerParams(
                vmem_limit_bytes=56 * 1024 * 1024, collective_id=0, has_side_effects=True
            ),
        )(lax.dynamic_index_in_dim(packed, me, 0, keepdims=False))
    else:
        held = lax.all_gather(packed, "scan", axis=1)
    numbers = held[0, :, rows, :3].astype(jnp.int32)
    strips = numbers[:, 0]
    all_cols = numbers[:, 1] * LANES + numbers[:, 2]

    wave_shape = jax.ShapeDtypeStruct((2, size, size), F32)
    patch = pl.pallas_call(
        cut_kernel,
        out_shape=wave_shape,
        in_specs=[SMEM, SMEM, SMEM, VMEM],
        out_specs=VMEM,
        scratch_shapes=[pltpu.VMEM((2, devices * rows + 8, padded_cols), F32)],
        compiler_params=PARAMS,
    )(strips, pos_row, pos_col, held)

    def whole(*shape):
        return pl.BlockSpec(shape, lambda m: (0,) * len(shape))

    mode_spec = pl.BlockSpec((1, 2, size, size), lambda m: (m, 0, 0, 0))
    table_spec = whole(2 * size, 2 * size)
    buffers = [pltpu.VMEM((2 * size, size), BF16), pltpu.VMEM((size, 2 * size), BF16)]
    far, power = pl.pallas_call(
        forward_kernel,
        grid=(modes,),
        out_shape=(
            jax.ShapeDtypeStruct((modes, 2, size, size), F32),
            jax.ShapeDtypeStruct((size, size), F32),
        ),
        in_specs=[mode_spec, whole(2, size, size), table_spec, table_spec],
        out_specs=(mode_spec, whole(size, size)),
        scratch_shapes=buffers,
        compiler_params=PARAMS,
    )(probe, patch, forward, inverse)
    power = power + swap(power) if groups == 2 else lax.psum(power, "mode")
    term, grad = pl.pallas_call(
        backward_kernel,
        grid=(modes,),
        out_shape=(jax.ShapeDtypeStruct((modes, 2, size, size), BF16), wave_shape),
        in_specs=[
            mode_spec,
            mode_spec,
            whole(2, size, size),
            whole(size, size),
            whole(size, size),
            table_spec,
            table_spec,
        ],
        out_specs=(mode_spec, whole(2, size, size)),
        scratch_shapes=[pltpu.VMEM((size, size), F32)] + buffers,
        compiler_params=PARAMS,
    )(far, probe, patch, amplitude[0], power, inverse, forward)
    probe_grad = lax.psum(term, "scan").astype(F32)

    if groups == 2:
        mine = lax.dynamic_index_in_dim(grad, me, 0, keepdims=True)
        other = lax.dynamic_index_in_dim(grad, 1 - me, 0, keepdims=True)
        grad = mine + swap(other)
    else:
        grad = lax.psum(grad, "mode")
    parts = grad.shape[0]
    pieces = pl.pallas_call(
        place_kernel,
        out_shape=jax.ShapeDtypeStruct((devices, parts, rows, size), F32),
        in_specs=[SMEM, SMEM, VMEM],
        out_specs=VMEM,
        scratch_shapes=[pltpu.VMEM((parts, size + 2 * rows + 8, size), F32)],
        compiler_params=PARAMS,
    )(strips, pos_row, grad)
    received = lax.all_to_all(pieces.astype(BF16), "scan", 0, 0, tiled=False).astype(F32)
    strip_grad = pl.pallas_call(
        add_kernel,
        out_shape=jax.ShapeDtypeStruct((parts, rows, cols), F32),
        in_specs=[SMEM, VMEM],
        out_specs=VMEM,
        scratch_shapes=[pltpu.VMEM((parts, rows, padded_cols), F32)],
        compiler_params=PARAMS,
    )(all_cols, received)
    if groups == 2:
        theirs = swap(strip_grad)
        strip_grad = jnp.where(
            me == 0,
            jnp.concatenate([strip_grad, theirs]),
            jnp.concatenate([theirs, strip_grad]),
        )
    return (strip_grad, probe_grad)


def solution(mesh):
    return jax.shard_map(
        shards,
        mesh=mesh,
        in_specs=(
            P(None, "scan", None),
            P("mode", None, None, None),
            P("scan", None, None),
            P("scan"),
            P("scan"),
            P("scan"),
        ),
        out_specs=(P(None, "scan", None), P("mode", None, None, None)),
        check_vma=False,
    )
```

```python
import math

import jax
import jax.numpy as jnp
import numpy as np
from jax import lax
from jax.experimental import pallas as pl
from jax.experimental.pallas import tpu as pltpu
from jax.sharding import PartitionSpec as P

F32 = jnp.float32
BF16 = jnp.bfloat16
LANES = 128
HALVES = 2
META = 8
PLANE = 4
TILE = 256
ORDER = (
    (0, 0), (0, 1), (0, 2), (1, 0), (0, 3), (1, 1), (0, 4), (2, 0), (1, 2), (1, 3),
    (0, 5), (0, 6), (3, 0), (2, 1), (1, 4), (0, 7), (2, 3), (9, 0), (10, 0), (2, 2),
    (1, 5), (4, 0), (2, 4), (3, 1), (3, 3), (5, 0), (3, 4), (4, 1), (4, 3), (10, 1),
    (3, 2), (1, 7), (4, 4), (2, 5), (5, 3), (6, 0), (1, 6), (4, 2), (7, 0), (5, 4),
    (5, 1), (6, 3), (3, 5), (2, 7), (6, 4), (2, 6), (6, 1), (5, 2), (4, 5), (7, 3),
    (3, 7), (3, 6), (7, 4), (5, 5), (4, 7), (7, 1), (4, 6), (6, 2), (5, 7), (6, 5),
    (5, 6), (10, 2), (6, 7), (6, 6), (7, 5), (7, 6), (7, 7), (7, 2), (11, 0),
)
PLANES_FIRST = (2,)
PARAMS = pltpu.CompilerParams(vmem_limit_bytes=56 * 1024 * 1024)
VMEM = pl.BlockSpec(memory_space=pltpu.VMEM)
SMEM = pl.BlockSpec(memory_space=pltpu.SMEM)
MESH = pl.DeviceIdType.MESH


def dft_tables(size):
    positions = np.arange(size, dtype=np.int32)
    angles = (positions[:, None] * positions[None, :] % size).astype(np.float32)
    angles = angles * np.float32(2.0 * math.pi / size)
    norm = np.float32(1.0 / math.sqrt(size))
    cosine, sine = np.cos(angles) * norm, np.sin(angles) * norm
    forward = np.block([[cosine, sine], [-sine, cosine]])
    inverse = np.block([[cosine, -sine], [sine, cosine]])
    return jnp.asarray(forward, BF16), jnp.asarray(inverse, BF16)


def gather_kernel(mine, out, line_send, line_recv, plane_send, plane_recv, swap_send, swap_recv):
    count = out.shape[1]
    lines = count // PLANE
    scan, mode = lax.axis_index("scan"), lax.axis_index("mode")
    line, place = scan // PLANE, lax.rem(scan, PLANE)
    in_line = [(lax.rem(line + k, lines) * PLANE + place, mode) for k in range(1, lines)]
    in_plane = [(line * PLANE + lax.rem(place + t, PLANE), mode) for t in range(1, PLANE)]
    partner = (scan, 1 - mode)

    barrier = pltpu.get_barrier_semaphore()
    for peer in in_line + in_plane + [partner]:
        pl.semaphore_signal(barrier, inc=1, device_id=peer, device_id_type=pl.DeviceIdType.MESH)
    pl.semaphore_wait(barrier, len(in_line) + len(in_plane) + 1)

    def push(src, dst, send, recv, peer):
        copy = pltpu.make_async_remote_copy(
            src_ref=src,
            dst_ref=dst,
            send_sem=send,
            recv_sem=recv,
            device_id=peer,
            device_id_type=pl.DeviceIdType.MESH,
        )
        copy.start()
        return copy

    own = out.at[mode, scan]
    line_copies = [
        push(mine, own, line_send.at[k], line_recv.at[k], peer) for k, peer in enumerate(in_line)
    ]
    plane_copies = [
        push(mine, own, plane_send.at[0, t], plane_recv.at[0, t], peer) for t, peer in enumerate(in_plane)
    ]
    out[mode, scan] = mine[...]
    for k, arriving in enumerate(line_copies):
        arriving.wait_recv()
        piece = out.at[mode, lax.rem(line + lines - k - 1, lines) * PLANE + place]
        plane_copies += [
            push(piece, piece, plane_send.at[k + 1, t], plane_recv.at[k + 1, t], peer)
            for t, peer in enumerate(in_plane)
        ]
    for copy in plane_copies:
        copy.wait_recv()
    last = push(out.at[mode], out.at[mode], swap_send, swap_recv, partner)
    for copy in line_copies + plane_copies:
        copy.wait_send()
    last.wait()


def cut_kernel(strips, row, col, held, patch, window):
    count, rows = held.shape[1], held.shape[2] - META
    size, cols = patch.shape[-1], held.shape[-1]
    wide = size + LANES

    def place(j, carry):
        at = pl.ds(pl.multiple_of(strips[j] * rows, 8), rows)
        for c in range(2):
            window[c, at, :cols] = held[c, j].astype(F32)[:rows]
        return carry

    lax.fori_loop(0, count, place, 0)
    across = pl.ds(pl.multiple_of(col[0] // LANES * LANES, LANES), wide)
    back = lax.rem(wide - lax.rem(col[0], LANES), wide)
    up = lax.rem(72 - lax.rem(row[0], 8), 72)
    for c in range(2):

        def cut(i, carry, c=c):
            block = window[c, pl.ds(pl.multiple_of(row[0] // 8 * 8 + i * 64, 8), 72), across]
            block = pltpu.roll(block, up, 0)[:64]
            patch[c, pl.ds(pl.multiple_of(i * 64, 64), 64), :] = pltpu.roll(block, back, 1)[:, :size]
            return carry

        lax.fori_loop(0, size // 64, cut, 0)


def forward_kernel(probe, patch, left, right, far, power, wave, half):
    size = patch.shape[-1]

    def leave(i, carry):
        at = pl.ds(pl.multiple_of(i * 64, 64), 64)
        low = pl.ds(pl.multiple_of(size + i * 64, 64), 64)
        pr, pi, xr, xi = probe[0, 0, at], probe[0, 1, at], patch[0, at], patch[1, at]
        wave[at] = (pr * xr - pi * xi).astype(BF16)
        wave[low] = (pr * xi + pi * xr).astype(BF16)
        return carry

    lax.fori_loop(0, size // 64, leave, 0)
    rows_product(left, wave, half)
    first = pl.program_id(0) == 0

    def across(i, carry):
        at = pl.ds(pl.multiple_of(i * TILE, TILE), TILE)
        both = jnp.dot(half[at], right[...], preferred_element_type=F32)
        re, im = both[:, :size], both[:, size:]
        far[0, 0, at] = re
        far[0, 1, at] = im
        here = re * re + im * im
        power[at] = jnp.where(first, here, power[at] + here)
        return carry

    lax.fori_loop(0, size // TILE, across, 0)


def rows_product(left, wave, half):
    size = wave.shape[-1]
    for c in range(2):

        def down(i, carry, c=c):
            at = pl.ds(pl.multiple_of(c * size + i * TILE, TILE), TILE)
            to = pl.ds(pl.multiple_of(i * TILE, TILE), TILE)
            product = jnp.dot(left[at], wave[...], preferred_element_type=F32)
            half[to, c * size : (c + 1) * size] = product.astype(BF16)
            return carry

        lax.fori_loop(0, size // TILE, down, 0)


def backward_kernel(far, probe, patch, measured, power, left, right, term, grad, scale, wave, half):
    size = patch.shape[-1]
    first = pl.program_id(0) == 0

    @pl.when(first)
    def _():
        total = jnp.maximum(power[...], 0.25)
        scale[...] = 1.0 - measured[...] / jnp.sqrt(total)

    def residual(i, carry):
        at = pl.ds(pl.multiple_of(i * 64, 64), 64)
        low = pl.ds(pl.multiple_of(size + i * 64, 64), 64)
        wave[at] = (far[0, 0, at] * scale[at]).astype(BF16)
        wave[low] = (far[0, 1, at] * scale[at]).astype(BF16)
        return carry

    lax.fori_loop(0, size // 64, residual, 0)
    rows_product(left, wave, half)

    def across(i, carry):
        at = pl.ds(pl.multiple_of(i * TILE, TILE), TILE)
        both = jnp.dot(half[at], right[...], preferred_element_type=F32)
        br, bi = both[:, :size], both[:, size:]
        pr, pi, xr, xi = probe[0, 0, at], probe[0, 1, at], patch[0, at], patch[1, at]
        term[0, 0, at] = (xr * br + xi * bi).astype(BF16)
        term[0, 1, at] = (xr * bi - xi * br).astype(BF16)
        re, im = pr * br + pi * bi, pr * bi - pi * br
        grad[0, at] = jnp.where(first, re, grad[0, at] + re)
        grad[1, at] = jnp.where(first, im, grad[1, at] + im)
        return carry

    lax.fori_loop(0, size // TILE, across, 0)


def mesh_peer(scan, mode, planes, dx, dy, dz):
    z, y, x = scan // 4, lax.rem(scan // 2, 2), lax.rem(scan, 2)
    x, y = lax.rem(x + dx, 2), lax.rem(y + dy, 2)
    return (lax.rem(z + dz, planes) * 4 + y * 2 + x, mode)


def core_kernel(
    strip_of, row, col, field_hbm, probe_hbm, measured_hbm, left_hbm, right_hbm, result, strip_grad,
    field, held_a, held_b, col_hot, row_hot, cut, probe, patch, measured, left, right,
    far, power, power_in, scale, wave, half, term, got1, sum1, got2, sum2, got3, sum3, got4,
    grad, grad_in, summed, pieces, landed,
    load, load_probe, hop_send, hop_recv, swap_send, swap_recv, send, recv,
    part_send, part_recv, piece_send, piece_recv, strip_send, strip_recv,
):
    modes, size = probe.shape[0], patch.shape[-1]
    devices = lax.axis_size("scan")
    strip, width = strip_grad.shape[1], strip_grad.shape[2]
    planes = devices // 4
    scan, mode = lax.axis_index("scan"), lax.axis_index("mode")
    z, y, x = scan // 4, lax.rem(scan // 2, 2), lax.rem(scan, 2)
    partner = (scan, 1 - mode)
    peer_x = mesh_peer(scan, mode, planes, 1, 0, 0)
    peer_y = mesh_peer(scan, mode, planes, 0, 1, 0)
    chunk = size // HALVES
    deep = pieces.shape[0] // devices

    barrier = pltpu.get_barrier_semaphore()
    levels = (z, z + 1 - 2 * lax.rem(z, 2), z + 2 - 4 * (z // 2), 3 - z)
    plane, plane_x, plane_y = y * 2 + x, y * 2 + 1 - x, (1 - y) * 2 + x
    plane_d = (1 - y) * 2 + 1 - x
    everyone = [partner, peer_x, peer_y] + [(levels[k] * 4 + plane, mode) for k in range(1, planes)]
    for peer in everyone:
        pl.semaphore_signal(barrier, inc=1, device_id=peer, device_id_type=MESH)
    own_load = pltpu.make_async_copy(field_hbm.at[mode], field, load.at[3])
    own_load.start()

    def probe_load(m):
        return pltpu.make_async_copy(probe_hbm.at[m], probe.at[m], load_probe.at[m])

    whole = [(left_hbm, left), (right_hbm, right), (measured_hbm, measured)]
    loads = [pltpu.make_async_copy(src, dst, load.at[i]) for i, (src, dst) in enumerate(whole)]
    probe_load(0).start()
    for copy in loads:
        copy.start()
    for m in range(1, modes):
        probe_load(m).start()

    def rows(start, count, step):
        return pl.ds(pl.multiple_of(start, step), count)

    def one_hot(mask):
        return jnp.where(mask, 1.0, 0.0).astype(BF16)

    held, parts_at = (held_a, held_b), (0, held_a.shape[1], width)

    def strip_rows(side, k):
        return rows((side * planes + levels[k]) * deep, deep, deep)

    which = lax.broadcasted_iota(jnp.int32, (deep - strip, width), 0)
    numbers = jnp.where(which == 1, lax.rem(col[0], LANES), col[0] // LANES)
    numbers = jnp.where(which == 0, strip_of[0], numbers).astype(F32)
    own_load.wait()
    own = jnp.concatenate([field[...], numbers]).astype(BF16)
    for i in range(2):
        held[i][strip_rows(plane, 0)] = own[:, parts_at[i] : parts_at[i + 1]]
    pl.semaphore_wait(barrier, len(everyone))

    def remote(src, dst, send_sem, recv_sem, peer):
        return pltpu.make_async_remote_copy(
            src_ref=src, dst_ref=dst, send_sem=send_sem, recv_sem=recv_sem, device_id=peer, device_id_type=MESH
        )

    def number(slot, which, lanes):
        block = held_a[rows(slot * deep + deep - 16, 16, 16), :lanes].astype(F32)
        at = 16 - (deep - strip) + which
        return block[at : at + 1].astype(jnp.int32)

    def hop(kind, i, k, side, peer):
        at = held[i].at[strip_rows(side, k)]
        return remote(at, at, hop_send.at[kind, i, k], hop_recv.at[kind, i, k], peer)

    def hop_z(i, k):
        at = held[i].at[strip_rows(plane, 0)]
        return remote(at, at, hop_send.at[0, i, k], hop_recv.at[0, i, k], (levels[k] * 4 + plane, mode))

    def spread(k):
        for i in range(2):
            hop(1, i, k, plane, peer_x).start()
            hop(2, 1 - i, k, plane, peer_y).start()

    def relay(k):
        hop(1, 0, k, plane_x, peer_x).wait_recv()
        hop(3, 0, k, plane_x, peer_y).start()
        hop(2, 1, k, plane_y, peer_y).wait_recv()
        hop(3, 1, k, plane_y, peer_x).start()

    def absorb(side, first=False, last=False):
        taken = planes * deep
        at = rows(side * taken, taken, taken)
        got = jnp.dot(held_a[at], col_hot[: held_a.shape[1]], preferred_element_type=F32)
        got = got + jnp.dot(held_b[at], col_hot[held_a.shape[1] :], preferred_element_type=F32)
        cut[...] = got.astype(BF16)
        lane = lax.broadcasted_iota(jnp.int32, (1, taken), 1)
        target = jnp.full((1, taken), -1, jnp.int32)
        for j in range(planes):
            ahead = lane - j * deep
            begin = number(side * planes + j, 0, taken) * strip
            target = jnp.where((ahead >= 0) & (ahead < strip), begin + ahead, target)
        target = target - row[0]

        def line_hot(i, carry):
            line = lax.broadcasted_iota(jnp.int32, (64, taken), 0) + i * 64
            row_hot[rows(i * 64, 64, 64)] = one_hot(line == target)
            return carry

        lax.fori_loop(0, size // 64, line_hot, 0)
        for i in range(size // TILE):
            at = pl.ds(i * TILE, TILE)
            piled = jnp.dot(row_hot[at], cut[...], preferred_element_type=F32)
            if not first:
                piled = power[at] + piled
            if last:
                patch[mode, at] = piled.astype(BF16)
                patch_swap(i).start()
            else:
                power[at] = piled

    def patch_swap(i):
        at = rows(i * TILE, TILE, TILE)
        own = patch.at[mode, at]
        return remote(own, own, hop_send.at[4, i, 0], hop_recv.at[4, i, 0], partner)

    def slot_of(j):
        return lax.rem(j, 4) * planes + j // 4

    for k in range(1, planes):
        hop_z(0, k).start()
        hop_z(1, k).start()
    spread(0)

    def column_hot(i, carry):
        at = rows(i * LANES, LANES, LANES)
        lane = lax.broadcasted_iota(jnp.int32, (LANES, size), 1)
        col_hot[at] = one_hot(lax.broadcasted_iota(jnp.int32, (LANES, size), 0) + i * LANES - lane == col[0])
        return carry

    lax.fori_loop(0, width // LANES, column_hot, 0)
    for k in range(1, planes):
        hop(0, 0, k, plane, partner).wait_recv()
        hop(0, 1, k, plane, partner).wait_recv()
        spread(k)
        relay(k - 1)
    relay(planes - 1)
    absorb(plane, first=True)
    for k in range(planes):
        hop(1, 1, k, plane_x, peer_x).wait_recv()
    absorb(plane_x)
    for k in range(planes):
        hop(2, 0, k, plane_y, peer_y).wait_recv()
    absorb(plane_y)
    for k in range(planes):
        hop(3, 0, k, plane_d, peer_y).wait_recv()
        hop(3, 1, k, plane_d, peer_x).wait_recv()
    absorb(plane_d, last=True)
    for copy in loads:
        copy.wait()
    for i in range(size // TILE):
        patch_swap(i).wait_recv()

    def place(u):
        return u // HALVES, u % HALVES * chunk

    near, far_z = levels[1] * 4 + plane, levels[2] * 4 + plane
    along = {"x": (peer_x, x), "y": (peer_y, y), "n": ((near, mode), lax.rem(z, 2)), "f": ((far_z, mode), z // 2)}
    sums, gots = (None, sum1, sum2, sum3), (None, got1, got2, got3, got4)

    def way(u, c, stage):
        axes = ("nfxy", "nfyx")[c] if u in PLANES_FIRST else ("xynf", "yxnf")[c]
        return along[axes[stage - 1]]

    def base(u, c, stage):
        low = place(u)[1]
        for s in range(1, stage + 1):
            low = low + way(u, c, s)[1] * (chunk >> s)
        return low

    def exchange(u, c, stage):
        m, low = place(u)
        if stage > 4:
            stage = 9 - stage
            count = chunk >> stage
            own = result.at[m, c, rows(base(u, c, stage), count, count)]
            peer, stage = way(u, c, stage)[0], 9 - stage
            return remote(own, own, send.at[stage - 1, u, c], recv.at[stage - 1, u, c], peer)
        peer, bit = way(u, c, stage)
        count = chunk >> stage
        away = (1 - bit) * count
        src = term.at[m, c, rows(low + away, count, count)] if stage == 1 else sums[stage - 1].at[u, c, rows(away, count, count)]
        return remote(src, gots[stage].at[u, c], send.at[stage - 1, u, c], recv.at[stage - 1, u, c], peer)

    def start(stage, u):
        for c in range(2):
            exchange(u, c, stage).start()

    def finish(stage, u):
        m, low = place(u)
        for c in range(2):
            exchange(u, c, stage).wait_recv()
            if stage > 4:
                continue
            count, bit = chunk >> stage, way(u, c, stage)[1]
            if stage == 1:
                mine = term[m, c, rows(low + bit * count, count, count)]
            else:
                mine = sums[stage - 1][u, c, rows(bit * count, count, count)]
            total = (mine.astype(F32) + gots[stage][u, c].astype(F32)).astype(BF16)
            if stage == 4:
                result[m, c, rows(base(u, c, 4), count, count)] = total
            else:
                sums[stage][u, c] = total

    def swap(i):
        at = rows(i * TILE, TILE, TILE)
        return remote(power.at[at], power_in.at[at], swap_send.at[i], swap_recv.at[i], partner)

    def product(table, source):
        out = jnp.dot(table[...], source[...], preferred_element_type=F32)
        half[:, :size] = out[:size].astype(BF16)
        half[:, size:] = out[size:].astype(BF16)

    def part(i):
        at = rows(i * TILE, TILE, TILE)
        return remote(grad.at[1 - mode, at], grad_in.at[at], part_send.at[i], part_recv.at[i], partner)

    mine = rows(scan * deep, deep, deep)

    def piece(k):
        to = lax.rem(scan + k, devices)
        return remote(pieces.at[rows(to * deep, deep, deep)], landed.at[mine], piece_send.at[k - 1], piece_recv.at[k - 1], (to, mode))

    def arrive(k):
        come = lax.rem(scan + devices - k, devices)
        at = rows(come * deep, deep, deep)
        return remote(pieces.at[at], landed.at[at], piece_send.at[k - 1], piece_recv.at[k - 1], (come, mode))

    def strip_swap():
        return remote(strip_grad.at[mode], strip_grad.at[mode], strip_send, strip_recv, partner)

    def cut_pieces():
        for i in range(size // TILE):
            part(i).wait_recv()
            at = pl.ds(i * TILE, TILE)
            summed[at] = (grad[mode, at] + grad_in[at]).astype(BF16)
        ahead = lax.broadcasted_iota(jnp.int32, (deep, size), 1) - lax.broadcasted_iota(jnp.int32, (deep, size), 0)

        def pick(j, carry):
            begin = number(slot_of(j), 0, size) * strip - row[0]
            wave[rows(j * deep, deep, deep)] = one_hot(ahead == begin)
            return carry

        lax.fori_loop(0, devices, pick, 0)

        def move(i, carry):
            at = rows(i * TILE, TILE, TILE)
            pieces[at] = jnp.dot(wave[at], summed[...], preferred_element_type=F32).astype(BF16)
            return carry

        lax.fori_loop(0, devices * deep // TILE, move, 0)
        landed[mine] = pieces[mine]

    def add_pieces():
        for k in range(1, devices):
            arrive(k).wait_recv()
        strip_grad[mode] = jnp.zeros((strip, width), F32)
        parts = size // LANES
        ahead = lax.broadcasted_iota(jnp.int32, (LANES, 2 * LANES), 1)
        ahead = ahead - lax.broadcasted_iota(jnp.int32, (LANES, 2 * LANES), 0)

        def one(j, carry):
            turn, whole_lanes = one_hot(ahead == number(slot_of(j), 1, 2 * LANES)), number(slot_of(j), 2, LANES)
            blocks = jnp.concatenate(
                [landed[rows(j * deep, deep, deep), b * LANES : (b + 1) * LANES] for b in range(parts)]
            )
            moved = jnp.dot(blocks, turn, preferred_element_type=F32)
            for b in range(parts + 1):
                here = moved[b * deep : b * deep + strip, :LANES] if b < parts else 0.0
                if b > 0:
                    here = here + moved[(b - 1) * deep : (b - 1) * deep + strip, LANES:]
                for t in range((width - size) // LANES + 1):
                    if b + t < width // LANES:
                        to = slice((b + t) * LANES, (b + t + 1) * LANES)
                        strip_grad[mode, :, to] += jnp.where(whole_lanes == t, here, 0.0)
            return carry

        lax.fori_loop(0, devices, one, 0)
        strip_swap().start()

    def forward(m, carry):
        probe_load(m).wait()

        def leave(i, carry):
            at, low = rows(i * 64, 64, 64), rows(size + i * 64, 64, 64)
            pr, pi, xr, xi = probe[m, 0, at], probe[m, 1, at], patch[0, at].astype(F32), patch[1, at].astype(F32)
            wave[at] = (pr * xr - pi * xi).astype(BF16)
            wave[low] = (pr * xi + pi * xr).astype(BF16)
            return carry

        lax.fori_loop(0, size // 64, leave, 0)
        product(left, wave)

        def across(i, carry):
            at = rows(i * TILE, TILE, TILE)
            both = jnp.dot(half[at], right[...], preferred_element_type=F32)
            re, im = both[:, :size], both[:, size:]
            far[m, 0, at] = re
            far[m, 1, at] = im
            here = re * re + im * im
            power[at] = jnp.where(m == 0, here, power[at] + here)

            @pl.when(m == modes - 1)
            def _():
                swap(i).start()

            return carry

        lax.fori_loop(0, size // TILE, across, 0)
        return carry

    lax.fori_loop(0, modes, forward, 0)
    for i in range(size // TILE):
        at = pl.ds(i * TILE, TILE)
        swap(i).wait_recv()
        total = jnp.maximum(power[at] + power_in[at], 0.25)
        scale[at] = 1.0 - measured[at] / jnp.sqrt(total)

    def backward(m):
        def residual(i, carry):
            at, low = rows(i * 64, 64, 64), rows(size + i * 64, 64, 64)
            wave[at] = (far[m, 0, at] * scale[at]).astype(BF16)
            wave[low] = (far[m, 1, at] * scale[at]).astype(BF16)
            return carry

        lax.fori_loop(0, size // 64, residual, 0)
        product(right, wave)

    def across_back(m, i):
        at = pl.ds(i * TILE, TILE)
        both = jnp.dot(half[at], left[...], preferred_element_type=F32)
        br, bi = both[:, :size], both[:, size:]
        pr, pi, xr, xi = probe[m, 0, at], probe[m, 1, at], patch[0, at].astype(F32), patch[1, at].astype(F32)
        term[m, 0, at] = (xr * br + xi * bi).astype(BF16)
        term[m, 1, at] = (xr * bi - xi * br).astype(BF16)
        re, im = pr * br + pi * bi, pr * bi - pi * br
        grad[0, at] = re if m == 0 else grad[0, at] + re
        grad[1, at] = im if m == 0 else grad[1, at] + im
        if m == modes - 1:
            part(i).start()

    for step, u in ORDER:
        if step == 0:
            if u % HALVES == 0:
                backward(u // HALVES)
            across_back(u // HALVES, u % HALVES)
            start(1, u)
        elif step < 8:
            finish(step, u)
            start(step + 1, u)
        elif step == 9:
            cut_pieces()
        elif step == 10:
            for k in range(1 + u, devices, 3):
                piece(k).start()
        else:
            add_pieces()

    for u in range(modes * HALVES):
        finish(8, u)
        for c in range(2):
            for stage in range(1, 9):
                exchange(u, c, stage).wait_send()
    for i in range(size // TILE):
        swap(i).wait_send()
        part(i).wait_send()
    for k in range(1, devices):
        piece(k).wait_send()
    strip_swap().wait()
    for i in range(size // TILE):
        patch_swap(i).wait_send()
    for i in range(2):
        for k in range(planes):
            if k:
                hop_z(i, k).wait_send()
            hop(1, i, k, plane, peer_x).wait_send()
            hop(2, i, k, plane, peer_y).wait_send()
            hop(3, i, k, (plane_x, plane_y)[i], (peer_y, peer_x)[i]).wait_send()


def cast_kernel(summed, strips, wide, strip_grad, block, done, strip_done):
    modes, depth = summed.shape[0], block.shape[0]
    last = pltpu.make_async_copy(strips, strip_grad, strip_done)
    last.start()

    def out(i):
        return pltpu.make_async_copy(block.at[i % depth], wide.at[i // 2, i % 2], done.at[i % depth])

    for i in range(2 * modes):
        if i >= depth:
            out(i - depth).wait()
        block[i % depth] = summed[i // 2, i % 2].astype(F32)
        out(i).start()
    for i in range(max(2 * modes - depth, 0), 2 * modes):
        out(i).wait()
    last.wait()


def place_kernel(strips, row, grad, out, padded):
    count, parts, rows, size = out.shape
    padded[...] = jnp.zeros_like(padded)
    padded[:, rows : rows + size, :] = grad[...]

    def one(j, carry):
        start = jnp.clip(strips[j] * rows - row[0], -rows, size) + rows
        base = pl.ds(pl.multiple_of(start // 8 * 8, 8), rows + 8)
        up = lax.rem(rows + 8 - lax.rem(start, 8), rows + 8)
        for k in range(parts):
            out[j, k] = pltpu.roll(padded[k, base, :], up, 0)[:rows]
        return carry

    lax.fori_loop(0, count, one, 0)


def add_kernel(cols, received, out, total):
    count, parts, rows, size = received.shape
    total[...] = jnp.zeros_like(total)
    edge = jnp.zeros((rows, LANES), F32)

    def one(j, carry):
        across = pl.ds(pl.multiple_of(cols[j] // LANES * LANES, LANES), size + LANES)
        shift = lax.rem(cols[j], LANES)
        for k in range(parts):
            piece = jnp.concatenate([received[j, k], edge], axis=1)
            total[k, :, across] += pltpu.roll(piece, shift, 1)
        return carry

    lax.fori_loop(0, count, one, 0)
    out[...] = total[:, :, : out.shape[-1]]


def shards(object_field, probe, amplitude, pos_row, pos_col, strip_of):
    size = probe.shape[-1]
    modes = probe.shape[0]
    rows, cols = object_field.shape[1], object_field.shape[2]
    devices, groups = lax.axis_size("scan"), lax.axis_size("mode")
    padded_cols = cols + LANES
    forward, inverse = dft_tables(size)

    def swap(x):
        return lax.ppermute(x, "mode", [(0, 1), (1, 0)])

    planes, deep = devices // 4, -(-rows // 16) * 16
    fits = groups == 2 and devices == 4 * planes and planes == 4 and size % (64 * HALVES * planes) == 0 and modes * HALVES == 8
    fits = fits and cols % LANES == 0 and size // TILE == 2
    fits = fits and deep - rows >= 8
    if fits and rows % 8 == 0 and devices * deep % TILE == 0 and devices * deep <= 2 * size:
        dma = pltpu.SemaphoreType.DMA
        chunks, chunk = modes * HALVES, size // HALVES
        vmem, lanes = pltpu.VMEM, (cols // LANES + 1) // 2 * LANES
        any_space = pl.BlockSpec(memory_space=pl.ANY)
        term, strip_grad = pl.pallas_call(
            core_kernel,
            out_shape=(vmem((modes, 2, size, size), BF16), vmem((2, rows, cols), F32)),
            in_specs=[SMEM] * 3 + [any_space] * 5,
            out_specs=(VMEM, VMEM),
            scratch_shapes=[
                vmem((rows, cols), F32),
                vmem((devices * deep, lanes), BF16),
                vmem((devices * deep, cols - lanes), BF16),
                vmem((cols, size), BF16),
                vmem((size, planes * deep), BF16),
                vmem((planes * deep, size), BF16),
                vmem((modes, 2, size, size), F32),
                vmem((2, size, size), BF16),
                vmem((size, size), F32),
                vmem((2 * size, 2 * size), BF16),
                vmem((2 * size, 2 * size), BF16),
                vmem((modes, 2, size, size), F32),
                vmem((size, size), F32),
                vmem((size, size), F32),
                vmem((size, size), F32),
                vmem((2 * size, size), BF16),
                vmem((size, 2 * size), BF16),
                vmem((modes, 2, size, size), BF16),
                vmem((chunks, 2, chunk // 2, size), BF16),
                vmem((chunks, 2, chunk // 2, size), BF16),
                vmem((chunks, 2, chunk // 4, size), BF16),
                vmem((chunks, 2, chunk // 4, size), BF16),
                vmem((chunks, 2, chunk // 8, size), BF16),
                vmem((chunks, 2, chunk // 8, size), BF16),
                vmem((chunks, 2, chunk // 16, size), BF16),
                vmem((2, size, size), F32),
                vmem((size, size), F32),
                vmem((size, size), BF16),
                vmem((devices * deep, size), BF16),
                vmem((devices * deep, size), BF16),
                dma((4,)),
                dma((modes,)),
                dma((5, 2, planes)),
                dma((5, 2, planes)),
                dma((size // TILE,)),
                dma((size // TILE,)),
                dma((8, chunks, 2)),
                dma((8, chunks, 2)),
                dma((size // TILE,)),
                dma((size // TILE,)),
                dma((devices - 1,)),
                dma((devices - 1,)),
                dma,
                dma,
            ],
            compiler_params=pltpu.CompilerParams(
                vmem_limit_bytes=56 * 1024 * 1024, collective_id=0, has_side_effects=True
            ),
        )(strip_of, pos_row, pos_col, object_field, probe, amplitude[0], forward, inverse)
        probe_grad, strip_grad = pl.pallas_call(
            cast_kernel,
            out_shape=(jax.ShapeDtypeStruct(term.shape, F32), jax.ShapeDtypeStruct(strip_grad.shape, F32)),
            in_specs=[VMEM] * 2,
            out_specs=(any_space, any_space),
            scratch_shapes=[vmem((4, size, size), F32), dma((4,)), dma],
            compiler_params=pltpu.CompilerParams(vmem_limit_bytes=16 * 1024 * 1024),
        )(pltpu.with_memory_space_constraint(term, vmem), pltpu.with_memory_space_constraint(strip_grad, vmem))
        return (strip_grad, probe_grad)

    lane = lax.broadcasted_iota(jnp.int32, (2, META, cols), 2)
    numbers = jnp.where(lane == 0, strip_of[0], jnp.where(lane == 1, pos_col[0] // LANES, pos_col[0] % LANES))
    packed = jnp.concatenate([object_field.astype(BF16), numbers.astype(BF16)], axis=1)
    me = lax.axis_index("mode")
    if groups == 2 and devices % PLANE == 0:
        dma, lines = pltpu.SemaphoreType.DMA, devices // PLANE
        held = pl.pallas_call(
            gather_kernel,
            out_shape=jax.ShapeDtypeStruct((2, devices, rows + META, cols), BF16),
            in_specs=[VMEM],
            out_specs=VMEM,
            scratch_shapes=[
                dma((max(lines - 1, 1),)),
                dma((max(lines - 1, 1),)),
                dma((lines, PLANE - 1)),
                dma((lines, PLANE - 1)),
                dma,
                dma,
            ],
            compiler_params=pltpu.CompilerParams(
                vmem_limit_bytes=56 * 1024 * 1024, collective_id=0, has_side_effects=True
            ),
        )(lax.dynamic_index_in_dim(packed, me, 0, keepdims=False))
    else:
        held = lax.all_gather(packed, "scan", axis=1)
    numbers = held[0, :, rows, :3].astype(jnp.int32)
    strips = numbers[:, 0]
    all_cols = numbers[:, 1] * LANES + numbers[:, 2]

    wave_shape = jax.ShapeDtypeStruct((2, size, size), F32)
    patch = pl.pallas_call(
        cut_kernel,
        out_shape=wave_shape,
        in_specs=[SMEM, SMEM, SMEM, VMEM],
        out_specs=VMEM,
        scratch_shapes=[pltpu.VMEM((2, devices * rows + 8, padded_cols), F32)],
        compiler_params=PARAMS,
    )(strips, pos_row, pos_col, held)

    def whole(*shape):
        return pl.BlockSpec(shape, lambda m: (0,) * len(shape))

    mode_spec = pl.BlockSpec((1, 2, size, size), lambda m: (m, 0, 0, 0))
    table_spec = whole(2 * size, 2 * size)
    buffers = [pltpu.VMEM((2 * size, size), BF16), pltpu.VMEM((size, 2 * size), BF16)]
    far, power = pl.pallas_call(
        forward_kernel,
        grid=(modes,),
        out_shape=(
            jax.ShapeDtypeStruct((modes, 2, size, size), F32),
            jax.ShapeDtypeStruct((size, size), F32),
        ),
        in_specs=[mode_spec, whole(2, size, size), table_spec, table_spec],
        out_specs=(mode_spec, whole(size, size)),
        scratch_shapes=buffers,
        compiler_params=PARAMS,
    )(probe, patch, forward, inverse)
    power = power + swap(power) if groups == 2 else lax.psum(power, "mode")
    term, grad = pl.pallas_call(
        backward_kernel,
        grid=(modes,),
        out_shape=(jax.ShapeDtypeStruct((modes, 2, size, size), BF16), wave_shape),
        in_specs=[
            mode_spec,
            mode_spec,
            whole(2, size, size),
            whole(size, size),
            whole(size, size),
            table_spec,
            table_spec,
        ],
        out_specs=(mode_spec, whole(2, size, size)),
        scratch_shapes=[pltpu.VMEM((size, size), F32)] + buffers,
        compiler_params=PARAMS,
    )(far, probe, patch, amplitude[0], power, inverse, forward)
    probe_grad = lax.psum(term, "scan").astype(F32)

    if groups == 2:
        mine = lax.dynamic_index_in_dim(grad, me, 0, keepdims=True)
        other = lax.dynamic_index_in_dim(grad, 1 - me, 0, keepdims=True)
        grad = mine + swap(other)
    else:
        grad = lax.psum(grad, "mode")
    parts = grad.shape[0]
    pieces = pl.pallas_call(
        place_kernel,
        out_shape=jax.ShapeDtypeStruct((devices, parts, rows, size), F32),
        in_specs=[SMEM, SMEM, VMEM],
        out_specs=VMEM,
        scratch_shapes=[pltpu.VMEM((parts, size + 2 * rows + 8, size), F32)],
        compiler_params=PARAMS,
    )(strips, pos_row, grad)
    received = lax.all_to_all(pieces.astype(BF16), "scan", 0, 0, tiled=False).astype(F32)
    strip_grad = pl.pallas_call(
        add_kernel,
        out_shape=jax.ShapeDtypeStruct((parts, rows, cols), F32),
        in_specs=[SMEM, VMEM],
        out_specs=VMEM,
        scratch_shapes=[pltpu.VMEM((parts, rows, padded_cols), F32)],
        compiler_params=PARAMS,
    )(all_cols, received)
    if groups == 2:
        theirs = swap(strip_grad)
        strip_grad = jnp.where(
            me == 0,
            jnp.concatenate([strip_grad, theirs]),
            jnp.concatenate([theirs, strip_grad]),
        )
    return (strip_grad, probe_grad)


def solution(mesh):
    return jax.shard_map(
        shards,
        mesh=mesh,
        in_specs=(
            P(None, "scan", None),
            P("mode", None, None, None),
            P("scan", None, None),
            P("scan"),
            P("scan"),
            P("scan"),
        ),
        out_specs=(P(None, "scan", None), P("mode", None, None, None)),
        check_vma=False,
    )
```

```python
import math

import jax
import jax.numpy as jnp
import numpy as np
from jax import lax
from jax.experimental import pallas as pl
from jax.experimental.pallas import tpu as pltpu
from jax.sharding import PartitionSpec as P

F32 = jnp.float32
BF16 = jnp.bfloat16
LANES = 128
HALVES = 2
META = 8
PLANE = 4
TILE = 256
ORDER = (
    (0, 0), (0, 1), (0, 2), (0, 3), (1, 0), (1, 1), (0, 4), (1, 3), (0, 5), (2, 1),
    (1, 2), (0, 6), (1, 4), (0, 7), (2, 3), (3, 1), (9, 0), (1, 5), (2, 0), (3, 3),
    (10, 1), (10, 2), (4, 1), (2, 4), (2, 2), (4, 3), (1, 6), (10, 3), (10, 4), (10, 5),
    (2, 5), (5, 1), (3, 4), (5, 3), (1, 7), (3, 0), (3, 5), (6, 1), (10, 6), (10, 7),
    (10, 8), (3, 2), (2, 7), (6, 3), (4, 5), (2, 6), (4, 4), (7, 1), (4, 2), (4, 0),
    (3, 7), (7, 3), (5, 5), (3, 6), (5, 4), (10, 9), (10, 10), (5, 0), (5, 2), (6, 5),
    (4, 7), (4, 6), (6, 4), (10, 11), (10, 12), (7, 5), (6, 0), (5, 7), (5, 6), (7, 4),
    (6, 2), (6, 7), (10, 13), (10, 14), (10, 15), (6, 6), (7, 0), (7, 2), (7, 7), (7, 6),
    (11, 0),
)
PLANES_FIRST = ((2, 0), (2, 1), (0, 1))
PARAMS = pltpu.CompilerParams(vmem_limit_bytes=56 * 1024 * 1024)
VMEM = pl.BlockSpec(memory_space=pltpu.VMEM)
SMEM = pl.BlockSpec(memory_space=pltpu.SMEM)
MESH = pl.DeviceIdType.MESH


def dft_tables(size):
    positions = np.arange(size, dtype=np.int32)
    angles = (positions[:, None] * positions[None, :] % size).astype(np.float32)
    angles = angles * np.float32(2.0 * math.pi / size)
    norm = np.float32(1.0 / math.sqrt(size))
    cosine, sine = np.cos(angles) * norm, np.sin(angles) * norm
    forward = np.block([[cosine, sine], [-sine, cosine]])
    inverse = np.block([[cosine, -sine], [sine, cosine]])
    return jnp.asarray(forward, BF16), jnp.asarray(inverse, BF16)


def gather_kernel(mine, out, line_send, line_recv, plane_send, plane_recv, swap_send, swap_recv):
    count = out.shape[1]
    lines = count // PLANE
    scan, mode = lax.axis_index("scan"), lax.axis_index("mode")
    line, place = scan // PLANE, lax.rem(scan, PLANE)
    in_line = [(lax.rem(line + k, lines) * PLANE + place, mode) for k in range(1, lines)]
    in_plane = [(line * PLANE + lax.rem(place + t, PLANE), mode) for t in range(1, PLANE)]
    partner = (scan, 1 - mode)

    barrier = pltpu.get_barrier_semaphore()
    for peer in in_line + in_plane + [partner]:
        pl.semaphore_signal(barrier, inc=1, device_id=peer, device_id_type=pl.DeviceIdType.MESH)
    pl.semaphore_wait(barrier, len(in_line) + len(in_plane) + 1)

    def push(src, dst, send, recv, peer):
        copy = pltpu.make_async_remote_copy(
            src_ref=src,
            dst_ref=dst,
            send_sem=send,
            recv_sem=recv,
            device_id=peer,
            device_id_type=pl.DeviceIdType.MESH,
        )
        copy.start()
        return copy

    own = out.at[mode, scan]
    line_copies = [
        push(mine, own, line_send.at[k], line_recv.at[k], peer) for k, peer in enumerate(in_line)
    ]
    plane_copies = [
        push(mine, own, plane_send.at[0, t], plane_recv.at[0, t], peer) for t, peer in enumerate(in_plane)
    ]
    out[mode, scan] = mine[...]
    for k, arriving in enumerate(line_copies):
        arriving.wait_recv()
        piece = out.at[mode, lax.rem(line + lines - k - 1, lines) * PLANE + place]
        plane_copies += [
            push(piece, piece, plane_send.at[k + 1, t], plane_recv.at[k + 1, t], peer)
            for t, peer in enumerate(in_plane)
        ]
    for copy in plane_copies:
        copy.wait_recv()
    last = push(out.at[mode], out.at[mode], swap_send, swap_recv, partner)
    for copy in line_copies + plane_copies:
        copy.wait_send()
    last.wait()


def cut_kernel(strips, row, col, held, patch, window):
    count, rows = held.shape[1], held.shape[2] - META
    size, cols = patch.shape[-1], held.shape[-1]
    wide = size + LANES

    def place(j, carry):
        at = pl.ds(pl.multiple_of(strips[j] * rows, 8), rows)
        for c in range(2):
            window[c, at, :cols] = held[c, j].astype(F32)[:rows]
        return carry

    lax.fori_loop(0, count, place, 0)
    across = pl.ds(pl.multiple_of(col[0] // LANES * LANES, LANES), wide)
    back = lax.rem(wide - lax.rem(col[0], LANES), wide)
    up = lax.rem(72 - lax.rem(row[0], 8), 72)
    for c in range(2):

        def cut(i, carry, c=c):
            block = window[c, pl.ds(pl.multiple_of(row[0] // 8 * 8 + i * 64, 8), 72), across]
            block = pltpu.roll(block, up, 0)[:64]
            patch[c, pl.ds(pl.multiple_of(i * 64, 64), 64), :] = pltpu.roll(block, back, 1)[:, :size]
            return carry

        lax.fori_loop(0, size // 64, cut, 0)


def forward_kernel(probe, patch, left, right, far, power, wave, half):
    size = patch.shape[-1]

    def leave(i, carry):
        at = pl.ds(pl.multiple_of(i * 64, 64), 64)
        low = pl.ds(pl.multiple_of(size + i * 64, 64), 64)
        pr, pi, xr, xi = probe[0, 0, at], probe[0, 1, at], patch[0, at], patch[1, at]
        wave[at] = (pr * xr - pi * xi).astype(BF16)
        wave[low] = (pr * xi + pi * xr).astype(BF16)
        return carry

    lax.fori_loop(0, size // 64, leave, 0)
    rows_product(left, wave, half)
    first = pl.program_id(0) == 0

    def across(i, carry):
        at = pl.ds(pl.multiple_of(i * TILE, TILE), TILE)
        both = jnp.dot(half[at], right[...], preferred_element_type=F32)
        re, im = both[:, :size], both[:, size:]
        far[0, 0, at] = re
        far[0, 1, at] = im
        here = re * re + im * im
        power[at] = jnp.where(first, here, power[at] + here)
        return carry

    lax.fori_loop(0, size // TILE, across, 0)


def rows_product(left, wave, half):
    size = wave.shape[-1]
    for c in range(2):

        def down(i, carry, c=c):
            at = pl.ds(pl.multiple_of(c * size + i * TILE, TILE), TILE)
            to = pl.ds(pl.multiple_of(i * TILE, TILE), TILE)
            product = jnp.dot(left[at], wave[...], preferred_element_type=F32)
            half[to, c * size : (c + 1) * size] = product.astype(BF16)
            return carry

        lax.fori_loop(0, size // TILE, down, 0)


def backward_kernel(far, probe, patch, measured, power, left, right, term, grad, scale, wave, half):
    size = patch.shape[-1]
    first = pl.program_id(0) == 0

    @pl.when(first)
    def _():
        total = jnp.maximum(power[...], 0.25)
        scale[...] = 1.0 - measured[...] / jnp.sqrt(total)

    def residual(i, carry):
        at = pl.ds(pl.multiple_of(i * 64, 64), 64)
        low = pl.ds(pl.multiple_of(size + i * 64, 64), 64)
        wave[at] = (far[0, 0, at] * scale[at]).astype(BF16)
        wave[low] = (far[0, 1, at] * scale[at]).astype(BF16)
        return carry

    lax.fori_loop(0, size // 64, residual, 0)
    rows_product(left, wave, half)

    def across(i, carry):
        at = pl.ds(pl.multiple_of(i * TILE, TILE), TILE)
        both = jnp.dot(half[at], right[...], preferred_element_type=F32)
        br, bi = both[:, :size], both[:, size:]
        pr, pi, xr, xi = probe[0, 0, at], probe[0, 1, at], patch[0, at], patch[1, at]
        term[0, 0, at] = (xr * br + xi * bi).astype(BF16)
        term[0, 1, at] = (xr * bi - xi * br).astype(BF16)
        re, im = pr * br + pi * bi, pr * bi - pi * br
        grad[0, at] = jnp.where(first, re, grad[0, at] + re)
        grad[1, at] = jnp.where(first, im, grad[1, at] + im)
        return carry

    lax.fori_loop(0, size // TILE, across, 0)


def mesh_peer(scan, mode, planes, dx, dy, dz):
    z, y, x = scan // 4, lax.rem(scan // 2, 2), lax.rem(scan, 2)
    x, y = lax.rem(x + dx, 2), lax.rem(y + dy, 2)
    return (lax.rem(z + dz, planes) * 4 + y * 2 + x, mode)


def core_kernel(
    strip_of, row, col, field_hbm, probe_hbm, measured_hbm, left_hbm, right_hbm, result, strip_grad,
    field, held_a, held_b, col_hot, row_hot, cut, probe, patch, measured, left, right,
    far, power, power_in, scale, wave, half, term, got1, sum1, got2, sum2, got3, sum3, got4,
    grad, grad_in, summed, pieces, landed,
    load, load_probe, hop_send, hop_recv, swap_send, swap_recv, send, recv,
    part_send, part_recv, piece_send, piece_recv, strip_send, strip_recv,
):
    modes, size = probe.shape[0], patch.shape[-1]
    devices = lax.axis_size("scan")
    strip, width = strip_grad.shape[1], strip_grad.shape[2]
    planes = devices // 4
    scan, mode = lax.axis_index("scan"), lax.axis_index("mode")
    z, y, x = scan // 4, lax.rem(scan // 2, 2), lax.rem(scan, 2)
    partner = (scan, 1 - mode)
    peer_x = mesh_peer(scan, mode, planes, 1, 0, 0)
    peer_y = mesh_peer(scan, mode, planes, 0, 1, 0)
    chunk = size // HALVES
    deep, tall = held_a.shape[0] // devices, pieces.shape[0] // devices

    barrier = pltpu.get_barrier_semaphore()
    levels = (z, z + 1 - 2 * lax.rem(z, 2), z + 2 - 4 * (z // 2), 3 - z)
    plane, plane_x, plane_y = y * 2 + x, y * 2 + 1 - x, (1 - y) * 2 + x
    plane_d = (1 - y) * 2 + 1 - x
    everyone = [partner, peer_x, peer_y] + [(levels[k] * 4 + plane, mode) for k in range(1, planes)]
    for peer in everyone:
        pl.semaphore_signal(barrier, inc=1, device_id=peer, device_id_type=MESH)
    own_load = pltpu.make_async_copy(field_hbm.at[mode], field, load.at[3])
    own_load.start()

    def probe_load(m):
        return pltpu.make_async_copy(probe_hbm.at[m], probe.at[m], load_probe.at[m])

    whole = [(left_hbm, left), (right_hbm, right), (measured_hbm, measured)]
    loads = [pltpu.make_async_copy(src, dst, load.at[i]) for i, (src, dst) in enumerate(whole)]
    probe_load(0).start()
    for copy in loads:
        copy.start()
    for m in range(1, modes):
        probe_load(m).start()

    def rows(start, count, step):
        return pl.ds(pl.multiple_of(start, step), count)

    def one_hot(mask):
        return jnp.where(mask, 1.0, 0.0).astype(BF16)

    held, parts_at = (held_a, held_b), (0, held_a.shape[1], width)

    def strip_rows(side, k):
        return rows((side * planes + levels[k]) * deep, deep, deep)

    which = lax.broadcasted_iota(jnp.int32, (deep - strip, width), 0)
    numbers = jnp.where(which == 1, lax.rem(col[0], LANES), col[0] // LANES)
    numbers = jnp.where(which == 0, strip_of[0], numbers).astype(F32)
    own_load.wait()
    own = jnp.concatenate([field[...], numbers]).astype(BF16)
    for i in range(2):
        held[i][strip_rows(plane, 0)] = own[:, parts_at[i] : parts_at[i + 1]]
    pl.semaphore_wait(barrier, len(everyone))

    def remote(src, dst, send_sem, recv_sem, peer):
        return pltpu.make_async_remote_copy(
            src_ref=src, dst_ref=dst, send_sem=send_sem, recv_sem=recv_sem, device_id=peer, device_id_type=MESH
        )

    def number(slot, which, lanes):
        block = held_a[rows(slot * deep + deep - 16, 16, 16), :lanes].astype(F32)
        at = 16 - (deep - strip) + which
        return block[at : at + 1].astype(jnp.int32)

    def hop(kind, i, k, side, peer):
        at = held[i].at[strip_rows(side, k)]
        return remote(at, at, hop_send.at[kind, i, k], hop_recv.at[kind, i, k], peer)

    def hop_z(i, k):
        at = held[i].at[strip_rows(plane, 0)]
        return remote(at, at, hop_send.at[0, i, k], hop_recv.at[0, i, k], (levels[k] * 4 + plane, mode))

    def spread(k):
        for i in range(2):
            hop(1, i, k, plane, peer_x).start()
            hop(2, 1 - i, k, plane, peer_y).start()

    def relay(k):
        hop(1, 0, k, plane_x, peer_x).wait_recv()
        hop(3, 0, k, plane_x, peer_y).start()
        hop(2, 1, k, plane_y, peer_y).wait_recv()
        hop(3, 1, k, plane_y, peer_x).start()

    def absorb(side, first=False, last=False):
        taken = planes * deep
        at = rows(side * taken, taken, taken)
        got = jnp.dot(held_a[at], col_hot[: held_a.shape[1]], preferred_element_type=F32)
        got = got + jnp.dot(held_b[at], col_hot[held_a.shape[1] :], preferred_element_type=F32)
        cut[...] = got.astype(BF16)
        lane = lax.broadcasted_iota(jnp.int32, (1, taken), 1)
        target = jnp.full((1, taken), -1, jnp.int32)
        for j in range(planes):
            ahead = lane - j * deep
            begin = number(side * planes + j, 0, taken) * strip
            target = jnp.where((ahead >= 0) & (ahead < strip), begin + ahead, target)
        target = target - row[0]

        def line_hot(i, carry):
            line = lax.broadcasted_iota(jnp.int32, (64, taken), 0) + i * 64
            row_hot[rows(i * 64, 64, 64)] = one_hot(line == target)
            return carry

        lax.fori_loop(0, size // 64, line_hot, 0)
        for i in range(size // TILE):
            at = pl.ds(i * TILE, TILE)
            piled = jnp.dot(row_hot[at], cut[...], preferred_element_type=F32)
            if not first:
                piled = power[at] + piled
            if last:
                patch[mode, at] = piled.astype(BF16)
                patch_swap(i).start()
            else:
                power[at] = piled

    def patch_swap(i):
        at = rows(i * TILE, TILE, TILE)
        own = patch.at[mode, at]
        return remote(own, own, hop_send.at[4, i, 0], hop_recv.at[4, i, 0], partner)

    def slot_of(j):
        return lax.rem(j, 4) * planes + j // 4

    for k in range(1, planes):
        hop_z(0, k).start()
        hop_z(1, k).start()
    spread(0)

    def column_hot(i, carry):
        at = rows(i * LANES, LANES, LANES)
        lane = lax.broadcasted_iota(jnp.int32, (LANES, size), 1)
        col_hot[at] = one_hot(lax.broadcasted_iota(jnp.int32, (LANES, size), 0) + i * LANES - lane == col[0])
        return carry

    lax.fori_loop(0, width // LANES, column_hot, 0)
    for k in range(1, planes):
        hop(0, 0, k, plane, partner).wait_recv()
        hop(0, 1, k, plane, partner).wait_recv()
        spread(k)
        relay(k - 1)
    relay(planes - 1)
    absorb(plane, first=True)
    for k in range(planes):
        hop(1, 1, k, plane_x, peer_x).wait_recv()
    absorb(plane_x)
    for k in range(planes):
        hop(2, 0, k, plane_y, peer_y).wait_recv()
    absorb(plane_y)
    for k in range(planes):
        hop(3, 0, k, plane_d, peer_y).wait_recv()
        hop(3, 1, k, plane_d, peer_x).wait_recv()
    absorb(plane_d, last=True)
    for copy in loads:
        copy.wait()
    for i in range(size // TILE):
        patch_swap(i).wait_recv()

    def place(u):
        return u // HALVES, u % HALVES * chunk

    near, far_z = levels[1] * 4 + plane, levels[2] * 4 + plane
    along = {"x": (peer_x, x), "y": (peer_y, y), "n": ((near, mode), lax.rem(z, 2)), "f": ((far_z, mode), z // 2)}
    sums, gots = (None, sum1, sum2, sum3), (None, got1, got2, got3, got4)

    def way(u, c, stage):
        axes = ("nfxy", "nfyx")[c] if (u, c) in PLANES_FIRST else ("xynf", "yxnf")[c]
        return along[axes[stage - 1]]

    def base(u, c, stage):
        low = place(u)[1]
        for s in range(1, stage + 1):
            low = low + way(u, c, s)[1] * (chunk >> s)
        return low

    def exchange(u, c, stage):
        m, low = place(u)
        if stage > 4:
            stage = 9 - stage
            count = chunk >> stage
            own = result.at[m, c, rows(base(u, c, stage), count, count)]
            peer, stage = way(u, c, stage)[0], 9 - stage
            return remote(own, own, send.at[stage - 1, u, c], recv.at[stage - 1, u, c], peer)
        peer, bit = way(u, c, stage)
        count = chunk >> stage
        away = (1 - bit) * count
        src = term.at[m, c, rows(low + away, count, count)] if stage == 1 else sums[stage - 1].at[u, c, rows(away, count, count)]
        return remote(src, gots[stage].at[u, c], send.at[stage - 1, u, c], recv.at[stage - 1, u, c], peer)

    def start(stage, u):
        for c in range(2):
            exchange(u, c, stage).start()

    def finish(stage, u):
        m, low = place(u)
        for c in range(2):
            exchange(u, c, stage).wait_recv()
            if stage > 4:
                continue
            count, bit = chunk >> stage, way(u, c, stage)[1]
            if stage == 1:
                mine = term[m, c, rows(low + bit * count, count, count)]
            else:
                mine = sums[stage - 1][u, c, rows(bit * count, count, count)]
            total = (mine.astype(F32) + gots[stage][u, c].astype(F32)).astype(BF16)
            if stage == 4:
                result[m, c, rows(base(u, c, 4), count, count)] = total
            else:
                sums[stage][u, c] = total

    def swap(i):
        at = rows(i * TILE, TILE, TILE)
        return remote(power.at[at], power_in.at[at], swap_send.at[i], swap_recv.at[i], partner)

    def product(table, source):
        out = jnp.dot(table[...], source[...], preferred_element_type=F32)
        half[:, :size] = out[:size].astype(BF16)
        half[:, size:] = out[size:].astype(BF16)

    def part(i):
        at = rows(i * TILE, TILE, TILE)
        return remote(grad.at[1 - mode, at], grad_in.at[at], part_send.at[i], part_recv.at[i], partner)

    mine = rows(scan * tall, tall, 16)

    def piece(k):
        to = lax.rem(scan + k, devices)
        return remote(pieces.at[rows(to * tall, tall, 16)], landed.at[mine], piece_send.at[k - 1], piece_recv.at[k - 1], (to, mode))

    def arrive(k):
        come = lax.rem(scan + devices - k, devices)
        at = rows(come * tall, tall, 16)
        return remote(pieces.at[at], landed.at[at], piece_send.at[k - 1], piece_recv.at[k - 1], (come, mode))

    def strip_swap():
        return remote(strip_grad.at[mode], strip_grad.at[mode], strip_send, strip_recv, partner)

    def cut_pieces():
        for i in range(size // TILE):
            part(i).wait_recv()
            at = pl.ds(i * TILE, TILE)
            summed[at] = (grad[mode, at] + grad_in[at]).astype(BF16)
        down = lax.broadcasted_iota(jnp.int32, (tall, size), 0)
        ahead = lax.broadcasted_iota(jnp.int32, (tall, size), 1) - jnp.where(down < strip, down, down - strip)

        def pick(i, carry):
            begins = [number(slot_of(2 * i + j), 0, size) * strip - row[0] for j in range(2)]
            wave[rows(i * tall, tall, 16)] = one_hot(ahead == jnp.where(down < strip, begins[0], begins[1]))
            return carry

        lax.fori_loop(0, devices // 2, pick, 0)

        def move(i, carry):
            out = jnp.dot(wave[rows(i * 4 * tall, 4 * tall, 16)], summed[...], preferred_element_type=F32)
            for j in range(8):
                block = out[j * strip : (j + 1) * strip]
                block = jnp.concatenate([block[:, : size // 2], block[:, size // 2 :]])
                pieces[rows((i * 8 + j) * tall, tall, 16)] = block.astype(BF16)
            return carry

        lax.fori_loop(0, devices // 8, move, 0)
        landed[mine] = pieces[mine]

    def add_pieces():
        for k in range(1, devices):
            arrive(k).wait_recv()
        strip_grad[mode] = jnp.zeros((strip, width), F32)
        parts = size // LANES
        ahead = lax.broadcasted_iota(jnp.int32, (LANES, 2 * LANES), 1)
        ahead = ahead - lax.broadcasted_iota(jnp.int32, (LANES, 2 * LANES), 0)

        def one(j, carry):
            turn, whole_lanes = one_hot(ahead == number(slot_of(j), 1, 2 * LANES)), number(slot_of(j), 2, LANES)
            piece_rows = landed[rows(j * tall, tall, 16)].astype(F32)
            blocks = jnp.concatenate(
                [
                    piece_rows[b * strip : (b + 1) * strip, at * LANES : (at + 1) * LANES]
                    for b in range(2)
                    for at in range(parts // 2)
                ]
            ).astype(BF16)
            moved = jnp.dot(blocks, turn, preferred_element_type=F32)
            for b in range(parts + 1):
                here = moved[b * strip : (b + 1) * strip, :LANES] if b < parts else 0.0
                if b > 0:
                    here = here + moved[(b - 1) * strip : b * strip, LANES:]
                for t in range((width - size) // LANES + 1):
                    if b + t < width // LANES:
                        to = slice((b + t) * LANES, (b + t + 1) * LANES)
                        strip_grad[mode, :, to] += jnp.where(whole_lanes == t, here, 0.0)
            return carry

        lax.fori_loop(0, devices, one, 0)
        strip_swap().start()

    def forward(m, carry):
        probe_load(m).wait()

        def leave(i, carry):
            at, low = rows(i * 64, 64, 64), rows(size + i * 64, 64, 64)
            pr, pi, xr, xi = probe[m, 0, at], probe[m, 1, at], patch[0, at].astype(F32), patch[1, at].astype(F32)
            wave[at] = (pr * xr - pi * xi).astype(BF16)
            wave[low] = (pr * xi + pi * xr).astype(BF16)
            return carry

        lax.fori_loop(0, size // 64, leave, 0)
        product(left, wave)

        def across(i, carry):
            at = rows(i * TILE, TILE, TILE)
            both = jnp.dot(half[at], right[...], preferred_element_type=F32)
            re, im = both[:, :size], both[:, size:]
            far[m, 0, at] = re
            far[m, 1, at] = im
            here = re * re + im * im
            power[at] = jnp.where(m == 0, here, power[at] + here)

            @pl.when(m == modes - 1)
            def _():
                swap(i).start()

            return carry

        lax.fori_loop(0, size // TILE, across, 0)
        return carry

    lax.fori_loop(0, modes, forward, 0)
    for i in range(size // TILE):
        at = pl.ds(i * TILE, TILE)
        swap(i).wait_recv()
        total = jnp.maximum(power[at] + power_in[at], 0.25)
        scale[at] = 1.0 - measured[at] / jnp.sqrt(total)

    def backward(m):
        def residual(i, carry):
            at, low = rows(i * 64, 64, 64), rows(size + i * 64, 64, 64)
            wave[at] = (far[m, 0, at] * scale[at]).astype(BF16)
            wave[low] = (far[m, 1, at] * scale[at]).astype(BF16)
            return carry

        lax.fori_loop(0, size // 64, residual, 0)
        product(right, wave)

    def across_back(m, i):
        at = pl.ds(i * TILE, TILE)
        both = jnp.dot(half[at], left[...], preferred_element_type=F32)
        br, bi = both[:, :size], both[:, size:]
        pr, pi, xr, xi = probe[m, 0, at], probe[m, 1, at], patch[0, at].astype(F32), patch[1, at].astype(F32)
        term[m, 0, at] = (xr * br + xi * bi).astype(BF16)
        term[m, 1, at] = (xr * bi - xi * br).astype(BF16)
        re, im = pr * br + pi * bi, pr * bi - pi * br
        grad[0, at] = re if m == 0 else grad[0, at] + re
        grad[1, at] = im if m == 0 else grad[1, at] + im
        if m == modes - 1:
            part(i).start()

    for step, u in ORDER:
        if step == 0:
            if u % HALVES == 0:
                backward(u // HALVES)
            across_back(u // HALVES, u % HALVES)
            start(1, u)
        elif step < 8:
            finish(step, u)
            start(step + 1, u)
        elif step == 9:
            cut_pieces()
        elif step == 10:
            piece(u).start()
        else:
            add_pieces()

    for u in range(modes * HALVES):
        finish(8, u)
        for c in range(2):
            for stage in range(1, 9):
                exchange(u, c, stage).wait_send()
    for i in range(size // TILE):
        swap(i).wait_send()
        part(i).wait_send()
    for k in range(1, devices):
        piece(k).wait_send()
    strip_swap().wait()
    for i in range(size // TILE):
        patch_swap(i).wait_send()
    for i in range(2):
        for k in range(planes):
            if k:
                hop_z(i, k).wait_send()
            hop(1, i, k, plane, peer_x).wait_send()
            hop(2, i, k, plane, peer_y).wait_send()
            hop(3, i, k, (plane_x, plane_y)[i], (peer_y, peer_x)[i]).wait_send()


def cast_kernel(summed, strips, wide, strip_grad, block, done, strip_done):
    modes, depth = summed.shape[0], block.shape[0]
    last = pltpu.make_async_copy(strips, strip_grad, strip_done)
    last.start()

    def out(i):
        return pltpu.make_async_copy(block.at[i % depth], wide.at[i // 2, i % 2], done.at[i % depth])

    for i in range(2 * modes):
        if i >= depth:
            out(i - depth).wait()
        block[i % depth] = summed[i // 2, i % 2].astype(F32)
        out(i).start()
    for i in range(max(2 * modes - depth, 0), 2 * modes):
        out(i).wait()
    last.wait()


def place_kernel(strips, row, grad, out, padded):
    count, parts, rows, size = out.shape
    padded[...] = jnp.zeros_like(padded)
    padded[:, rows : rows + size, :] = grad[...]

    def one(j, carry):
        start = jnp.clip(strips[j] * rows - row[0], -rows, size) + rows
        base = pl.ds(pl.multiple_of(start // 8 * 8, 8), rows + 8)
        up = lax.rem(rows + 8 - lax.rem(start, 8), rows + 8)
        for k in range(parts):
            out[j, k] = pltpu.roll(padded[k, base, :], up, 0)[:rows]
        return carry

    lax.fori_loop(0, count, one, 0)


def add_kernel(cols, received, out, total):
    count, parts, rows, size = received.shape
    total[...] = jnp.zeros_like(total)
    edge = jnp.zeros((rows, LANES), F32)

    def one(j, carry):
        across = pl.ds(pl.multiple_of(cols[j] // LANES * LANES, LANES), size + LANES)
        shift = lax.rem(cols[j], LANES)
        for k in range(parts):
            piece = jnp.concatenate([received[j, k], edge], axis=1)
            total[k, :, across] += pltpu.roll(piece, shift, 1)
        return carry

    lax.fori_loop(0, count, one, 0)
    out[...] = total[:, :, : out.shape[-1]]


def shards(object_field, probe, amplitude, pos_row, pos_col, strip_of):
    size = probe.shape[-1]
    modes = probe.shape[0]
    rows, cols = object_field.shape[1], object_field.shape[2]
    devices, groups = lax.axis_size("scan"), lax.axis_size("mode")
    padded_cols = cols + LANES
    forward, inverse = dft_tables(size)

    def swap(x):
        return lax.ppermute(x, "mode", [(0, 1), (1, 0)])

    planes, deep = devices // 4, -(-rows // 16) * 16
    fits = groups == 2 and devices == 4 * planes and planes == 4 and size % (64 * HALVES * planes) == 0 and modes * HALVES == 8
    fits = fits and cols % LANES == 0 and size // TILE == 2
    fits = fits and deep - rows >= 8
    fits = fits and 2 * rows % 16 == 0 and size % (2 * LANES) == 0
    if fits and rows % 8 == 0 and devices * deep % TILE == 0 and devices * deep <= 2 * size:
        dma = pltpu.SemaphoreType.DMA
        chunks, chunk = modes * HALVES, size // HALVES
        vmem, lanes = pltpu.VMEM, (cols // LANES + 1) // 2 * LANES
        any_space = pl.BlockSpec(memory_space=pl.ANY)
        term, strip_grad = pl.pallas_call(
            core_kernel,
            out_shape=(vmem((modes, 2, size, size), BF16), vmem((2, rows, cols), F32)),
            in_specs=[SMEM] * 3 + [any_space] * 5,
            out_specs=(VMEM, VMEM),
            scratch_shapes=[
                vmem((rows, cols), F32),
                vmem((devices * deep, lanes), BF16),
                vmem((devices * deep, cols - lanes), BF16),
                vmem((cols, size), BF16),
                vmem((size, planes * deep), BF16),
                vmem((planes * deep, size), BF16),
                vmem((modes, 2, size, size), F32),
                vmem((2, size, size), BF16),
                vmem((size, size), F32),
                vmem((2 * size, 2 * size), BF16),
                vmem((2 * size, 2 * size), BF16),
                vmem((modes, 2, size, size), F32),
                vmem((size, size), F32),
                vmem((size, size), F32),
                vmem((size, size), F32),
                vmem((2 * size, size), BF16),
                vmem((size, 2 * size), BF16),
                vmem((modes, 2, size, size), BF16),
                vmem((chunks, 2, chunk // 2, size), BF16),
                vmem((chunks, 2, chunk // 2, size), BF16),
                vmem((chunks, 2, chunk // 4, size), BF16),
                vmem((chunks, 2, chunk // 4, size), BF16),
                vmem((chunks, 2, chunk // 8, size), BF16),
                vmem((chunks, 2, chunk // 8, size), BF16),
                vmem((chunks, 2, chunk // 16, size), BF16),
                vmem((2, size, size), F32),
                vmem((size, size), F32),
                vmem((size, size), BF16),
                vmem((devices * 2 * rows, size // 2), BF16),
                vmem((devices * 2 * rows, size // 2), BF16),
                dma((4,)),
                dma((modes,)),
                dma((5, 2, planes)),
                dma((5, 2, planes)),
                dma((size // TILE,)),
                dma((size // TILE,)),
                dma((8, chunks, 2)),
                dma((8, chunks, 2)),
                dma((size // TILE,)),
                dma((size // TILE,)),
                dma((devices - 1,)),
                dma((devices - 1,)),
                dma,
                dma,
            ],
            compiler_params=pltpu.CompilerParams(
                vmem_limit_bytes=56 * 1024 * 1024, collective_id=0, has_side_effects=True
            ),
        )(strip_of, pos_row, pos_col, object_field, probe, amplitude[0], forward, inverse)
        probe_grad, strip_grad = pl.pallas_call(
            cast_kernel,
            out_shape=(jax.ShapeDtypeStruct(term.shape, F32), jax.ShapeDtypeStruct(strip_grad.shape, F32)),
            in_specs=[VMEM] * 2,
            out_specs=(any_space, any_space),
            scratch_shapes=[vmem((4, size, size), F32), dma((4,)), dma],
            compiler_params=pltpu.CompilerParams(vmem_limit_bytes=16 * 1024 * 1024),
        )(pltpu.with_memory_space_constraint(term, vmem), pltpu.with_memory_space_constraint(strip_grad, vmem))
        return (strip_grad, probe_grad)

    lane = lax.broadcasted_iota(jnp.int32, (2, META, cols), 2)
    numbers = jnp.where(lane == 0, strip_of[0], jnp.where(lane == 1, pos_col[0] // LANES, pos_col[0] % LANES))
    packed = jnp.concatenate([object_field.astype(BF16), numbers.astype(BF16)], axis=1)
    me = lax.axis_index("mode")
    if groups == 2 and devices % PLANE == 0:
        dma, lines = pltpu.SemaphoreType.DMA, devices // PLANE
        held = pl.pallas_call(
            gather_kernel,
            out_shape=jax.ShapeDtypeStruct((2, devices, rows + META, cols), BF16),
            in_specs=[VMEM],
            out_specs=VMEM,
            scratch_shapes=[
                dma((max(lines - 1, 1),)),
                dma((max(lines - 1, 1),)),
                dma((lines, PLANE - 1)),
                dma((lines, PLANE - 1)),
                dma,
                dma,
            ],
            compiler_params=pltpu.CompilerParams(
                vmem_limit_bytes=56 * 1024 * 1024, collective_id=0, has_side_effects=True
            ),
        )(lax.dynamic_index_in_dim(packed, me, 0, keepdims=False))
    else:
        held = lax.all_gather(packed, "scan", axis=1)
    numbers = held[0, :, rows, :3].astype(jnp.int32)
    strips = numbers[:, 0]
    all_cols = numbers[:, 1] * LANES + numbers[:, 2]

    wave_shape = jax.ShapeDtypeStruct((2, size, size), F32)
    patch = pl.pallas_call(
        cut_kernel,
        out_shape=wave_shape,
        in_specs=[SMEM, SMEM, SMEM, VMEM],
        out_specs=VMEM,
        scratch_shapes=[pltpu.VMEM((2, devices * rows + 8, padded_cols), F32)],
        compiler_params=PARAMS,
    )(strips, pos_row, pos_col, held)

    def whole(*shape):
        return pl.BlockSpec(shape, lambda m: (0,) * len(shape))

    mode_spec = pl.BlockSpec((1, 2, size, size), lambda m: (m, 0, 0, 0))
    table_spec = whole(2 * size, 2 * size)
    buffers = [pltpu.VMEM((2 * size, size), BF16), pltpu.VMEM((size, 2 * size), BF16)]
    far, power = pl.pallas_call(
        forward_kernel,
        grid=(modes,),
        out_shape=(
            jax.ShapeDtypeStruct((modes, 2, size, size), F32),
            jax.ShapeDtypeStruct((size, size), F32),
        ),
        in_specs=[mode_spec, whole(2, size, size), table_spec, table_spec],
        out_specs=(mode_spec, whole(size, size)),
        scratch_shapes=buffers,
        compiler_params=PARAMS,
    )(probe, patch, forward, inverse)
    power = power + swap(power) if groups == 2 else lax.psum(power, "mode")
    term, grad = pl.pallas_call(
        backward_kernel,
        grid=(modes,),
        out_shape=(jax.ShapeDtypeStruct((modes, 2, size, size), BF16), wave_shape),
        in_specs=[
            mode_spec,
            mode_spec,
            whole(2, size, size),
            whole(size, size),
            whole(size, size),
            table_spec,
            table_spec,
        ],
        out_specs=(mode_spec, whole(2, size, size)),
        scratch_shapes=[pltpu.VMEM((size, size), F32)] + buffers,
        compiler_params=PARAMS,
    )(far, probe, patch, amplitude[0], power, inverse, forward)
    probe_grad = lax.psum(term, "scan").astype(F32)

    if groups == 2:
        mine = lax.dynamic_index_in_dim(grad, me, 0, keepdims=True)
        other = lax.dynamic_index_in_dim(grad, 1 - me, 0, keepdims=True)
        grad = mine + swap(other)
    else:
        grad = lax.psum(grad, "mode")
    parts = grad.shape[0]
    pieces = pl.pallas_call(
        place_kernel,
        out_shape=jax.ShapeDtypeStruct((devices, parts, rows, size), F32),
        in_specs=[SMEM, SMEM, VMEM],
        out_specs=VMEM,
        scratch_shapes=[pltpu.VMEM((parts, size + 2 * rows + 8, size), F32)],
        compiler_params=PARAMS,
    )(strips, pos_row, grad)
    received = lax.all_to_all(pieces.astype(BF16), "scan", 0, 0, tiled=False).astype(F32)
    strip_grad = pl.pallas_call(
        add_kernel,
        out_shape=jax.ShapeDtypeStruct((parts, rows, cols), F32),
        in_specs=[SMEM, VMEM],
        out_specs=VMEM,
        scratch_shapes=[pltpu.VMEM((parts, rows, padded_cols), F32)],
        compiler_params=PARAMS,
    )(all_cols, received)
    if groups == 2:
        theirs = swap(strip_grad)
        strip_grad = jnp.where(
            me == 0,
            jnp.concatenate([strip_grad, theirs]),
            jnp.concatenate([theirs, strip_grad]),
        )
    return (strip_grad, probe_grad)


def solution(mesh):
    return jax.shard_map(
        shards,
        mesh=mesh,
        in_specs=(
            P(None, "scan", None),
            P("mode", None, None, None),
            P("scan", None, None),
            P("scan"),
            P("scan"),
            P("scan"),
        ),
        out_specs=(P(None, "scan", None), P("mode", None, None, None)),
        check_vma=False,
    )
```

```python
import math

import jax
import jax.numpy as jnp
import numpy as np
from jax import lax
from jax.experimental import pallas as pl
from jax.experimental.pallas import tpu as pltpu
from jax.sharding import PartitionSpec as P

F32 = jnp.float32
BF16 = jnp.bfloat16
LANES = 128
HALVES = 2
META = 8
PLANE = 4
TILE = 256
ORDER = (
    (0, 0), (0, 1), (0, 2), (0, 3), (1, 0), (1, 1), (0, 4), (1, 2), (0, 5), (2, 1),
    (1, 3), (0, 6), (1, 4), (3, 1), (0, 7), (2, 2), (9, 0), (10, 1), (2, 0), (3, 2),
    (2, 3), (10, 2), (10, 3), (4, 1), (10, 4), (2, 4), (10, 5), (4, 2), (10, 6), (3, 4),
    (10, 7), (1, 7), (5, 1), (1, 5), (3, 0), (10, 8), (3, 3), (5, 2), (1, 6), (2, 7),
    (6, 1), (4, 4), (2, 5), (4, 3), (6, 2), (4, 0), (3, 7), (2, 6), (10, 9), (7, 1),
    (3, 5), (7, 2), (5, 4), (10, 10), (4, 7), (3, 6), (4, 5), (6, 4), (5, 0), (10, 11),
    (5, 7), (5, 3), (10, 12), (4, 6), (7, 4), (5, 5), (6, 0), (6, 7), (10, 13), (5, 6),
    (6, 3), (10, 14), (6, 5), (10, 15), (7, 0), (6, 6), (7, 5), (7, 3), (7, 6), (7, 7),
    (11, 0),
)
PLANES_FIRST = ((3, 0), (3, 1), (0, 1))
PARAMS = pltpu.CompilerParams(vmem_limit_bytes=56 * 1024 * 1024)
VMEM = pl.BlockSpec(memory_space=pltpu.VMEM)
SMEM = pl.BlockSpec(memory_space=pltpu.SMEM)
MESH = pl.DeviceIdType.MESH


def dft_tables(size):
    positions = np.arange(size, dtype=np.int32)
    angles = (positions[:, None] * positions[None, :] % size).astype(np.float32)
    angles = angles * np.float32(2.0 * math.pi / size)
    norm = np.float32(1.0 / math.sqrt(size))
    cosine, sine = np.cos(angles) * norm, np.sin(angles) * norm
    forward = np.block([[cosine, sine], [-sine, cosine]])
    inverse = np.block([[cosine, -sine], [sine, cosine]])
    return jnp.asarray(forward, BF16), jnp.asarray(inverse, BF16)


def gather_kernel(mine, out, line_send, line_recv, plane_send, plane_recv, swap_send, swap_recv):
    count = out.shape[1]
    lines = count // PLANE
    scan, mode = lax.axis_index("scan"), lax.axis_index("mode")
    line, place = scan // PLANE, lax.rem(scan, PLANE)
    in_line = [(lax.rem(line + k, lines) * PLANE + place, mode) for k in range(1, lines)]
    in_plane = [(line * PLANE + lax.rem(place + t, PLANE), mode) for t in range(1, PLANE)]
    partner = (scan, 1 - mode)

    barrier = pltpu.get_barrier_semaphore()
    for peer in in_line + in_plane + [partner]:
        pl.semaphore_signal(barrier, inc=1, device_id=peer, device_id_type=pl.DeviceIdType.MESH)
    pl.semaphore_wait(barrier, len(in_line) + len(in_plane) + 1)

    def push(src, dst, send, recv, peer):
        copy = pltpu.make_async_remote_copy(
            src_ref=src,
            dst_ref=dst,
            send_sem=send,
            recv_sem=recv,
            device_id=peer,
            device_id_type=pl.DeviceIdType.MESH,
        )
        copy.start()
        return copy

    own = out.at[mode, scan]
    line_copies = [
        push(mine, own, line_send.at[k], line_recv.at[k], peer) for k, peer in enumerate(in_line)
    ]
    plane_copies = [
        push(mine, own, plane_send.at[0, t], plane_recv.at[0, t], peer) for t, peer in enumerate(in_plane)
    ]
    out[mode, scan] = mine[...]
    for k, arriving in enumerate(line_copies):
        arriving.wait_recv()
        piece = out.at[mode, lax.rem(line + lines - k - 1, lines) * PLANE + place]
        plane_copies += [
            push(piece, piece, plane_send.at[k + 1, t], plane_recv.at[k + 1, t], peer)
            for t, peer in enumerate(in_plane)
        ]
    for copy in plane_copies:
        copy.wait_recv()
    last = push(out.at[mode], out.at[mode], swap_send, swap_recv, partner)
    for copy in line_copies + plane_copies:
        copy.wait_send()
    last.wait()


def cut_kernel(strips, row, col, held, patch, window):
    count, rows = held.shape[1], held.shape[2] - META
    size, cols = patch.shape[-1], held.shape[-1]
    wide = size + LANES

    def place(j, carry):
        at = pl.ds(pl.multiple_of(strips[j] * rows, 8), rows)
        for c in range(2):
            window[c, at, :cols] = held[c, j].astype(F32)[:rows]
        return carry

    lax.fori_loop(0, count, place, 0)
    across = pl.ds(pl.multiple_of(col[0] // LANES * LANES, LANES), wide)
    back = lax.rem(wide - lax.rem(col[0], LANES), wide)
    up = lax.rem(72 - lax.rem(row[0], 8), 72)
    for c in range(2):

        def cut(i, carry, c=c):
            block = window[c, pl.ds(pl.multiple_of(row[0] // 8 * 8 + i * 64, 8), 72), across]
            block = pltpu.roll(block, up, 0)[:64]
            patch[c, pl.ds(pl.multiple_of(i * 64, 64), 64), :] = pltpu.roll(block, back, 1)[:, :size]
            return carry

        lax.fori_loop(0, size // 64, cut, 0)


def forward_kernel(probe, patch, left, right, far, power, wave, half):
    size = patch.shape[-1]

    def leave(i, carry):
        at = pl.ds(pl.multiple_of(i * 64, 64), 64)
        low = pl.ds(pl.multiple_of(size + i * 64, 64), 64)
        pr, pi, xr, xi = probe[0, 0, at], probe[0, 1, at], patch[0, at], patch[1, at]
        wave[at] = (pr * xr - pi * xi).astype(BF16)
        wave[low] = (pr * xi + pi * xr).astype(BF16)
        return carry

    lax.fori_loop(0, size // 64, leave, 0)
    rows_product(left, wave, half)
    first = pl.program_id(0) == 0

    def across(i, carry):
        at = pl.ds(pl.multiple_of(i * TILE, TILE), TILE)
        both = jnp.dot(half[at], right[...], preferred_element_type=F32)
        re, im = both[:, :size], both[:, size:]
        far[0, 0, at] = re
        far[0, 1, at] = im
        here = re * re + im * im
        power[at] = jnp.where(first, here, power[at] + here)
        return carry

    lax.fori_loop(0, size // TILE, across, 0)


def rows_product(left, wave, half):
    size = wave.shape[-1]
    for c in range(2):

        def down(i, carry, c=c):
            at = pl.ds(pl.multiple_of(c * size + i * TILE, TILE), TILE)
            to = pl.ds(pl.multiple_of(i * TILE, TILE), TILE)
            product = jnp.dot(left[at], wave[...], preferred_element_type=F32)
            half[to, c * size : (c + 1) * size] = product.astype(BF16)
            return carry

        lax.fori_loop(0, size // TILE, down, 0)


def backward_kernel(far, probe, patch, measured, power, left, right, term, grad, scale, wave, half):
    size = patch.shape[-1]
    first = pl.program_id(0) == 0

    @pl.when(first)
    def _():
        total = jnp.maximum(power[...], 0.25)
        scale[...] = 1.0 - measured[...] / jnp.sqrt(total)

    def residual(i, carry):
        at = pl.ds(pl.multiple_of(i * 64, 64), 64)
        low = pl.ds(pl.multiple_of(size + i * 64, 64), 64)
        wave[at] = (far[0, 0, at] * scale[at]).astype(BF16)
        wave[low] = (far[0, 1, at] * scale[at]).astype(BF16)
        return carry

    lax.fori_loop(0, size // 64, residual, 0)
    rows_product(left, wave, half)

    def across(i, carry):
        at = pl.ds(pl.multiple_of(i * TILE, TILE), TILE)
        both = jnp.dot(half[at], right[...], preferred_element_type=F32)
        br, bi = both[:, :size], both[:, size:]
        pr, pi, xr, xi = probe[0, 0, at], probe[0, 1, at], patch[0, at], patch[1, at]
        term[0, 0, at] = (xr * br + xi * bi).astype(BF16)
        term[0, 1, at] = (xr * bi - xi * br).astype(BF16)
        re, im = pr * br + pi * bi, pr * bi - pi * br
        grad[0, at] = jnp.where(first, re, grad[0, at] + re)
        grad[1, at] = jnp.where(first, im, grad[1, at] + im)
        return carry

    lax.fori_loop(0, size // TILE, across, 0)


def mesh_peer(scan, mode, planes, dx, dy, dz):
    z, y, x = scan // 4, lax.rem(scan // 2, 2), lax.rem(scan, 2)
    x, y = lax.rem(x + dx, 2), lax.rem(y + dy, 2)
    return (lax.rem(z + dz, planes) * 4 + y * 2 + x, mode)


def core_kernel(
    strip_of, row, col, field_hbm, probe_hbm, measured_hbm, left_hbm, right_hbm, result, strip_grad,
    field, held_a, held_b, col_hot, row_hot, cut, probe, patch, measured, left, right,
    far, power, power_in, scale, wave, half, term, got1, sum1, got2, sum2, got3, sum3, got4,
    grad, grad_in, summed, pieces, landed,
    load, load_probe, hop_send, hop_recv, swap_send, swap_recv, send, recv,
    part_send, part_recv, piece_send, piece_recv, strip_send, strip_recv,
):
    modes, size = probe.shape[0], patch.shape[-1]
    devices = lax.axis_size("scan")
    strip, width = strip_grad.shape[1], strip_grad.shape[2]
    planes = devices // 4
    scan, mode = lax.axis_index("scan"), lax.axis_index("mode")
    z, y, x = scan // 4, lax.rem(scan // 2, 2), lax.rem(scan, 2)
    partner = (scan, 1 - mode)
    peer_x = mesh_peer(scan, mode, planes, 1, 0, 0)
    peer_y = mesh_peer(scan, mode, planes, 0, 1, 0)
    chunk = size // HALVES
    deep, tall = held_a.shape[0] // devices, pieces.shape[0] // devices

    barrier = pltpu.get_barrier_semaphore()
    levels = (z, z + 1 - 2 * lax.rem(z, 2), z + 2 - 4 * (z // 2), 3 - z)
    plane, plane_x, plane_y = y * 2 + x, y * 2 + 1 - x, (1 - y) * 2 + x
    plane_d = (1 - y) * 2 + 1 - x
    everyone = [partner, peer_x, peer_y] + [(levels[k] * 4 + plane, mode) for k in range(1, planes)]
    for peer in everyone:
        pl.semaphore_signal(barrier, inc=1, device_id=peer, device_id_type=MESH)
    own_load = pltpu.make_async_copy(field_hbm.at[mode], field, load.at[3])
    own_load.start()

    def probe_load(m):
        return pltpu.make_async_copy(probe_hbm.at[m], probe.at[m], load_probe.at[m])

    whole = [(left_hbm, left), (right_hbm, right), (measured_hbm, measured)]
    loads = [pltpu.make_async_copy(src, dst, load.at[i]) for i, (src, dst) in enumerate(whole)]
    probe_load(0).start()
    for copy in loads:
        copy.start()
    for m in range(1, modes):
        probe_load(m).start()

    def rows(start, count, step):
        return pl.ds(pl.multiple_of(start, step), count)

    def one_hot(mask):
        return jnp.where(mask, 1.0, 0.0).astype(BF16)

    held, parts_at = (held_a, held_b), (0, held_a.shape[1], width)

    def strip_rows(side, k):
        return rows((side * planes + levels[k]) * deep, deep, deep)

    which = lax.broadcasted_iota(jnp.int32, (deep - strip, width), 0)
    numbers = jnp.where(which == 1, lax.rem(col[0], LANES), col[0] // LANES)
    numbers = jnp.where(which == 0, strip_of[0], numbers).astype(F32)
    own_load.wait()
    own = jnp.concatenate([field[...], numbers]).astype(BF16)
    for i in range(2):
        held[i][strip_rows(plane, 0)] = own[:, parts_at[i] : parts_at[i + 1]]
    pl.semaphore_wait(barrier, len(everyone))

    def remote(src, dst, send_sem, recv_sem, peer):
        return pltpu.make_async_remote_copy(
            src_ref=src, dst_ref=dst, send_sem=send_sem, recv_sem=recv_sem, device_id=peer, device_id_type=MESH
        )

    def number(slot, which, lanes):
        block = held_a[rows(slot * deep + deep - 16, 16, 16), :lanes].astype(F32)
        at = 16 - (deep - strip) + which
        return block[at : at + 1].astype(jnp.int32)

    def hop(kind, i, k, side, peer):
        at = held[i].at[strip_rows(side, k)]
        return remote(at, at, hop_send.at[kind, i, k], hop_recv.at[kind, i, k], peer)

    def hop_z(i, k):
        at = held[i].at[strip_rows(plane, 0)]
        return remote(at, at, hop_send.at[0, i, k], hop_recv.at[0, i, k], (levels[k] * 4 + plane, mode))

    def spread(k):
        for i in range(2):
            hop(1, i, k, plane, peer_x).start()
            hop(2, 1 - i, k, plane, peer_y).start()

    def relay(k):
        i = 0 if k < planes // 2 else 1
        hop(1, i, k, plane_x, peer_x).wait_recv()
        hop(3, i, k, plane_x, peer_y).start()
        hop(2, 1 - i, k, plane_y, peer_y).wait_recv()
        hop(3, 1 - i, k, plane_y, peer_x).start()

    def absorb(side, first=False, last=False):
        taken = planes * deep
        at = rows(side * taken, taken, taken)
        got = jnp.dot(held_a[at], col_hot[: held_a.shape[1]], preferred_element_type=F32)
        got = got + jnp.dot(held_b[at], col_hot[held_a.shape[1] :], preferred_element_type=F32)
        cut[...] = got.astype(BF16)
        lane = lax.broadcasted_iota(jnp.int32, (1, taken), 1)
        target = jnp.full((1, taken), -1, jnp.int32)
        for j in range(planes):
            ahead = lane - j * deep
            begin = number(side * planes + j, 0, taken) * strip
            target = jnp.where((ahead >= 0) & (ahead < strip), begin + ahead, target)
        target = target - row[0]

        def line_hot(i, carry):
            line = lax.broadcasted_iota(jnp.int32, (64, taken), 0) + i * 64
            row_hot[rows(i * 64, 64, 64)] = one_hot(line == target)
            return carry

        lax.fori_loop(0, size // 64, line_hot, 0)
        for i in range(size // TILE):
            at = pl.ds(i * TILE, TILE)
            piled = jnp.dot(row_hot[at], cut[...], preferred_element_type=F32)
            if not first:
                piled = power[at] + piled
            if last:
                patch[mode, at] = piled.astype(BF16)
                patch_swap(i).start()
            else:
                power[at] = piled

    def patch_swap(i):
        at = rows(i * TILE, TILE, TILE)
        own = patch.at[mode, at]
        return remote(own, own, hop_send.at[4, i, 0], hop_recv.at[4, i, 0], partner)

    def slot_of(j):
        return lax.rem(j, 4) * planes + j // 4

    for k in range(1, planes):
        hop_z(0, k).start()
        hop_z(1, k).start()
    spread(0)

    def column_hot(i, carry):
        at = rows(i * LANES, LANES, LANES)
        lane = lax.broadcasted_iota(jnp.int32, (LANES, size), 1)
        col_hot[at] = one_hot(lax.broadcasted_iota(jnp.int32, (LANES, size), 0) + i * LANES - lane == col[0])
        return carry

    lax.fori_loop(0, width // LANES, column_hot, 0)
    for k in range(1, planes):
        hop(0, 0, k, plane, partner).wait_recv()
        hop(0, 1, k, plane, partner).wait_recv()
        spread(k)
        relay(k - 1)
    relay(planes - 1)
    absorb(plane, first=True)
    for k in range(planes):
        hop(1, int(k < planes // 2), k, plane_x, peer_x).wait_recv()
    absorb(plane_x)
    for k in range(planes):
        hop(2, int(k >= planes // 2), k, plane_y, peer_y).wait_recv()
    absorb(plane_y)
    for k in range(planes):
        hop(3, 0, k, plane_d, peer_y).wait_recv()
        hop(3, 1, k, plane_d, peer_x).wait_recv()
    absorb(plane_d, last=True)
    for copy in loads:
        copy.wait()
    for i in range(size // TILE):
        patch_swap(i).wait_recv()

    def place(u):
        return u // HALVES, u % HALVES * chunk

    near, far_z = levels[1] * 4 + plane, levels[2] * 4 + plane
    along = {"x": (peer_x, x), "y": (peer_y, y), "n": ((near, mode), lax.rem(z, 2)), "f": ((far_z, mode), z // 2)}
    sums, gots = (None, sum1, sum2, sum3), (None, got1, got2, got3, got4)

    def way(u, c, stage):
        axes = ("nfxy", "nfyx")[c] if (u, c) in PLANES_FIRST else ("xynf", "yxnf")[c]
        return along[axes[stage - 1]]

    def base(u, c, stage):
        low = place(u)[1]
        for s in range(1, stage + 1):
            low = low + way(u, c, s)[1] * (chunk >> s)
        return low

    def exchange(u, c, stage):
        m, low = place(u)
        if stage > 4:
            stage = 9 - stage
            count = chunk >> stage
            own = result.at[m, c, rows(base(u, c, stage), count, count)]
            peer, stage = way(u, c, stage)[0], 9 - stage
            return remote(own, own, send.at[stage - 1, u, c], recv.at[stage - 1, u, c], peer)
        peer, bit = way(u, c, stage)
        count = chunk >> stage
        away = (1 - bit) * count
        src = term.at[m, c, rows(low + away, count, count)] if stage == 1 else sums[stage - 1].at[u, c, rows(away, count, count)]
        return remote(src, gots[stage].at[u, c], send.at[stage - 1, u, c], recv.at[stage - 1, u, c], peer)

    def start(stage, u):
        for c in range(2):
            exchange(u, c, stage).start()

    def finish(stage, u):
        m, low = place(u)
        for c in range(2):
            exchange(u, c, stage).wait_recv()
            if stage > 4:
                continue
            count, bit = chunk >> stage, way(u, c, stage)[1]
            if stage == 1:
                mine = term[m, c, rows(low + bit * count, count, count)]
            else:
                mine = sums[stage - 1][u, c, rows(bit * count, count, count)]
            total = (mine.astype(F32) + gots[stage][u, c].astype(F32)).astype(BF16)
            if stage == 4:
                result[m, c, rows(base(u, c, 4), count, count)] = total
            else:
                sums[stage][u, c] = total

    def swap(i):
        at = rows(i * TILE, TILE, TILE)
        return remote(power.at[at], power_in.at[at], swap_send.at[i], swap_recv.at[i], partner)

    def product(table, source):
        out = jnp.dot(table[...], source[...], preferred_element_type=F32)
        half[:, :size] = out[:size].astype(BF16)
        half[:, size:] = out[size:].astype(BF16)

    def part(i):
        at = rows(i * TILE, TILE, TILE)
        return remote(grad.at[1 - mode, at], grad_in.at[at], part_send.at[i], part_recv.at[i], partner)

    mine = rows(scan * tall, tall, 16)

    def piece(k):
        to = lax.rem(scan + k, devices)
        return remote(pieces.at[rows(to * tall, tall, 16)], landed.at[mine], piece_send.at[k - 1], piece_recv.at[k - 1], (to, mode))

    def arrive(k):
        come = lax.rem(scan + devices - k, devices)
        at = rows(come * tall, tall, 16)
        return remote(pieces.at[at], landed.at[at], piece_send.at[k - 1], piece_recv.at[k - 1], (come, mode))

    def strip_swap():
        return remote(strip_grad.at[mode], strip_grad.at[mode], strip_send, strip_recv, partner)

    def cut_pieces():
        for i in range(size // TILE):
            part(i).wait_recv()
            at = pl.ds(i * TILE, TILE)
            summed[at] = (grad[mode, at] + grad_in[at]).astype(BF16)
        down = lax.broadcasted_iota(jnp.int32, (tall, size), 0)
        ahead = lax.broadcasted_iota(jnp.int32, (tall, size), 1) - jnp.where(down < strip, down, down - strip)

        def pick(i, carry):
            begins = [number(slot_of(2 * i + j), 0, size) * strip - row[0] for j in range(2)]
            wave[rows(i * tall, tall, 16)] = one_hot(ahead == jnp.where(down < strip, begins[0], begins[1]))
            return carry

        lax.fori_loop(0, devices // 2, pick, 0)

        def move(i, carry):
            out = jnp.dot(wave[rows(i * 4 * tall, 4 * tall, 16)], summed[...], preferred_element_type=F32)
            for j in range(8):
                block = out[j * strip : (j + 1) * strip]
                block = jnp.concatenate([block[:, : size // 2], block[:, size // 2 :]])
                pieces[rows((i * 8 + j) * tall, tall, 16)] = block.astype(BF16)
            return carry

        lax.fori_loop(0, devices // 8, move, 0)
        landed[mine] = pieces[mine]

    def add_pieces():
        for k in range(1, devices):
            arrive(k).wait_recv()
        strip_grad[mode] = jnp.zeros((strip, width), F32)
        parts = size // LANES
        ahead = lax.broadcasted_iota(jnp.int32, (LANES, 2 * LANES), 1)
        ahead = ahead - lax.broadcasted_iota(jnp.int32, (LANES, 2 * LANES), 0)

        def one(j, carry):
            turn, whole_lanes = one_hot(ahead == number(slot_of(j), 1, 2 * LANES)), number(slot_of(j), 2, LANES)
            piece_rows = landed[rows(j * tall, tall, 16)].astype(F32)
            blocks = jnp.concatenate(
                [
                    piece_rows[b * strip : (b + 1) * strip, at * LANES : (at + 1) * LANES]
                    for b in range(2)
                    for at in range(parts // 2)
                ]
            ).astype(BF16)
            moved = jnp.dot(blocks, turn, preferred_element_type=F32)
            for b in range(parts + 1):
                here = moved[b * strip : (b + 1) * strip, :LANES] if b < parts else 0.0
                if b > 0:
                    here = here + moved[(b - 1) * strip : b * strip, LANES:]
                for t in range((width - size) // LANES + 1):
                    if b + t < width // LANES:
                        to = slice((b + t) * LANES, (b + t + 1) * LANES)
                        strip_grad[mode, :, to] += jnp.where(whole_lanes == t, here, 0.0)
            return carry

        lax.fori_loop(0, devices, one, 0)
        strip_swap().start()

    def leave(m, at, low):
        pr, pi, xr, xi = probe[m, 0, at], probe[m, 1, at], patch[0, at].astype(F32), patch[1, at].astype(F32)
        wave[at] = (pr * xr - pi * xi).astype(BF16)
        wave[low] = (pr * xi + pi * xr).astype(BF16)

    def forward(m, carry):
        @pl.when(m < modes - 1)
        def _():
            probe_load(m + 1).wait()

        product(left, wave)
        after = jnp.minimum(m + 1, modes - 1)

        def across(i, carry):
            at = rows(i * TILE, TILE, TILE)
            leave(after, at, rows(size + i * TILE, TILE, TILE))
            both = jnp.dot(half[at], right[...], preferred_element_type=F32)
            re, im = both[:, :size], both[:, size:]
            far[m, 0, at] = re
            far[m, 1, at] = im
            here = re * re + im * im
            power[at] = jnp.where(m == 0, here, power[at] + here)

            @pl.when(m == modes - 1)
            def _():
                swap(i).start()

            return carry

        lax.fori_loop(0, size // TILE, across, 0)
        return carry

    def first_leave(i, carry):
        leave(0, rows(i * 64, 64, 64), rows(size + i * 64, 64, 64))
        return carry

    probe_load(0).wait()
    lax.fori_loop(0, size // 64, first_leave, 0)
    lax.fori_loop(0, modes, forward, 0)
    for i in range(size // TILE):
        at = pl.ds(i * TILE, TILE)
        swap(i).wait_recv()
        total = jnp.maximum(power[at] + power_in[at], 0.25)
        scale[at] = 1.0 - measured[at] / jnp.sqrt(total)

    def residual(m, at, low):
        wave[at] = (far[m, 0, at] * scale[at]).astype(BF16)
        wave[low] = (far[m, 1, at] * scale[at]).astype(BF16)

    def backward(m):
        if m == 0:

            def first_residual(i, carry):
                residual(0, rows(i * 64, 64, 64), rows(size + i * 64, 64, 64))
                return carry

            lax.fori_loop(0, size // 64, first_residual, 0)
        product(right, wave)

    def across_back(m, i):
        at = pl.ds(i * TILE, TILE)
        if m < modes - 1:
            residual(m + 1, at, pl.ds(size + i * TILE, TILE))
        both = jnp.dot(half[at], left[...], preferred_element_type=F32)
        br, bi = both[:, :size], both[:, size:]
        pr, pi, xr, xi = probe[m, 0, at], probe[m, 1, at], patch[0, at].astype(F32), patch[1, at].astype(F32)
        term[m, 0, at] = (xr * br + xi * bi).astype(BF16)
        term[m, 1, at] = (xr * bi - xi * br).astype(BF16)
        re, im = pr * br + pi * bi, pr * bi - pi * br
        grad[0, at] = re if m == 0 else grad[0, at] + re
        grad[1, at] = im if m == 0 else grad[1, at] + im
        if m == modes - 1:
            part(i).start()

    for step, u in ORDER:
        if step == 0:
            if u % HALVES == 0:
                backward(u // HALVES)
            across_back(u // HALVES, u % HALVES)
            start(1, u)
        elif step < 8:
            finish(step, u)
            start(step + 1, u)
        elif step == 9:
            cut_pieces()
        elif step == 10:
            piece(u).start()
        else:
            add_pieces()

    for u in range(modes * HALVES):
        finish(8, u)
        for c in range(2):
            for stage in range(1, 9):
                exchange(u, c, stage).wait_send()
    for i in range(size // TILE):
        swap(i).wait_send()
        part(i).wait_send()
    for k in range(1, devices):
        piece(k).wait_send()
    strip_swap().wait()
    for i in range(size // TILE):
        patch_swap(i).wait_send()
    for i in range(2):
        for k in range(planes):
            if k:
                hop_z(i, k).wait_send()
            hop(1, i, k, plane, peer_x).wait_send()
            hop(2, i, k, plane, peer_y).wait_send()
            swapped = i if k < planes // 2 else 1 - i
            hop(3, i, k, (plane_x, plane_y)[swapped], (peer_y, peer_x)[swapped]).wait_send()


def cast_kernel(summed, strips, wide, strip_grad, block, done, strip_done):
    modes, depth = summed.shape[0], block.shape[0]
    last = pltpu.make_async_copy(strips, strip_grad, strip_done)
    last.start()

    def out(i):
        return pltpu.make_async_copy(block.at[i % depth], wide.at[i // 2, i % 2], done.at[i % depth])

    for i in range(2 * modes):
        if i >= depth:
            out(i - depth).wait()
        block[i % depth] = summed[i // 2, i % 2].astype(F32)
        out(i).start()
    for i in range(max(2 * modes - depth, 0), 2 * modes):
        out(i).wait()
    last.wait()


def place_kernel(strips, row, grad, out, padded):
    count, parts, rows, size = out.shape
    padded[...] = jnp.zeros_like(padded)
    padded[:, rows : rows + size, :] = grad[...]

    def one(j, carry):
        start = jnp.clip(strips[j] * rows - row[0], -rows, size) + rows
        base = pl.ds(pl.multiple_of(start // 8 * 8, 8), rows + 8)
        up = lax.rem(rows + 8 - lax.rem(start, 8), rows + 8)
        for k in range(parts):
            out[j, k] = pltpu.roll(padded[k, base, :], up, 0)[:rows]
        return carry

    lax.fori_loop(0, count, one, 0)


def add_kernel(cols, received, out, total):
    count, parts, rows, size = received.shape
    total[...] = jnp.zeros_like(total)
    edge = jnp.zeros((rows, LANES), F32)

    def one(j, carry):
        across = pl.ds(pl.multiple_of(cols[j] // LANES * LANES, LANES), size + LANES)
        shift = lax.rem(cols[j], LANES)
        for k in range(parts):
            piece = jnp.concatenate([received[j, k], edge], axis=1)
            total[k, :, across] += pltpu.roll(piece, shift, 1)
        return carry

    lax.fori_loop(0, count, one, 0)
    out[...] = total[:, :, : out.shape[-1]]


def shards(object_field, probe, amplitude, pos_row, pos_col, strip_of):
    size = probe.shape[-1]
    modes = probe.shape[0]
    rows, cols = object_field.shape[1], object_field.shape[2]
    devices, groups = lax.axis_size("scan"), lax.axis_size("mode")
    padded_cols = cols + LANES
    forward, inverse = dft_tables(size)

    def swap(x):
        return lax.ppermute(x, "mode", [(0, 1), (1, 0)])

    planes, deep = devices // 4, -(-rows // 16) * 16
    fits = groups == 2 and devices == 4 * planes and planes == 4 and size % (64 * HALVES * planes) == 0 and modes * HALVES == 8
    fits = fits and cols % LANES == 0 and size // TILE == 2
    fits = fits and deep - rows >= 8
    fits = fits and 2 * rows % 16 == 0 and size % (2 * LANES) == 0
    if fits and rows % 8 == 0 and devices * deep % TILE == 0 and devices * deep <= 2 * size:
        dma = pltpu.SemaphoreType.DMA
        chunks, chunk = modes * HALVES, size // HALVES
        vmem, lanes = pltpu.VMEM, (cols // LANES + 1) // 2 * LANES
        any_space = pl.BlockSpec(memory_space=pl.ANY)
        term, strip_grad = pl.pallas_call(
            core_kernel,
            out_shape=(vmem((modes, 2, size, size), BF16), vmem((2, rows, cols), F32)),
            in_specs=[SMEM] * 3 + [any_space] * 5,
            out_specs=(VMEM, VMEM),
            scratch_shapes=[
                vmem((rows, cols), F32),
                vmem((devices * deep, lanes), BF16),
                vmem((devices * deep, cols - lanes), BF16),
                vmem((cols, size), BF16),
                vmem((size, planes * deep), BF16),
                vmem((planes * deep, size), BF16),
                vmem((modes, 2, size, size), F32),
                vmem((2, size, size), BF16),
                vmem((size, size), F32),
                vmem((2 * size, 2 * size), BF16),
                vmem((2 * size, 2 * size), BF16),
                vmem((modes, 2, size, size), F32),
                vmem((size, size), F32),
                vmem((size, size), F32),
                vmem((size, size), F32),
                vmem((2 * size, size), BF16),
                vmem((size, 2 * size), BF16),
                vmem((modes, 2, size, size), BF16),
                vmem((chunks, 2, chunk // 2, size), BF16),
                vmem((chunks, 2, chunk // 2, size), BF16),
                vmem((chunks, 2, chunk // 4, size), BF16),
                vmem((chunks, 2, chunk // 4, size), BF16),
                vmem((chunks, 2, chunk // 8, size), BF16),
                vmem((chunks, 2, chunk // 8, size), BF16),
                vmem((chunks, 2, chunk // 16, size), BF16),
                vmem((2, size, size), F32),
                vmem((size, size), F32),
                vmem((size, size), BF16),
                vmem((devices * 2 * rows, size // 2), BF16),
                vmem((devices * 2 * rows, size // 2), BF16),
                dma((4,)),
                dma((modes,)),
                dma((5, 2, planes)),
                dma((5, 2, planes)),
                dma((size // TILE,)),
                dma((size // TILE,)),
                dma((8, chunks, 2)),
                dma((8, chunks, 2)),
                dma((size // TILE,)),
                dma((size // TILE,)),
                dma((devices - 1,)),
                dma((devices - 1,)),
                dma,
                dma,
            ],
            compiler_params=pltpu.CompilerParams(
                vmem_limit_bytes=56 * 1024 * 1024, collective_id=0, has_side_effects=True
            ),
        )(strip_of, pos_row, pos_col, object_field, probe, amplitude[0], forward, inverse)
        probe_grad, strip_grad = pl.pallas_call(
            cast_kernel,
            out_shape=(jax.ShapeDtypeStruct(term.shape, F32), jax.ShapeDtypeStruct(strip_grad.shape, F32)),
            in_specs=[VMEM] * 2,
            out_specs=(any_space, any_space),
            scratch_shapes=[vmem((4, size, size), F32), dma((4,)), dma],
            compiler_params=pltpu.CompilerParams(vmem_limit_bytes=16 * 1024 * 1024),
        )(pltpu.with_memory_space_constraint(term, vmem), pltpu.with_memory_space_constraint(strip_grad, vmem))
        return (strip_grad, probe_grad)

    lane = lax.broadcasted_iota(jnp.int32, (2, META, cols), 2)
    numbers = jnp.where(lane == 0, strip_of[0], jnp.where(lane == 1, pos_col[0] // LANES, pos_col[0] % LANES))
    packed = jnp.concatenate([object_field.astype(BF16), numbers.astype(BF16)], axis=1)
    me = lax.axis_index("mode")
    if groups == 2 and devices % PLANE == 0:
        dma, lines = pltpu.SemaphoreType.DMA, devices // PLANE
        held = pl.pallas_call(
            gather_kernel,
            out_shape=jax.ShapeDtypeStruct((2, devices, rows + META, cols), BF16),
            in_specs=[VMEM],
            out_specs=VMEM,
            scratch_shapes=[
                dma((max(lines - 1, 1),)),
                dma((max(lines - 1, 1),)),
                dma((lines, PLANE - 1)),
                dma((lines, PLANE - 1)),
                dma,
                dma,
            ],
            compiler_params=pltpu.CompilerParams(
                vmem_limit_bytes=56 * 1024 * 1024, collective_id=0, has_side_effects=True
            ),
        )(lax.dynamic_index_in_dim(packed, me, 0, keepdims=False))
    else:
        held = lax.all_gather(packed, "scan", axis=1)
    numbers = held[0, :, rows, :3].astype(jnp.int32)
    strips = numbers[:, 0]
    all_cols = numbers[:, 1] * LANES + numbers[:, 2]

    wave_shape = jax.ShapeDtypeStruct((2, size, size), F32)
    patch = pl.pallas_call(
        cut_kernel,
        out_shape=wave_shape,
        in_specs=[SMEM, SMEM, SMEM, VMEM],
        out_specs=VMEM,
        scratch_shapes=[pltpu.VMEM((2, devices * rows + 8, padded_cols), F32)],
        compiler_params=PARAMS,
    )(strips, pos_row, pos_col, held)

    def whole(*shape):
        return pl.BlockSpec(shape, lambda m: (0,) * len(shape))

    mode_spec = pl.BlockSpec((1, 2, size, size), lambda m: (m, 0, 0, 0))
    table_spec = whole(2 * size, 2 * size)
    buffers = [pltpu.VMEM((2 * size, size), BF16), pltpu.VMEM((size, 2 * size), BF16)]
    far, power = pl.pallas_call(
        forward_kernel,
        grid=(modes,),
        out_shape=(
            jax.ShapeDtypeStruct((modes, 2, size, size), F32),
            jax.ShapeDtypeStruct((size, size), F32),
        ),
        in_specs=[mode_spec, whole(2, size, size), table_spec, table_spec],
        out_specs=(mode_spec, whole(size, size)),
        scratch_shapes=buffers,
        compiler_params=PARAMS,
    )(probe, patch, forward, inverse)
    power = power + swap(power) if groups == 2 else lax.psum(power, "mode")
    term, grad = pl.pallas_call(
        backward_kernel,
        grid=(modes,),
        out_shape=(jax.ShapeDtypeStruct((modes, 2, size, size), BF16), wave_shape),
        in_specs=[
            mode_spec,
            mode_spec,
            whole(2, size, size),
            whole(size, size),
            whole(size, size),
            table_spec,
            table_spec,
        ],
        out_specs=(mode_spec, whole(2, size, size)),
        scratch_shapes=[pltpu.VMEM((size, size), F32)] + buffers,
        compiler_params=PARAMS,
    )(far, probe, patch, amplitude[0], power, inverse, forward)
    probe_grad = lax.psum(term, "scan").astype(F32)

    if groups == 2:
        mine = lax.dynamic_index_in_dim(grad, me, 0, keepdims=True)
        other = lax.dynamic_index_in_dim(grad, 1 - me, 0, keepdims=True)
        grad = mine + swap(other)
    else:
        grad = lax.psum(grad, "mode")
    parts = grad.shape[0]
    pieces = pl.pallas_call(
        place_kernel,
        out_shape=jax.ShapeDtypeStruct((devices, parts, rows, size), F32),
        in_specs=[SMEM, SMEM, VMEM],
        out_specs=VMEM,
        scratch_shapes=[pltpu.VMEM((parts, size + 2 * rows + 8, size), F32)],
        compiler_params=PARAMS,
    )(strips, pos_row, grad)
    received = lax.all_to_all(pieces.astype(BF16), "scan", 0, 0, tiled=False).astype(F32)
    strip_grad = pl.pallas_call(
        add_kernel,
        out_shape=jax.ShapeDtypeStruct((parts, rows, cols), F32),
        in_specs=[SMEM, VMEM],
        out_specs=VMEM,
        scratch_shapes=[pltpu.VMEM((parts, rows, padded_cols), F32)],
        compiler_params=PARAMS,
    )(all_cols, received)
    if groups == 2:
        theirs = swap(strip_grad)
        strip_grad = jnp.where(
            me == 0,
            jnp.concatenate([strip_grad, theirs]),
            jnp.concatenate([theirs, strip_grad]),
        )
    return (strip_grad, probe_grad)


def solution(mesh):
    return jax.shard_map(
        shards,
        mesh=mesh,
        in_specs=(
            P(None, "scan", None),
            P("mode", None, None, None),
            P("scan", None, None),
            P("scan"),
            P("scan"),
            P("scan"),
        ),
        out_specs=(P(None, "scan", None), P("mode", None, None, None)),
        check_vma=False,
    )
```

```python
import math

import jax
import jax.numpy as jnp
import numpy as np
from jax import lax
from jax.experimental import pallas as pl
from jax.experimental.pallas import tpu as pltpu
from jax.sharding import PartitionSpec as P

F32 = jnp.float32
BF16 = jnp.bfloat16
LANES = 128
HALVES = 2
META = 8
PLANE = 4
TILE = 256
ORDER = (
    (0, 0), (0, 1), (0, 2), (0, 3), (0, 4), (1, 0), (1, 1), (1, 3), (0, 5), (1, 2),
    (0, 6), (1, 4), (2, 1), (0, 7), (2, 3), (2, 0), (9, 0), (10, 1), (3, 1), (3, 3),
    (1, 5), (10, 2), (10, 3), (10, 4), (2, 4), (4, 1), (4, 3), (10, 5), (3, 4), (3, 0),
    (2, 2), (10, 6), (1, 6), (2, 5), (5, 1), (1, 7), (5, 3), (3, 2), (3, 5), (10, 7),
    (10, 8), (6, 1), (10, 9), (6, 3), (2, 7), (4, 5), (2, 6), (4, 0), (4, 2), (4, 4),
    (7, 1), (5, 2), (3, 7), (5, 5), (7, 3), (3, 6), (10, 10), (5, 4), (10, 11), (4, 7),
    (6, 5), (5, 0), (4, 6), (10, 12), (10, 13), (6, 4), (7, 5), (6, 0), (5, 6), (7, 4),
    (5, 7), (6, 2), (10, 14), (10, 15), (6, 6), (6, 7), (7, 0), (7, 2), (7, 6), (7, 7),
    (11, 0),
)
PLANES_FIRST = ((2, 0), (2, 1), (0, 1))
PARAMS = pltpu.CompilerParams(vmem_limit_bytes=56 * 1024 * 1024)
VMEM = pl.BlockSpec(memory_space=pltpu.VMEM)
SMEM = pl.BlockSpec(memory_space=pltpu.SMEM)
MESH = pl.DeviceIdType.MESH


def dft_tables(size):
    positions = np.arange(size, dtype=np.int32)
    angles = (positions[:, None] * positions[None, :] % size).astype(np.float32)
    angles = angles * np.float32(2.0 * math.pi / size)
    norm = np.float32(1.0 / math.sqrt(size))
    cosine, sine = np.cos(angles) * norm, np.sin(angles) * norm
    forward = np.block([[cosine, sine], [-sine, cosine]])
    inverse = np.block([[cosine, -sine], [sine, cosine]])
    return jnp.asarray(forward, BF16), jnp.asarray(inverse, BF16)


def gather_kernel(mine, out, line_send, line_recv, plane_send, plane_recv, swap_send, swap_recv):
    count = out.shape[1]
    lines = count // PLANE
    scan, mode = lax.axis_index("scan"), lax.axis_index("mode")
    line, place = scan // PLANE, lax.rem(scan, PLANE)
    in_line = [(lax.rem(line + k, lines) * PLANE + place, mode) for k in range(1, lines)]
    in_plane = [(line * PLANE + lax.rem(place + t, PLANE), mode) for t in range(1, PLANE)]
    partner = (scan, 1 - mode)

    barrier = pltpu.get_barrier_semaphore()
    for peer in in_line + in_plane + [partner]:
        pl.semaphore_signal(barrier, inc=1, device_id=peer, device_id_type=pl.DeviceIdType.MESH)
    pl.semaphore_wait(barrier, len(in_line) + len(in_plane) + 1)

    def push(src, dst, send, recv, peer):
        copy = pltpu.make_async_remote_copy(
            src_ref=src,
            dst_ref=dst,
            send_sem=send,
            recv_sem=recv,
            device_id=peer,
            device_id_type=pl.DeviceIdType.MESH,
        )
        copy.start()
        return copy

    own = out.at[mode, scan]
    line_copies = [
        push(mine, own, line_send.at[k], line_recv.at[k], peer) for k, peer in enumerate(in_line)
    ]
    plane_copies = [
        push(mine, own, plane_send.at[0, t], plane_recv.at[0, t], peer) for t, peer in enumerate(in_plane)
    ]
    out[mode, scan] = mine[...]
    for k, arriving in enumerate(line_copies):
        arriving.wait_recv()
        piece = out.at[mode, lax.rem(line + lines - k - 1, lines) * PLANE + place]
        plane_copies += [
            push(piece, piece, plane_send.at[k + 1, t], plane_recv.at[k + 1, t], peer)
            for t, peer in enumerate(in_plane)
        ]
    for copy in plane_copies:
        copy.wait_recv()
    last = push(out.at[mode], out.at[mode], swap_send, swap_recv, partner)
    for copy in line_copies + plane_copies:
        copy.wait_send()
    last.wait()


def cut_kernel(strips, row, col, held, patch, window):
    count, rows = held.shape[1], held.shape[2] - META
    size, cols = patch.shape[-1], held.shape[-1]
    wide = size + LANES

    def place(j, carry):
        at = pl.ds(pl.multiple_of(strips[j] * rows, 8), rows)
        for c in range(2):
            window[c, at, :cols] = held[c, j].astype(F32)[:rows]
        return carry

    lax.fori_loop(0, count, place, 0)
    across = pl.ds(pl.multiple_of(col[0] // LANES * LANES, LANES), wide)
    back = lax.rem(wide - lax.rem(col[0], LANES), wide)
    up = lax.rem(72 - lax.rem(row[0], 8), 72)
    for c in range(2):

        def cut(i, carry, c=c):
            block = window[c, pl.ds(pl.multiple_of(row[0] // 8 * 8 + i * 64, 8), 72), across]
            block = pltpu.roll(block, up, 0)[:64]
            patch[c, pl.ds(pl.multiple_of(i * 64, 64), 64), :] = pltpu.roll(block, back, 1)[:, :size]
            return carry

        lax.fori_loop(0, size // 64, cut, 0)


def forward_kernel(probe, patch, left, right, far, power, wave, half):
    size = patch.shape[-1]

    def leave(i, carry):
        at = pl.ds(pl.multiple_of(i * 64, 64), 64)
        low = pl.ds(pl.multiple_of(size + i * 64, 64), 64)
        pr, pi, xr, xi = probe[0, 0, at], probe[0, 1, at], patch[0, at], patch[1, at]
        wave[at] = (pr * xr - pi * xi).astype(BF16)
        wave[low] = (pr * xi + pi * xr).astype(BF16)
        return carry

    lax.fori_loop(0, size // 64, leave, 0)
    rows_product(left, wave, half)
    first = pl.program_id(0) == 0

    def across(i, carry):
        at = pl.ds(pl.multiple_of(i * TILE, TILE), TILE)
        both = jnp.dot(half[at], right[...], preferred_element_type=F32)
        re, im = both[:, :size], both[:, size:]
        far[0, 0, at] = re
        far[0, 1, at] = im
        here = re * re + im * im
        power[at] = jnp.where(first, here, power[at] + here)
        return carry

    lax.fori_loop(0, size // TILE, across, 0)


def rows_product(left, wave, half):
    size = wave.shape[-1]
    for c in range(2):

        def down(i, carry, c=c):
            at = pl.ds(pl.multiple_of(c * size + i * TILE, TILE), TILE)
            to = pl.ds(pl.multiple_of(i * TILE, TILE), TILE)
            product = jnp.dot(left[at], wave[...], preferred_element_type=F32)
            half[to, c * size : (c + 1) * size] = product.astype(BF16)
            return carry

        lax.fori_loop(0, size // TILE, down, 0)


def backward_kernel(far, probe, patch, measured, power, left, right, term, grad, scale, wave, half):
    size = patch.shape[-1]
    first = pl.program_id(0) == 0

    @pl.when(first)
    def _():
        total = jnp.maximum(power[...], 0.25)
        scale[...] = 1.0 - measured[...] / jnp.sqrt(total)

    def residual(i, carry):
        at = pl.ds(pl.multiple_of(i * 64, 64), 64)
        low = pl.ds(pl.multiple_of(size + i * 64, 64), 64)
        wave[at] = (far[0, 0, at] * scale[at]).astype(BF16)
        wave[low] = (far[0, 1, at] * scale[at]).astype(BF16)
        return carry

    lax.fori_loop(0, size // 64, residual, 0)
    rows_product(left, wave, half)

    def across(i, carry):
        at = pl.ds(pl.multiple_of(i * TILE, TILE), TILE)
        both = jnp.dot(half[at], right[...], preferred_element_type=F32)
        br, bi = both[:, :size], both[:, size:]
        pr, pi, xr, xi = probe[0, 0, at], probe[0, 1, at], patch[0, at], patch[1, at]
        term[0, 0, at] = (xr * br + xi * bi).astype(BF16)
        term[0, 1, at] = (xr * bi - xi * br).astype(BF16)
        re, im = pr * br + pi * bi, pr * bi - pi * br
        grad[0, at] = jnp.where(first, re, grad[0, at] + re)
        grad[1, at] = jnp.where(first, im, grad[1, at] + im)
        return carry

    lax.fori_loop(0, size // TILE, across, 0)


def mesh_peer(scan, mode, planes, dx, dy, dz):
    z, y, x = scan // 4, lax.rem(scan // 2, 2), lax.rem(scan, 2)
    x, y = lax.rem(x + dx, 2), lax.rem(y + dy, 2)
    return (lax.rem(z + dz, planes) * 4 + y * 2 + x, mode)


def core_kernel(
    strip_of, row, col, field_hbm, probe_hbm, measured_hbm, left_hbm, right_hbm, result, strip_grad,
    field, held_a, held_b, col_hot, row_hot, cut, probe, patch, measured, left, right,
    far, power, power_in, scale, wave, half, term, got1, sum1, got2, sum2, got3, sum3, got4,
    grad, grad_in, summed, pieces, landed,
    load, load_probe, hop_send, hop_recv, swap_send, swap_recv, send, recv,
    part_send, part_recv, piece_send, piece_recv, strip_send, strip_recv,
):
    modes, size = probe.shape[0], patch.shape[-1]
    devices = lax.axis_size("scan")
    strip, width = strip_grad.shape[1], strip_grad.shape[2]
    planes = devices // 4
    scan, mode = lax.axis_index("scan"), lax.axis_index("mode")
    z, y, x = scan // 4, lax.rem(scan // 2, 2), lax.rem(scan, 2)
    partner = (scan, 1 - mode)
    peer_x = mesh_peer(scan, mode, planes, 1, 0, 0)
    peer_y = mesh_peer(scan, mode, planes, 0, 1, 0)
    chunk = size // HALVES
    deep, tall = held_a.shape[0] // devices, pieces.shape[0] // devices

    barrier = pltpu.get_barrier_semaphore()
    levels = (z, z + 1 - 2 * lax.rem(z, 2), z + 2 - 4 * (z // 2), 3 - z)
    plane, plane_x, plane_y = y * 2 + x, y * 2 + 1 - x, (1 - y) * 2 + x
    plane_d = (1 - y) * 2 + 1 - x
    everyone = [partner, peer_x, peer_y] + [(levels[k] * 4 + plane, mode) for k in range(1, planes)]
    for peer in everyone:
        pl.semaphore_signal(barrier, inc=1, device_id=peer, device_id_type=MESH)
    own_load = pltpu.make_async_copy(field_hbm.at[mode], field, load.at[3])
    own_load.start()

    def probe_load(m):
        return pltpu.make_async_copy(probe_hbm.at[m], probe.at[m], load_probe.at[m])

    whole = [(left_hbm, left), (right_hbm, right), (measured_hbm, measured)]
    loads = [pltpu.make_async_copy(src, dst, load.at[i]) for i, (src, dst) in enumerate(whole)]
    probe_load(0).start()
    for copy in loads:
        copy.start()
    for m in range(1, modes):
        probe_load(m).start()

    def rows(start, count, step):
        return pl.ds(pl.multiple_of(start, step), count)

    def one_hot(mask):
        return jnp.where(mask, 1.0, 0.0).astype(BF16)

    held, parts_at = (held_a, held_b), (0, held_a.shape[1], width)

    def strip_rows(side, k):
        return rows((side * planes + levels[k]) * deep, deep, deep)

    which = lax.broadcasted_iota(jnp.int32, (deep - strip, width), 0)
    numbers = jnp.where(which == 1, lax.rem(col[0], LANES), col[0] // LANES)
    numbers = jnp.where(which == 0, strip_of[0], numbers).astype(F32)
    own_load.wait()
    own = jnp.concatenate([field[...], numbers]).astype(BF16)
    for i in range(2):
        held[i][strip_rows(plane, 0)] = own[:, parts_at[i] : parts_at[i + 1]]
    pl.semaphore_wait(barrier, len(everyone))

    def remote(src, dst, send_sem, recv_sem, peer):
        return pltpu.make_async_remote_copy(
            src_ref=src, dst_ref=dst, send_sem=send_sem, recv_sem=recv_sem, device_id=peer, device_id_type=MESH
        )

    def number(slot, which, lanes):
        block = held_a[rows(slot * deep + deep - 16, 16, 16), :lanes].astype(F32)
        at = 16 - (deep - strip) + which
        return block[at : at + 1].astype(jnp.int32)

    def hop(kind, i, k, side, peer):
        at = held[i].at[strip_rows(side, k)]
        return remote(at, at, hop_send.at[kind, i, k], hop_recv.at[kind, i, k], peer)

    def hop_z(i, k):
        at = held[i].at[strip_rows(plane, 0)]
        return remote(at, at, hop_send.at[0, i, k], hop_recv.at[0, i, k], (levels[k] * 4 + plane, mode))

    def spread(k):
        for i in range(2):
            hop(1, i, k, plane, peer_x).start()
            hop(2, 1 - i, k, plane, peer_y).start()

    def relay(k):
        hop(1, 0, k, plane_x, peer_x).wait_recv()
        hop(3, 0, k, plane_x, peer_y).start()
        hop(2, 1, k, plane_y, peer_y).wait_recv()
        hop(3, 1, k, plane_y, peer_x).start()

    def absorb(side, first=False, last=False):
        taken = planes * deep
        at = rows(side * taken, taken, taken)
        got = jnp.dot(held_a[at], col_hot[: held_a.shape[1]], preferred_element_type=F32)
        got = got + jnp.dot(held_b[at], col_hot[held_a.shape[1] :], preferred_element_type=F32)
        cut[...] = got.astype(BF16)
        lane = lax.broadcasted_iota(jnp.int32, (1, taken), 1)
        target = jnp.full((1, taken), -1, jnp.int32)
        for j in range(planes):
            ahead = lane - j * deep
            begin = number(side * planes + j, 0, taken) * strip
            target = jnp.where((ahead >= 0) & (ahead < strip), begin + ahead, target)
        target = target - row[0]

        def line_hot(i, carry):
            line = lax.broadcasted_iota(jnp.int32, (64, taken), 0) + i * 64
            row_hot[rows(i * 64, 64, 64)] = one_hot(line == target)
            return carry

        lax.fori_loop(0, size // 64, line_hot, 0)
        for i in range(size // TILE):
            at = pl.ds(i * TILE, TILE)
            piled = jnp.dot(row_hot[at], cut[...], preferred_element_type=F32)
            if not first:
                piled = power[at] + piled
            if last:
                patch[mode, at] = piled.astype(BF16)
                patch_swap(i).start()
            else:
                power[at] = piled

    def patch_swap(i):
        at = rows(i * TILE, TILE, TILE)
        own = patch.at[mode, at]
        return remote(own, own, hop_send.at[4, i, 0], hop_recv.at[4, i, 0], partner)

    def slot_of(j):
        return lax.rem(j, 4) * planes + j // 4

    for k in range(1, planes):
        hop_z(0, k).start()
        hop_z(1, k).start()
    spread(0)

    def column_hot(i, carry):
        at = rows(i * LANES, LANES, LANES)
        lane = lax.broadcasted_iota(jnp.int32, (LANES, size), 1)
        col_hot[at] = one_hot(lax.broadcasted_iota(jnp.int32, (LANES, size), 0) + i * LANES - lane == col[0])
        return carry

    lax.fori_loop(0, width // LANES, column_hot, 0)
    for k in range(1, planes):
        hop(0, 0, k, plane, partner).wait_recv()
        hop(0, 1, k, plane, partner).wait_recv()
        spread(k)
        relay(k - 1)
    relay(planes - 1)
    absorb(plane, first=True)
    for k in range(planes):
        hop(1, 1, k, plane_x, peer_x).wait_recv()
    absorb(plane_x)
    for k in range(planes):
        hop(2, 0, k, plane_y, peer_y).wait_recv()
    absorb(plane_y)
    for k in range(planes):
        hop(3, 0, k, plane_d, peer_y).wait_recv()
        hop(3, 1, k, plane_d, peer_x).wait_recv()
    absorb(plane_d, last=True)
    for copy in loads:
        copy.wait()
    for i in range(size // TILE):
        patch_swap(i).wait_recv()

    def place(u):
        return u // HALVES, u % HALVES * chunk

    near, far_z = levels[1] * 4 + plane, levels[2] * 4 + plane
    along = {"x": (peer_x, x), "y": (peer_y, y), "n": ((near, mode), lax.rem(z, 2)), "f": ((far_z, mode), z // 2)}
    sums, gots = (None, sum1, sum2, sum3), (None, got1, got2, got3, got4)

    def way(u, c, stage):
        axes = ("nfxy", "nfyx")[c] if (u, c) in PLANES_FIRST else ("xynf", "yxnf")[c]
        return along[axes[stage - 1]]

    def base(u, c, stage):
        low = place(u)[1]
        for s in range(1, stage + 1):
            low = low + way(u, c, s)[1] * (chunk >> s)
        return low

    def exchange(u, c, stage):
        m, low = place(u)
        if stage > 4:
            stage = 9 - stage
            count = chunk >> stage
            own = result.at[m, c, rows(base(u, c, stage), count, count)]
            peer, stage = way(u, c, stage)[0], 9 - stage
            return remote(own, own, send.at[stage - 1, u, c], recv.at[stage - 1, u, c], peer)
        peer, bit = way(u, c, stage)
        count = chunk >> stage
        away = (1 - bit) * count
        src = term.at[m, c, rows(low + away, count, count)] if stage == 1 else sums[stage - 1].at[u, c, rows(away, count, count)]
        return remote(src, gots[stage].at[u, c], send.at[stage - 1, u, c], recv.at[stage - 1, u, c], peer)

    def start(stage, u):
        for c in range(2):
            exchange(u, c, stage).start()

    def finish(stage, u):
        m, low = place(u)
        for c in range(2):
            exchange(u, c, stage).wait_recv()
            if stage > 4:
                continue
            count, bit = chunk >> stage, way(u, c, stage)[1]
            if stage == 1:
                mine = term[m, c, rows(low + bit * count, count, count)]
            else:
                mine = sums[stage - 1][u, c, rows(bit * count, count, count)]
            total = (mine.astype(F32) + gots[stage][u, c].astype(F32)).astype(BF16)
            if stage == 4:
                result[m, c, rows(base(u, c, 4), count, count)] = total
            else:
                sums[stage][u, c] = total

    def swap(i):
        at = rows(i * TILE, TILE, TILE)
        return remote(power.at[at], power_in.at[at], swap_send.at[i], swap_recv.at[i], partner)

    def product(table, source):
        out = jnp.dot(table[...], source[...], preferred_element_type=F32)
        half[:, :size] = out[:size].astype(BF16)
        half[:, size:] = out[size:].astype(BF16)

    def part(i):
        at = rows(i * TILE, TILE, TILE)
        return remote(grad.at[1 - mode, at], grad_in.at[at], part_send.at[i], part_recv.at[i], partner)

    mine = rows(scan * tall, tall, 16)

    def piece(k):
        to = lax.rem(scan + k, devices)
        return remote(pieces.at[rows(to * tall, tall, 16)], landed.at[mine], piece_send.at[k - 1], piece_recv.at[k - 1], (to, mode))

    def arrive(k):
        come = lax.rem(scan + devices - k, devices)
        at = rows(come * tall, tall, 16)
        return remote(pieces.at[at], landed.at[at], piece_send.at[k - 1], piece_recv.at[k - 1], (come, mode))

    def strip_swap():
        return remote(strip_grad.at[mode], strip_grad.at[mode], strip_send, strip_recv, partner)

    def cut_pieces():
        for i in range(size // TILE):
            part(i).wait_recv()
            at = pl.ds(i * TILE, TILE)
            summed[at] = (grad[mode, at] + grad_in[at]).astype(BF16)
        down = lax.broadcasted_iota(jnp.int32, (tall, size), 0)
        ahead = lax.broadcasted_iota(jnp.int32, (tall, size), 1) - jnp.where(down < strip, down, down - strip)

        def pick(i, carry):
            begins = [number(slot_of(2 * i + j), 0, size) * strip - row[0] for j in range(2)]
            wave[rows(i * tall, tall, 16)] = one_hot(ahead == jnp.where(down < strip, begins[0], begins[1]))
            return carry

        lax.fori_loop(0, devices // 2, pick, 0)

        def move(i, carry):
            out = jnp.dot(wave[rows(i * 4 * tall, 4 * tall, 16)], summed[...], preferred_element_type=F32)
            for j in range(8):
                block = out[j * strip : (j + 1) * strip]
                block = jnp.concatenate([block[:, : size // 2], block[:, size // 2 :]])
                pieces[rows((i * 8 + j) * tall, tall, 16)] = block.astype(BF16)
            return carry

        lax.fori_loop(0, devices // 8, move, 0)
        landed[mine] = pieces[mine]

    def add_pieces():
        for k in range(1, devices):
            arrive(k).wait_recv()
        strip_grad[mode] = jnp.zeros((strip, width), F32)
        parts = size // LANES
        ahead = lax.broadcasted_iota(jnp.int32, (LANES, 2 * LANES), 1)
        ahead = ahead - lax.broadcasted_iota(jnp.int32, (LANES, 2 * LANES), 0)

        def one(j, carry):
            turn, whole_lanes = one_hot(ahead == number(slot_of(j), 1, 2 * LANES)), number(slot_of(j), 2, LANES)
            piece_rows = landed[rows(j * tall, tall, 16)].astype(F32)
            blocks = jnp.concatenate(
                [
                    piece_rows[b * strip : (b + 1) * strip, at * LANES : (at + 1) * LANES]
                    for b in range(2)
                    for at in range(parts // 2)
                ]
            ).astype(BF16)
            moved = jnp.dot(blocks, turn, preferred_element_type=F32)
            for b in range(parts + 1):
                here = moved[b * strip : (b + 1) * strip, :LANES] if b < parts else 0.0
                if b > 0:
                    here = here + moved[(b - 1) * strip : b * strip, LANES:]
                for t in range((width - size) // LANES + 1):
                    if b + t < width // LANES:
                        to = slice((b + t) * LANES, (b + t + 1) * LANES)
                        strip_grad[mode, :, to] += jnp.where(whole_lanes == t, here, 0.0)
            return carry

        lax.fori_loop(0, devices, one, 0)
        strip_swap().start()

    def forward(m, carry, tile=size):
        probe_load(m).wait()

        def leave(i, carry):
            at, low = rows(i * 64, 64, 64), rows(size + i * 64, 64, 64)
            pr, pi, xr, xi = probe[m, 0, at], probe[m, 1, at], patch[0, at].astype(F32), patch[1, at].astype(F32)
            wave[at] = (pr * xr - pi * xi).astype(BF16)
            wave[low] = (pr * xi + pi * xr).astype(BF16)
            return carry

        lax.fori_loop(0, size // 64, leave, 0)
        product(left, wave)

        for i in range(size // tile):
            at = pl.ds(i * tile, tile)
            both = jnp.dot(half[at], right[...], preferred_element_type=F32)
            re, im = both[:, :size], both[:, size:]
            far[m, 0, at] = re
            far[m, 1, at] = im
            here = re * re + im * im
            power[at] = jnp.where(m == 0, here, power[at] + here)
            if tile == TILE:
                swap(i).start()
        return carry

    lax.fori_loop(0, modes - 1, forward, 0)
    forward(modes - 1, 0, TILE)
    for i in range(size // TILE):
        at = pl.ds(i * TILE, TILE)
        swap(i).wait_recv()
        total = jnp.maximum(power[at] + power_in[at], 0.25)
        scale[at] = 1.0 - measured[at] / jnp.sqrt(total)

    def backward(m):
        def residual(i, carry):
            at, low = rows(i * 64, 64, 64), rows(size + i * 64, 64, 64)
            wave[at] = (far[m, 0, at] * scale[at]).astype(BF16)
            wave[low] = (far[m, 1, at] * scale[at]).astype(BF16)
            return carry

        lax.fori_loop(0, size // 64, residual, 0)
        product(right, wave)

    def across_back(m, i):
        at = pl.ds(i * TILE, TILE)
        both = jnp.dot(half[at], left[...], preferred_element_type=F32)
        br, bi = both[:, :size], both[:, size:]
        pr, pi, xr, xi = probe[m, 0, at], probe[m, 1, at], patch[0, at].astype(F32), patch[1, at].astype(F32)
        term[m, 0, at] = (xr * br + xi * bi).astype(BF16)
        term[m, 1, at] = (xr * bi - xi * br).astype(BF16)
        re, im = pr * br + pi * bi, pr * bi - pi * br
        grad[0, at] = re if m == 0 else grad[0, at] + re
        grad[1, at] = im if m == 0 else grad[1, at] + im
        if m == modes - 1:
            part(i).start()

    for step, u in ORDER:
        if step == 0:
            if u % HALVES == 0:
                backward(u // HALVES)
            across_back(u // HALVES, u % HALVES)
            start(1, u)
        elif step < 8:
            finish(step, u)
            start(step + 1, u)
        elif step == 9:
            cut_pieces()
        elif step == 10:
            piece(u).start()
        else:
            add_pieces()

    for u in range(modes * HALVES):
        finish(8, u)
        for c in range(2):
            for stage in range(1, 9):
                exchange(u, c, stage).wait_send()
    for i in range(size // TILE):
        swap(i).wait_send()
        part(i).wait_send()
    for k in range(1, devices):
        piece(k).wait_send()
    strip_swap().wait()
    for i in range(size // TILE):
        patch_swap(i).wait_send()
    for i in range(2):
        for k in range(planes):
            if k:
                hop_z(i, k).wait_send()
            hop(1, i, k, plane, peer_x).wait_send()
            hop(2, i, k, plane, peer_y).wait_send()
            hop(3, i, k, (plane_x, plane_y)[i], (peer_y, peer_x)[i]).wait_send()


def cast_kernel(summed, strips, wide, strip_grad, block, done, strip_done):
    modes, depth = summed.shape[0], block.shape[0]
    last = pltpu.make_async_copy(strips, strip_grad, strip_done)
    last.start()

    def out(i):
        return pltpu.make_async_copy(block.at[i % depth], wide.at[i // 2, i % 2], done.at[i % depth])

    for i in range(2 * modes):
        if i >= depth:
            out(i - depth).wait()
        block[i % depth] = summed[i // 2, i % 2].astype(F32)
        out(i).start()
    for i in range(max(2 * modes - depth, 0), 2 * modes):
        out(i).wait()
    last.wait()


def place_kernel(strips, row, grad, out, padded):
    count, parts, rows, size = out.shape
    padded[...] = jnp.zeros_like(padded)
    padded[:, rows : rows + size, :] = grad[...]

    def one(j, carry):
        start = jnp.clip(strips[j] * rows - row[0], -rows, size) + rows
        base = pl.ds(pl.multiple_of(start // 8 * 8, 8), rows + 8)
        up = lax.rem(rows + 8 - lax.rem(start, 8), rows + 8)
        for k in range(parts):
            out[j, k] = pltpu.roll(padded[k, base, :], up, 0)[:rows]
        return carry

    lax.fori_loop(0, count, one, 0)


def add_kernel(cols, received, out, total):
    count, parts, rows, size = received.shape
    total[...] = jnp.zeros_like(total)
    edge = jnp.zeros((rows, LANES), F32)

    def one(j, carry):
        across = pl.ds(pl.multiple_of(cols[j] // LANES * LANES, LANES), size + LANES)
        shift = lax.rem(cols[j], LANES)
        for k in range(parts):
            piece = jnp.concatenate([received[j, k], edge], axis=1)
            total[k, :, across] += pltpu.roll(piece, shift, 1)
        return carry

    lax.fori_loop(0, count, one, 0)
    out[...] = total[:, :, : out.shape[-1]]


def shards(object_field, probe, amplitude, pos_row, pos_col, strip_of):
    size = probe.shape[-1]
    modes = probe.shape[0]
    rows, cols = object_field.shape[1], object_field.shape[2]
    devices, groups = lax.axis_size("scan"), lax.axis_size("mode")
    padded_cols = cols + LANES
    forward, inverse = dft_tables(size)

    def swap(x):
        return lax.ppermute(x, "mode", [(0, 1), (1, 0)])

    planes, deep = devices // 4, -(-rows // 16) * 16
    fits = groups == 2 and devices == 4 * planes and planes == 4 and size % (64 * HALVES * planes) == 0 and modes * HALVES == 8
    fits = fits and cols % LANES == 0 and size // TILE == 2
    fits = fits and deep - rows >= 8
    fits = fits and 2 * rows % 16 == 0 and size % (2 * LANES) == 0
    if fits and rows % 8 == 0 and devices * deep % TILE == 0 and devices * deep <= 2 * size:
        dma = pltpu.SemaphoreType.DMA
        chunks, chunk = modes * HALVES, size // HALVES
        vmem, lanes = pltpu.VMEM, (cols // LANES + 1) // 2 * LANES
        any_space = pl.BlockSpec(memory_space=pl.ANY)
        term, strip_grad = pl.pallas_call(
            core_kernel,
            out_shape=(vmem((modes, 2, size, size), BF16), vmem((2, rows, cols), F32)),
            in_specs=[SMEM] * 3 + [any_space] * 5,
            out_specs=(VMEM, VMEM),
            scratch_shapes=[
                vmem((rows, cols), F32),
                vmem((devices * deep, lanes), BF16),
                vmem((devices * deep, cols - lanes), BF16),
                vmem((cols, size), BF16),
                vmem((size, planes * deep), BF16),
                vmem((planes * deep, size), BF16),
                vmem((modes, 2, size, size), F32),
                vmem((2, size, size), BF16),
                vmem((size, size), F32),
                vmem((2 * size, 2 * size), BF16),
                vmem((2 * size, 2 * size), BF16),
                vmem((modes, 2, size, size), F32),
                vmem((size, size), F32),
                vmem((size, size), F32),
                vmem((size, size), F32),
                vmem((2 * size, size), BF16),
                vmem((size, 2 * size), BF16),
                vmem((modes, 2, size, size), BF16),
                vmem((chunks, 2, chunk // 2, size), BF16),
                vmem((chunks, 2, chunk // 2, size), BF16),
                vmem((chunks, 2, chunk // 4, size), BF16),
                vmem((chunks, 2, chunk // 4, size), BF16),
                vmem((chunks, 2, chunk // 8, size), BF16),
                vmem((chunks, 2, chunk // 8, size), BF16),
                vmem((chunks, 2, chunk // 16, size), BF16),
                vmem((2, size, size), F32),
                vmem((size, size), F32),
                vmem((size, size), BF16),
                vmem((devices * 2 * rows, size // 2), BF16),
                vmem((devices * 2 * rows, size // 2), BF16),
                dma((4,)),
                dma((modes,)),
                dma((5, 2, planes)),
                dma((5, 2, planes)),
                dma((size // TILE,)),
                dma((size // TILE,)),
                dma((8, chunks, 2)),
                dma((8, chunks, 2)),
                dma((size // TILE,)),
                dma((size // TILE,)),
                dma((devices - 1,)),
                dma((devices - 1,)),
                dma,
                dma,
            ],
            compiler_params=pltpu.CompilerParams(
                vmem_limit_bytes=56 * 1024 * 1024, collective_id=0, has_side_effects=True
            ),
        )(strip_of, pos_row, pos_col, object_field, probe, amplitude[0], forward, inverse)
        probe_grad, strip_grad = pl.pallas_call(
            cast_kernel,
            out_shape=(jax.ShapeDtypeStruct(term.shape, F32), jax.ShapeDtypeStruct(strip_grad.shape, F32)),
            in_specs=[VMEM] * 2,
            out_specs=(any_space, any_space),
            scratch_shapes=[vmem((4, size, size), F32), dma((4,)), dma],
            compiler_params=pltpu.CompilerParams(vmem_limit_bytes=16 * 1024 * 1024),
        )(pltpu.with_memory_space_constraint(term, vmem), pltpu.with_memory_space_constraint(strip_grad, vmem))
        return (strip_grad, probe_grad)

    lane = lax.broadcasted_iota(jnp.int32, (2, META, cols), 2)
    numbers = jnp.where(lane == 0, strip_of[0], jnp.where(lane == 1, pos_col[0] // LANES, pos_col[0] % LANES))
    packed = jnp.concatenate([object_field.astype(BF16), numbers.astype(BF16)], axis=1)
    me = lax.axis_index("mode")
    if groups == 2 and devices % PLANE == 0:
        dma, lines = pltpu.SemaphoreType.DMA, devices // PLANE
        held = pl.pallas_call(
            gather_kernel,
            out_shape=jax.ShapeDtypeStruct((2, devices, rows + META, cols), BF16),
            in_specs=[VMEM],
            out_specs=VMEM,
            scratch_shapes=[
                dma((max(lines - 1, 1),)),
                dma((max(lines - 1, 1),)),
                dma((lines, PLANE - 1)),
                dma((lines, PLANE - 1)),
                dma,
                dma,
            ],
            compiler_params=pltpu.CompilerParams(
                vmem_limit_bytes=56 * 1024 * 1024, collective_id=0, has_side_effects=True
            ),
        )(lax.dynamic_index_in_dim(packed, me, 0, keepdims=False))
    else:
        held = lax.all_gather(packed, "scan", axis=1)
    numbers = held[0, :, rows, :3].astype(jnp.int32)
    strips = numbers[:, 0]
    all_cols = numbers[:, 1] * LANES + numbers[:, 2]

    wave_shape = jax.ShapeDtypeStruct((2, size, size), F32)
    patch = pl.pallas_call(
        cut_kernel,
        out_shape=wave_shape,
        in_specs=[SMEM, SMEM, SMEM, VMEM],
        out_specs=VMEM,
        scratch_shapes=[pltpu.VMEM((2, devices * rows + 8, padded_cols), F32)],
        compiler_params=PARAMS,
    )(strips, pos_row, pos_col, held)

    def whole(*shape):
        return pl.BlockSpec(shape, lambda m: (0,) * len(shape))

    mode_spec = pl.BlockSpec((1, 2, size, size), lambda m: (m, 0, 0, 0))
    table_spec = whole(2 * size, 2 * size)
    buffers = [pltpu.VMEM((2 * size, size), BF16), pltpu.VMEM((size, 2 * size), BF16)]
    far, power = pl.pallas_call(
        forward_kernel,
        grid=(modes,),
        out_shape=(
            jax.ShapeDtypeStruct((modes, 2, size, size), F32),
            jax.ShapeDtypeStruct((size, size), F32),
        ),
        in_specs=[mode_spec, whole(2, size, size), table_spec, table_spec],
        out_specs=(mode_spec, whole(size, size)),
        scratch_shapes=buffers,
        compiler_params=PARAMS,
    )(probe, patch, forward, inverse)
    power = power + swap(power) if groups == 2 else lax.psum(power, "mode")
    term, grad = pl.pallas_call(
        backward_kernel,
        grid=(modes,),
        out_shape=(jax.ShapeDtypeStruct((modes, 2, size, size), BF16), wave_shape),
        in_specs=[
            mode_spec,
            mode_spec,
            whole(2, size, size),
            whole(size, size),
            whole(size, size),
            table_spec,
            table_spec,
        ],
        out_specs=(mode_spec, whole(2, size, size)),
        scratch_shapes=[pltpu.VMEM((size, size), F32)] + buffers,
        compiler_params=PARAMS,
    )(far, probe, patch, amplitude[0], power, inverse, forward)
    probe_grad = lax.psum(term, "scan").astype(F32)

    if groups == 2:
        mine = lax.dynamic_index_in_dim(grad, me, 0, keepdims=True)
        other = lax.dynamic_index_in_dim(grad, 1 - me, 0, keepdims=True)
        grad = mine + swap(other)
    else:
        grad = lax.psum(grad, "mode")
    parts = grad.shape[0]
    pieces = pl.pallas_call(
        place_kernel,
        out_shape=jax.ShapeDtypeStruct((devices, parts, rows, size), F32),
        in_specs=[SMEM, SMEM, VMEM],
        out_specs=VMEM,
        scratch_shapes=[pltpu.VMEM((parts, size + 2 * rows + 8, size), F32)],
        compiler_params=PARAMS,
    )(strips, pos_row, grad)
    received = lax.all_to_all(pieces.astype(BF16), "scan", 0, 0, tiled=False).astype(F32)
    strip_grad = pl.pallas_call(
        add_kernel,
        out_shape=jax.ShapeDtypeStruct((parts, rows, cols), F32),
        in_specs=[SMEM, VMEM],
        out_specs=VMEM,
        scratch_shapes=[pltpu.VMEM((parts, rows, padded_cols), F32)],
        compiler_params=PARAMS,
    )(all_cols, received)
    if groups == 2:
        theirs = swap(strip_grad)
        strip_grad = jnp.where(
            me == 0,
            jnp.concatenate([strip_grad, theirs]),
            jnp.concatenate([theirs, strip_grad]),
        )
    return (strip_grad, probe_grad)


def solution(mesh):
    return jax.shard_map(
        shards,
        mesh=mesh,
        in_specs=(
            P(None, "scan", None),
            P("mode", None, None, None),
            P("scan", None, None),
            P("scan"),
            P("scan"),
            P("scan"),
        ),
        out_specs=(P(None, "scan", None), P("mode", None, None, None)),
        check_vma=False,
    )
```

```python
import math

import jax
import jax.numpy as jnp
import numpy as np
from jax import lax
from jax.experimental import pallas as pl
from jax.experimental.pallas import tpu as pltpu
from jax.sharding import PartitionSpec as P

F32 = jnp.float32
BF16 = jnp.bfloat16
LANES = 128
HALVES = 2
META = 8
PLANE = 4
TILE = 256
ORDER = (
    (0, 0), (0, 1), (0, 2), (0, 3), (0, 4), (1, 0), (1, 1), (1, 3), (0, 5), (1, 2),
    (0, 6), (1, 4), (2, 1), (0, 7), (2, 3), (2, 0), (9, 0), (10, 1), (3, 1), (3, 3),
    (1, 5), (10, 2), (10, 3), (10, 4), (2, 4), (4, 1), (4, 3), (10, 5), (3, 4), (3, 0),
    (2, 2), (10, 6), (1, 6), (2, 5), (5, 1), (1, 7), (5, 3), (3, 2), (3, 5), (10, 7),
    (10, 8), (6, 1), (10, 9), (6, 3), (2, 7), (4, 5), (2, 6), (4, 0), (4, 2), (4, 4),
    (7, 1), (5, 2), (3, 7), (5, 5), (7, 3), (3, 6), (10, 10), (5, 4), (10, 11), (4, 7),
    (6, 5), (5, 0), (4, 6), (10, 12), (10, 13), (6, 4), (7, 5), (6, 0), (5, 6), (7, 4),
    (5, 7), (6, 2), (10, 14), (10, 15), (6, 6), (6, 7), (7, 0), (7, 2), (7, 6), (7, 7),
    (11, 0),
)
PLANES_FIRST = ((2, 0), (2, 1), (0, 1))
PARAMS = pltpu.CompilerParams(vmem_limit_bytes=56 * 1024 * 1024)
VMEM = pl.BlockSpec(memory_space=pltpu.VMEM)
SMEM = pl.BlockSpec(memory_space=pltpu.SMEM)
MESH = pl.DeviceIdType.MESH


def dft_tables(size):
    positions = np.arange(size, dtype=np.int32)
    angles = (positions[:, None] * positions[None, :] % size).astype(np.float32)
    angles = angles * np.float32(2.0 * math.pi / size)
    norm = np.float32(1.0 / math.sqrt(size))
    cosine, sine = np.cos(angles) * norm, np.sin(angles) * norm
    forward = np.block([[cosine, sine], [-sine, cosine]])
    inverse = np.block([[cosine, -sine], [sine, cosine]])
    return jnp.asarray(forward, BF16), jnp.asarray(inverse, BF16)


def gather_kernel(mine, out, line_send, line_recv, plane_send, plane_recv, swap_send, swap_recv):
    count = out.shape[1]
    lines = count // PLANE
    scan, mode = lax.axis_index("scan"), lax.axis_index("mode")
    line, place = scan // PLANE, lax.rem(scan, PLANE)
    in_line = [(lax.rem(line + k, lines) * PLANE + place, mode) for k in range(1, lines)]
    in_plane = [(line * PLANE + lax.rem(place + t, PLANE), mode) for t in range(1, PLANE)]
    partner = (scan, 1 - mode)

    barrier = pltpu.get_barrier_semaphore()
    for peer in in_line + in_plane + [partner]:
        pl.semaphore_signal(barrier, inc=1, device_id=peer, device_id_type=pl.DeviceIdType.MESH)
    pl.semaphore_wait(barrier, len(in_line) + len(in_plane) + 1)

    def push(src, dst, send, recv, peer):
        copy = pltpu.make_async_remote_copy(
            src_ref=src,
            dst_ref=dst,
            send_sem=send,
            recv_sem=recv,
            device_id=peer,
            device_id_type=pl.DeviceIdType.MESH,
        )
        copy.start()
        return copy

    own = out.at[mode, scan]
    line_copies = [
        push(mine, own, line_send.at[k], line_recv.at[k], peer) for k, peer in enumerate(in_line)
    ]
    plane_copies = [
        push(mine, own, plane_send.at[0, t], plane_recv.at[0, t], peer) for t, peer in enumerate(in_plane)
    ]
    out[mode, scan] = mine[...]
    for k, arriving in enumerate(line_copies):
        arriving.wait_recv()
        piece = out.at[mode, lax.rem(line + lines - k - 1, lines) * PLANE + place]
        plane_copies += [
            push(piece, piece, plane_send.at[k + 1, t], plane_recv.at[k + 1, t], peer)
            for t, peer in enumerate(in_plane)
        ]
    for copy in plane_copies:
        copy.wait_recv()
    last = push(out.at[mode], out.at[mode], swap_send, swap_recv, partner)
    for copy in line_copies + plane_copies:
        copy.wait_send()
    last.wait()


def cut_kernel(strips, row, col, held, patch, window):
    count, rows = held.shape[1], held.shape[2] - META
    size, cols = patch.shape[-1], held.shape[-1]
    wide = size + LANES

    def place(j, carry):
        at = pl.ds(pl.multiple_of(strips[j] * rows, 8), rows)
        for c in range(2):
            window[c, at, :cols] = held[c, j].astype(F32)[:rows]
        return carry

    lax.fori_loop(0, count, place, 0)
    across = pl.ds(pl.multiple_of(col[0] // LANES * LANES, LANES), wide)
    back = lax.rem(wide - lax.rem(col[0], LANES), wide)
    up = lax.rem(72 - lax.rem(row[0], 8), 72)
    for c in range(2):

        def cut(i, carry, c=c):
            block = window[c, pl.ds(pl.multiple_of(row[0] // 8 * 8 + i * 64, 8), 72), across]
            block = pltpu.roll(block, up, 0)[:64]
            patch[c, pl.ds(pl.multiple_of(i * 64, 64), 64), :] = pltpu.roll(block, back, 1)[:, :size]
            return carry

        lax.fori_loop(0, size // 64, cut, 0)


def forward_kernel(probe, patch, left, right, far, power, wave, half):
    size = patch.shape[-1]

    def leave(i, carry):
        at = pl.ds(pl.multiple_of(i * 64, 64), 64)
        low = pl.ds(pl.multiple_of(size + i * 64, 64), 64)
        pr, pi, xr, xi = probe[0, 0, at], probe[0, 1, at], patch[0, at], patch[1, at]
        wave[at] = (pr * xr - pi * xi).astype(BF16)
        wave[low] = (pr * xi + pi * xr).astype(BF16)
        return carry

    lax.fori_loop(0, size // 64, leave, 0)
    rows_product(left, wave, half)
    first = pl.program_id(0) == 0

    def across(i, carry):
        at = pl.ds(pl.multiple_of(i * TILE, TILE), TILE)
        both = jnp.dot(half[at], right[...], preferred_element_type=F32)
        re, im = both[:, :size], both[:, size:]
        far[0, 0, at] = re
        far[0, 1, at] = im
        here = re * re + im * im
        power[at] = jnp.where(first, here, power[at] + here)
        return carry

    lax.fori_loop(0, size // TILE, across, 0)


def rows_product(left, wave, half):
    size = wave.shape[-1]
    for c in range(2):

        def down(i, carry, c=c):
            at = pl.ds(pl.multiple_of(c * size + i * TILE, TILE), TILE)
            to = pl.ds(pl.multiple_of(i * TILE, TILE), TILE)
            product = jnp.dot(left[at], wave[...], preferred_element_type=F32)
            half[to, c * size : (c + 1) * size] = product.astype(BF16)
            return carry

        lax.fori_loop(0, size // TILE, down, 0)


def backward_kernel(far, probe, patch, measured, power, left, right, term, grad, scale, wave, half):
    size = patch.shape[-1]
    first = pl.program_id(0) == 0

    @pl.when(first)
    def _():
        total = jnp.maximum(power[...], 0.25)
        scale[...] = 1.0 - measured[...] / jnp.sqrt(total)

    def residual(i, carry):
        at = pl.ds(pl.multiple_of(i * 64, 64), 64)
        low = pl.ds(pl.multiple_of(size + i * 64, 64), 64)
        wave[at] = (far[0, 0, at] * scale[at]).astype(BF16)
        wave[low] = (far[0, 1, at] * scale[at]).astype(BF16)
        return carry

    lax.fori_loop(0, size // 64, residual, 0)
    rows_product(left, wave, half)

    def across(i, carry):
        at = pl.ds(pl.multiple_of(i * TILE, TILE), TILE)
        both = jnp.dot(half[at], right[...], preferred_element_type=F32)
        br, bi = both[:, :size], both[:, size:]
        pr, pi, xr, xi = probe[0, 0, at], probe[0, 1, at], patch[0, at], patch[1, at]
        term[0, 0, at] = (xr * br + xi * bi).astype(BF16)
        term[0, 1, at] = (xr * bi - xi * br).astype(BF16)
        re, im = pr * br + pi * bi, pr * bi - pi * br
        grad[0, at] = jnp.where(first, re, grad[0, at] + re)
        grad[1, at] = jnp.where(first, im, grad[1, at] + im)
        return carry

    lax.fori_loop(0, size // TILE, across, 0)


def mesh_peer(scan, mode, planes, dx, dy, dz):
    z, y, x = scan // 4, lax.rem(scan // 2, 2), lax.rem(scan, 2)
    x, y = lax.rem(x + dx, 2), lax.rem(y + dy, 2)
    return (lax.rem(z + dz, planes) * 4 + y * 2 + x, mode)


def core_kernel(
    strip_of, row, col, field_hbm, probe_hbm, measured_hbm, left_hbm, right_hbm, result, strip_grad,
    field, held_a, held_b, col_hot, row_hot, cut, probe, patch, measured, left, right,
    far, power, power_in, scale, wave, half, term, got1, sum1, got2, sum2, got3, sum3, got4,
    grad, grad_in, summed, pieces, landed,
    load, load_probe, hop_send, hop_recv, swap_send, swap_recv, send, recv,
    part_send, part_recv, piece_send, piece_recv, strip_send, strip_recv,
):
    modes, size = probe.shape[0], patch.shape[-1]
    devices = lax.axis_size("scan")
    strip, width = strip_grad.shape[1], strip_grad.shape[2]
    planes = devices // 4
    scan, mode = lax.axis_index("scan"), lax.axis_index("mode")
    z, y, x = scan // 4, lax.rem(scan // 2, 2), lax.rem(scan, 2)
    partner = (scan, 1 - mode)
    peer_x = mesh_peer(scan, mode, planes, 1, 0, 0)
    peer_y = mesh_peer(scan, mode, planes, 0, 1, 0)
    chunk = size // HALVES
    deep, tall = held_a.shape[0] // devices, pieces.shape[0] // devices

    barrier = pltpu.get_barrier_semaphore()
    levels = (z, z + 1 - 2 * lax.rem(z, 2), z + 2 - 4 * (z // 2), 3 - z)
    plane, plane_x, plane_y = y * 2 + x, y * 2 + 1 - x, (1 - y) * 2 + x
    plane_d = (1 - y) * 2 + 1 - x
    everyone = [partner, peer_x, peer_y] + [(levels[k] * 4 + plane, mode) for k in range(1, planes)]
    for peer in everyone:
        pl.semaphore_signal(barrier, inc=1, device_id=peer, device_id_type=MESH)
    own_load = pltpu.make_async_copy(field_hbm.at[mode], field, load.at[3])
    own_load.start()

    def probe_load(m):
        return pltpu.make_async_copy(probe_hbm.at[m], probe.at[m], load_probe.at[m])

    whole = [(left_hbm, left), (right_hbm, right), (measured_hbm, measured)]
    loads = [pltpu.make_async_copy(src, dst, load.at[i]) for i, (src, dst) in enumerate(whole)]
    probe_load(0).start()
    for copy in loads:
        copy.start()
    for m in range(1, modes):
        probe_load(m).start()

    def rows(start, count, step):
        return pl.ds(pl.multiple_of(start, step), count)

    def one_hot(mask):
        return jnp.where(mask, 1.0, 0.0).astype(BF16)

    held, parts_at = (held_a, held_b), (0, held_a.shape[1], width)

    def strip_rows(side, k):
        return rows((side * planes + levels[k]) * deep, deep, deep)

    which = lax.broadcasted_iota(jnp.int32, (deep - strip, width), 0)
    numbers = jnp.where(which == 1, lax.rem(col[0], LANES), col[0] // LANES)
    numbers = jnp.where(which == 0, strip_of[0], numbers).astype(F32)
    own_load.wait()
    own = jnp.concatenate([field[...], numbers]).astype(BF16)
    for i in range(2):
        held[i][strip_rows(plane, 0)] = own[:, parts_at[i] : parts_at[i + 1]]
    pl.semaphore_wait(barrier, len(everyone))

    def remote(src, dst, send_sem, recv_sem, peer):
        return pltpu.make_async_remote_copy(
            src_ref=src, dst_ref=dst, send_sem=send_sem, recv_sem=recv_sem, device_id=peer, device_id_type=MESH
        )

    def number(slot, which, lanes):
        block = held_a[rows(slot * deep + deep - 16, 16, 16), :lanes].astype(F32)
        at = 16 - (deep - strip) + which
        return block[at : at + 1].astype(jnp.int32)

    def hop(kind, i, k, side, peer):
        at = held[i].at[strip_rows(side, k)]
        return remote(at, at, hop_send.at[kind, i, k], hop_recv.at[kind, i, k], peer)

    def hop_z(i, k):
        at = held[i].at[strip_rows(plane, 0)]
        return remote(at, at, hop_send.at[0, i, k], hop_recv.at[0, i, k], (levels[k] * 4 + plane, mode))

    def spread(k):
        for i in range(2):
            hop(1, i, k, plane, peer_x).start()
            hop(2, 1 - i, k, plane, peer_y).start()

    def relay(k):
        hop(1, 0, k, plane_x, peer_x).wait_recv()
        hop(3, 0, k, plane_x, peer_y).start()
        hop(2, 1, k, plane_y, peer_y).wait_recv()
        hop(3, 1, k, plane_y, peer_x).start()

    def absorb(side, first=False, last=False):
        taken = planes * deep
        at = rows(side * taken, taken, taken)
        got = jnp.dot(held_a[at], col_hot[: held_a.shape[1]], preferred_element_type=F32)
        got = got + jnp.dot(held_b[at], col_hot[held_a.shape[1] :], preferred_element_type=F32)
        cut[...] = got.astype(BF16)
        lane = lax.broadcasted_iota(jnp.int32, (1, taken), 1)
        target = jnp.full((1, taken), -1, jnp.int32)
        for j in range(planes):
            ahead = lane - j * deep
            begin = number(side * planes + j, 0, taken) * strip
            target = jnp.where((ahead >= 0) & (ahead < strip), begin + ahead, target)
        target = target - row[0]

        def line_hot(i, carry):
            line = lax.broadcasted_iota(jnp.int32, (64, taken), 0) + i * 64
            row_hot[rows(i * 64, 64, 64)] = one_hot(line == target)
            return carry

        lax.fori_loop(0, size // 64, line_hot, 0)
        for i in range(size // TILE):
            at = pl.ds(i * TILE, TILE)
            piled = jnp.dot(row_hot[at], cut[...], preferred_element_type=F32)
            if not first:
                piled = power[at] + piled
            if last:
                patch[mode, at] = piled.astype(BF16)
                patch_swap(i).start()
            else:
                power[at] = piled

    def patch_swap(i):
        at = rows(i * TILE, TILE, TILE)
        own = patch.at[mode, at]
        return remote(own, own, hop_send.at[4, i, 0], hop_recv.at[4, i, 0], partner)

    def slot_of(j):
        return lax.rem(j, 4) * planes + j // 4

    for k in range(1, planes):
        hop_z(0, k).start()
        hop_z(1, k).start()
    spread(0)

    def column_hot(i, carry):
        at = rows(i * LANES, LANES, LANES)
        lane = lax.broadcasted_iota(jnp.int32, (LANES, size), 1)
        col_hot[at] = one_hot(lax.broadcasted_iota(jnp.int32, (LANES, size), 0) + i * LANES - lane == col[0])
        return carry

    lax.fori_loop(0, width // LANES, column_hot, 0)
    for k in range(1, planes):
        hop(0, 0, k, plane, partner).wait_recv()
        hop(0, 1, k, plane, partner).wait_recv()
        spread(k)
        relay(k - 1)
    relay(planes - 1)
    absorb(plane, first=True)
    for k in range(planes):
        hop(1, 1, k, plane_x, peer_x).wait_recv()
    absorb(plane_x)
    for k in range(planes):
        hop(2, 0, k, plane_y, peer_y).wait_recv()
    absorb(plane_y)
    for k in range(planes):
        hop(3, 0, k, plane_d, peer_y).wait_recv()
        hop(3, 1, k, plane_d, peer_x).wait_recv()
    absorb(plane_d, last=True)
    for copy in loads:
        copy.wait()
    for i in range(size // TILE):
        patch_swap(i).wait_recv()

    def place(u):
        return u // HALVES, u % HALVES * chunk

    near, far_z = levels[1] * 4 + plane, levels[2] * 4 + plane
    along = {"x": (peer_x, x), "y": (peer_y, y), "n": ((near, mode), lax.rem(z, 2)), "f": ((far_z, mode), z // 2)}
    sums, gots = (None, sum1, sum2, sum3), (None, got1, got2, got3, got4)

    def way(u, c, stage):
        axes = ("nfxy", "nfyx")[c] if (u, c) in PLANES_FIRST else ("xynf", "yxnf")[c]
        return along[axes[stage - 1]]

    def base(u, c, stage):
        low = place(u)[1]
        for s in range(1, stage + 1):
            low = low + way(u, c, s)[1] * (chunk >> s)
        return low

    def exchange(u, c, stage):
        m, low = place(u)
        if stage > 4:
            stage = 9 - stage
            count = chunk >> stage
            own = result.at[m, c, rows(base(u, c, stage), count, count)]
            peer, stage = way(u, c, stage)[0], 9 - stage
            return remote(own, own, send.at[stage - 1, u, c], recv.at[stage - 1, u, c], peer)
        peer, bit = way(u, c, stage)
        count = chunk >> stage
        away = (1 - bit) * count
        src = term.at[m, c, rows(low + away, count, count)] if stage == 1 else sums[stage - 1].at[u, c, rows(away, count, count)]
        return remote(src, gots[stage].at[u, c], send.at[stage - 1, u, c], recv.at[stage - 1, u, c], peer)

    def start(stage, u):
        for c in range(2):
            exchange(u, c, stage).start()

    def finish(stage, u):
        m, low = place(u)
        for c in range(2):
            exchange(u, c, stage).wait_recv()
            if stage > 4:
                continue
            count, bit = chunk >> stage, way(u, c, stage)[1]
            if stage == 1:
                mine = term[m, c, rows(low + bit * count, count, count)]
            else:
                mine = sums[stage - 1][u, c, rows(bit * count, count, count)]
            total = (mine.astype(F32) + gots[stage][u, c].astype(F32)).astype(BF16)
            if stage == 4:
                result[m, c, rows(base(u, c, 4), count, count)] = total
            else:
                sums[stage][u, c] = total

    def swap(i):
        at = rows(i * TILE, TILE, TILE)
        return remote(power.at[at], power_in.at[at], swap_send.at[i], swap_recv.at[i], partner)

    def product(table, source):
        out = jnp.dot(table[...], source[...], preferred_element_type=F32)
        half[:, :size] = out[:size].astype(BF16)
        half[:, size:] = out[size:].astype(BF16)

    def part(i):
        at = rows(i * TILE, TILE, TILE)
        return remote(grad.at[1 - mode, at], grad_in.at[at], part_send.at[i], part_recv.at[i], partner)

    mine = rows(scan * tall, tall, 16)

    def piece(k):
        to = lax.rem(scan + k, devices)
        return remote(pieces.at[rows(to * tall, tall, 16)], landed.at[mine], piece_send.at[k - 1], piece_recv.at[k - 1], (to, mode))

    def arrive(k):
        come = lax.rem(scan + devices - k, devices)
        at = rows(come * tall, tall, 16)
        return remote(pieces.at[at], landed.at[at], piece_send.at[k - 1], piece_recv.at[k - 1], (come, mode))

    def strip_swap():
        return remote(strip_grad.at[mode], strip_grad.at[mode], strip_send, strip_recv, partner)

    def cut_pieces():
        for i in range(size // TILE):
            part(i).wait_recv()
            at = pl.ds(i * TILE, TILE)
            summed[at] = (grad[mode, at] + grad_in[at]).astype(BF16)
        down = lax.broadcasted_iota(jnp.int32, (tall, size), 0)
        ahead = lax.broadcasted_iota(jnp.int32, (tall, size), 1) - jnp.where(down < strip, down, down - strip)

        def pick(i, carry):
            begins = [number(slot_of(2 * i + j), 0, size) * strip - row[0] for j in range(2)]
            wave[rows(i * tall, tall, 16)] = one_hot(ahead == jnp.where(down < strip, begins[0], begins[1]))
            return carry

        lax.fori_loop(0, devices // 2, pick, 0)

        def move(i, carry):
            out = jnp.dot(wave[rows(i * 4 * tall, 4 * tall, 16)], summed[...], preferred_element_type=F32)
            for j in range(8):
                block = out[j * strip : (j + 1) * strip]
                block = jnp.concatenate([block[:, : size // 2], block[:, size // 2 :]])
                pieces[rows((i * 8 + j) * tall, tall, 16)] = block.astype(BF16)
            return carry

        lax.fori_loop(0, devices // 8, move, 0)
        landed[mine] = pieces[mine]

    def add_pieces():
        for k in range(1, devices):
            arrive(k).wait_recv()
        strip_grad[mode] = jnp.zeros((strip, width), F32)
        parts = size // LANES
        ahead = lax.broadcasted_iota(jnp.int32, (LANES, 2 * LANES), 1)
        ahead = ahead - lax.broadcasted_iota(jnp.int32, (LANES, 2 * LANES), 0)

        def one(j, carry):
            turn, whole_lanes = one_hot(ahead == number(slot_of(j), 1, 2 * LANES)), number(slot_of(j), 2, LANES)
            piece_rows = landed[rows(j * tall, tall, 16)].astype(F32)
            blocks = jnp.concatenate(
                [
                    piece_rows[b * strip : (b + 1) * strip, at * LANES : (at + 1) * LANES]
                    for b in range(2)
                    for at in range(parts // 2)
                ]
            ).astype(BF16)
            moved = jnp.dot(blocks, turn, preferred_element_type=F32)
            for b in range(parts + 1):
                here = moved[b * strip : (b + 1) * strip, :LANES] if b < parts else 0.0
                if b > 0:
                    here = here + moved[(b - 1) * strip : b * strip, LANES:]
                for t in range((width - size) // LANES + 1):
                    if b + t < width // LANES:
                        to = slice((b + t) * LANES, (b + t + 1) * LANES)
                        strip_grad[mode, :, to] += jnp.where(whole_lanes == t, here, 0.0)
            return carry

        lax.fori_loop(0, devices, one, 0)
        strip_swap().start()

    def forward(m, carry, tile=size):
        probe_load(m).wait()

        def leave(i, carry):
            at, low = rows(i * 64, 64, 64), rows(size + i * 64, 64, 64)
            pr, pi, xr, xi = probe[m, 0, at], probe[m, 1, at], patch[0, at].astype(F32), patch[1, at].astype(F32)
            wave[at] = (pr * xr - pi * xi).astype(BF16)
            wave[low] = (pr * xi + pi * xr).astype(BF16)
            return carry

        lax.fori_loop(0, size // 64, leave, 0)
        product(left, wave)

        for i in range(size // tile):
            at = pl.ds(i * tile, tile)
            both = jnp.dot(half[at], right[...], preferred_element_type=F32)
            re, im = both[:, :size], both[:, size:]
            far[m, 0, at] = re
            far[m, 1, at] = im
            here = re * re + im * im
            power[at] = jnp.where(m == 0, here, power[at] + here)
            if tile == TILE:
                swap(i).start()
        return carry

    lax.fori_loop(0, modes - 1, forward, 0)
    forward(modes - 1, 0, TILE)
    for i in range(size // TILE):
        at = pl.ds(i * TILE, TILE)
        swap(i).wait_recv()
        total = jnp.maximum(power[at] + power_in[at], 0.25)
        scale[at] = 1.0 - measured[at] / jnp.sqrt(total)

    def backward(m):
        def residual(i, carry):
            at, low = rows(i * 64, 64, 64), rows(size + i * 64, 64, 64)
            wave[at] = (far[m, 0, at] * scale[at]).astype(BF16)
            wave[low] = (far[m, 1, at] * scale[at]).astype(BF16)
            return carry

        lax.fori_loop(0, size // 64, residual, 0)
        product(right, wave)

    def across_back(m, i):
        at = pl.ds(i * TILE, TILE)
        both = jnp.dot(half[at], left[...], preferred_element_type=F32)
        br, bi = both[:, :size], both[:, size:]
        pr, pi, xr, xi = probe[m, 0, at], probe[m, 1, at], patch[0, at].astype(F32), patch[1, at].astype(F32)
        term[m, 0, at] = (xr * br + xi * bi).astype(BF16)
        term[m, 1, at] = (xr * bi - xi * br).astype(BF16)
        re, im = pr * br + pi * bi, pr * bi - pi * br
        grad[0, at] = re if m == 0 else grad[0, at] + re
        grad[1, at] = im if m == 0 else grad[1, at] + im
        if m == modes - 1:
            part(i).start()

    for step, u in ORDER:
        if step == 0:
            if u % HALVES == 0:
                backward(u // HALVES)
            across_back(u // HALVES, u % HALVES)
            start(1, u)
        elif step < 8:
            finish(step, u)
            start(step + 1, u)
        elif step == 9:
            cut_pieces()
        elif step == 10:
            piece(u).start()
        else:
            add_pieces()

    for u in range(modes * HALVES):
        finish(8, u)
        for c in range(2):
            for stage in range(1, 9):
                exchange(u, c, stage).wait_send()
    for i in range(size // TILE):
        swap(i).wait_send()
        part(i).wait_send()
    for k in range(1, devices):
        piece(k).wait_send()
    strip_swap().wait()
    for i in range(size // TILE):
        patch_swap(i).wait_send()
    for i in range(2):
        for k in range(planes):
            if k:
                hop_z(i, k).wait_send()
            hop(1, i, k, plane, peer_x).wait_send()
            hop(2, i, k, plane, peer_y).wait_send()
            hop(3, i, k, (plane_x, plane_y)[i], (peer_y, peer_x)[i]).wait_send()


def cast_kernel(summed, strips, wide, strip_grad, block, done, strip_done):
    modes, depth = summed.shape[0], block.shape[0]
    last = pltpu.make_async_copy(strips, strip_grad, strip_done)
    last.start()

    half = block.shape[1]
    count = 2 * modes * (summed.shape[2] // half)

    def at(ref, i):
        return ref.at[i // 4, i // 2 % 2, pl.ds(i % 2 * half, half)]

    def out(i):
        return pltpu.make_async_copy(block.at[i % depth], at(wide, i), done.at[i % depth])

    for i in range(count):
        if i >= depth:
            out(i - depth).wait()
        block[i % depth] = at(summed, i)[...].astype(F32)
        out(i).start()
    for i in range(max(count - depth, 0), count):
        out(i).wait()
    last.wait()


def place_kernel(strips, row, grad, out, padded):
    count, parts, rows, size = out.shape
    padded[...] = jnp.zeros_like(padded)
    padded[:, rows : rows + size, :] = grad[...]

    def one(j, carry):
        start = jnp.clip(strips[j] * rows - row[0], -rows, size) + rows
        base = pl.ds(pl.multiple_of(start // 8 * 8, 8), rows + 8)
        up = lax.rem(rows + 8 - lax.rem(start, 8), rows + 8)
        for k in range(parts):
            out[j, k] = pltpu.roll(padded[k, base, :], up, 0)[:rows]
        return carry

    lax.fori_loop(0, count, one, 0)


def add_kernel(cols, received, out, total):
    count, parts, rows, size = received.shape
    total[...] = jnp.zeros_like(total)
    edge = jnp.zeros((rows, LANES), F32)

    def one(j, carry):
        across = pl.ds(pl.multiple_of(cols[j] // LANES * LANES, LANES), size + LANES)
        shift = lax.rem(cols[j], LANES)
        for k in range(parts):
            piece = jnp.concatenate([received[j, k], edge], axis=1)
            total[k, :, across] += pltpu.roll(piece, shift, 1)
        return carry

    lax.fori_loop(0, count, one, 0)
    out[...] = total[:, :, : out.shape[-1]]


def shards(object_field, probe, amplitude, pos_row, pos_col, strip_of):
    size = probe.shape[-1]
    modes = probe.shape[0]
    rows, cols = object_field.shape[1], object_field.shape[2]
    devices, groups = lax.axis_size("scan"), lax.axis_size("mode")
    padded_cols = cols + LANES
    forward, inverse = dft_tables(size)

    def swap(x):
        return lax.ppermute(x, "mode", [(0, 1), (1, 0)])

    planes, deep = devices // 4, -(-rows // 16) * 16
    fits = groups == 2 and devices == 4 * planes and planes == 4 and size % (64 * HALVES * planes) == 0 and modes * HALVES == 8
    fits = fits and cols % LANES == 0 and size // TILE == 2
    fits = fits and deep - rows >= 8
    fits = fits and 2 * rows % 16 == 0 and size % (2 * LANES) == 0
    if fits and rows % 8 == 0 and devices * deep % TILE == 0 and devices * deep <= 2 * size:
        dma = pltpu.SemaphoreType.DMA
        chunks, chunk = modes * HALVES, size // HALVES
        vmem, lanes = pltpu.VMEM, (cols // LANES + 1) // 2 * LANES
        any_space = pl.BlockSpec(memory_space=pl.ANY)
        term, strip_grad = pl.pallas_call(
            core_kernel,
            out_shape=(vmem((modes, 2, size, size), BF16), vmem((2, rows, cols), F32)),
            in_specs=[SMEM] * 3 + [any_space] * 5,
            out_specs=(VMEM, VMEM),
            scratch_shapes=[
                vmem((rows, cols), F32),
                vmem((devices * deep, lanes), BF16),
                vmem((devices * deep, cols - lanes), BF16),
                vmem((cols, size), BF16),
                vmem((size, planes * deep), BF16),
                vmem((planes * deep, size), BF16),
                vmem((modes, 2, size, size), F32),
                vmem((2, size, size), BF16),
                vmem((size, size), F32),
                vmem((2 * size, 2 * size), BF16),
                vmem((2 * size, 2 * size), BF16),
                vmem((modes, 2, size, size), F32),
                vmem((size, size), F32),
                vmem((size, size), F32),
                vmem((size, size), F32),
                vmem((2 * size, size), BF16),
                vmem((size, 2 * size), BF16),
                vmem((modes, 2, size, size), BF16),
                vmem((chunks, 2, chunk // 2, size), BF16),
                vmem((chunks, 2, chunk // 2, size), BF16),
                vmem((chunks, 2, chunk // 4, size), BF16),
                vmem((chunks, 2, chunk // 4, size), BF16),
                vmem((chunks, 2, chunk // 8, size), BF16),
                vmem((chunks, 2, chunk // 8, size), BF16),
                vmem((chunks, 2, chunk // 16, size), BF16),
                vmem((2, size, size), F32),
                vmem((size, size), F32),
                vmem((size, size), BF16),
                vmem((devices * 2 * rows, size // 2), BF16),
                vmem((devices * 2 * rows, size // 2), BF16),
                dma((4,)),
                dma((modes,)),
                dma((5, 2, planes)),
                dma((5, 2, planes)),
                dma((size // TILE,)),
                dma((size // TILE,)),
                dma((8, chunks, 2)),
                dma((8, chunks, 2)),
                dma((size // TILE,)),
                dma((size // TILE,)),
                dma((devices - 1,)),
                dma((devices - 1,)),
                dma,
                dma,
            ],
            compiler_params=pltpu.CompilerParams(
                vmem_limit_bytes=56 * 1024 * 1024, collective_id=0, has_side_effects=True
            ),
        )(strip_of, pos_row, pos_col, object_field, probe, amplitude[0], forward, inverse)
        probe_grad, strip_grad = pl.pallas_call(
            cast_kernel,
            out_shape=(jax.ShapeDtypeStruct(term.shape, F32), jax.ShapeDtypeStruct(strip_grad.shape, F32)),
            in_specs=[VMEM] * 2,
            out_specs=(any_space, any_space),
            scratch_shapes=[vmem((16, size // 2, size), F32), dma((16,)), dma],
            compiler_params=pltpu.CompilerParams(vmem_limit_bytes=16 * 1024 * 1024),
        )(pltpu.with_memory_space_constraint(term, vmem), pltpu.with_memory_space_constraint(strip_grad, vmem))
        return (strip_grad, probe_grad)

    lane = lax.broadcasted_iota(jnp.int32, (2, META, cols), 2)
    numbers = jnp.where(lane == 0, strip_of[0], jnp.where(lane == 1, pos_col[0] // LANES, pos_col[0] % LANES))
    packed = jnp.concatenate([object_field.astype(BF16), numbers.astype(BF16)], axis=1)
    me = lax.axis_index("mode")
    if groups == 2 and devices % PLANE == 0:
        dma, lines = pltpu.SemaphoreType.DMA, devices // PLANE
        held = pl.pallas_call(
            gather_kernel,
            out_shape=jax.ShapeDtypeStruct((2, devices, rows + META, cols), BF16),
            in_specs=[VMEM],
            out_specs=VMEM,
            scratch_shapes=[
                dma((max(lines - 1, 1),)),
                dma((max(lines - 1, 1),)),
                dma((lines, PLANE - 1)),
                dma((lines, PLANE - 1)),
                dma,
                dma,
            ],
            compiler_params=pltpu.CompilerParams(
                vmem_limit_bytes=56 * 1024 * 1024, collective_id=0, has_side_effects=True
            ),
        )(lax.dynamic_index_in_dim(packed, me, 0, keepdims=False))
    else:
        held = lax.all_gather(packed, "scan", axis=1)
    numbers = held[0, :, rows, :3].astype(jnp.int32)
    strips = numbers[:, 0]
    all_cols = numbers[:, 1] * LANES + numbers[:, 2]

    wave_shape = jax.ShapeDtypeStruct((2, size, size), F32)
    patch = pl.pallas_call(
        cut_kernel,
        out_shape=wave_shape,
        in_specs=[SMEM, SMEM, SMEM, VMEM],
        out_specs=VMEM,
        scratch_shapes=[pltpu.VMEM((2, devices * rows + 8, padded_cols), F32)],
        compiler_params=PARAMS,
    )(strips, pos_row, pos_col, held)

    def whole(*shape):
        return pl.BlockSpec(shape, lambda m: (0,) * len(shape))

    mode_spec = pl.BlockSpec((1, 2, size, size), lambda m: (m, 0, 0, 0))
    table_spec = whole(2 * size, 2 * size)
    buffers = [pltpu.VMEM((2 * size, size), BF16), pltpu.VMEM((size, 2 * size), BF16)]
    far, power = pl.pallas_call(
        forward_kernel,
        grid=(modes,),
        out_shape=(
            jax.ShapeDtypeStruct((modes, 2, size, size), F32),
            jax.ShapeDtypeStruct((size, size), F32),
        ),
        in_specs=[mode_spec, whole(2, size, size), table_spec, table_spec],
        out_specs=(mode_spec, whole(size, size)),
        scratch_shapes=buffers,
        compiler_params=PARAMS,
    )(probe, patch, forward, inverse)
    power = power + swap(power) if groups == 2 else lax.psum(power, "mode")
    term, grad = pl.pallas_call(
        backward_kernel,
        grid=(modes,),
        out_shape=(jax.ShapeDtypeStruct((modes, 2, size, size), BF16), wave_shape),
        in_specs=[
            mode_spec,
            mode_spec,
            whole(2, size, size),
            whole(size, size),
            whole(size, size),
            table_spec,
            table_spec,
        ],
        out_specs=(mode_spec, whole(2, size, size)),
        scratch_shapes=[pltpu.VMEM((size, size), F32)] + buffers,
        compiler_params=PARAMS,
    )(far, probe, patch, amplitude[0], power, inverse, forward)
    probe_grad = lax.psum(term, "scan").astype(F32)

    if groups == 2:
        mine = lax.dynamic_index_in_dim(grad, me, 0, keepdims=True)
        other = lax.dynamic_index_in_dim(grad, 1 - me, 0, keepdims=True)
        grad = mine + swap(other)
    else:
        grad = lax.psum(grad, "mode")
    parts = grad.shape[0]
    pieces = pl.pallas_call(
        place_kernel,
        out_shape=jax.ShapeDtypeStruct((devices, parts, rows, size), F32),
        in_specs=[SMEM, SMEM, VMEM],
        out_specs=VMEM,
        scratch_shapes=[pltpu.VMEM((parts, size + 2 * rows + 8, size), F32)],
        compiler_params=PARAMS,
    )(strips, pos_row, grad)
    received = lax.all_to_all(pieces.astype(BF16), "scan", 0, 0, tiled=False).astype(F32)
    strip_grad = pl.pallas_call(
        add_kernel,
        out_shape=jax.ShapeDtypeStruct((parts, rows, cols), F32),
        in_specs=[SMEM, VMEM],
        out_specs=VMEM,
        scratch_shapes=[pltpu.VMEM((parts, rows, padded_cols), F32)],
        compiler_params=PARAMS,
    )(all_cols, received)
    if groups == 2:
        theirs = swap(strip_grad)
        strip_grad = jnp.where(
            me == 0,
            jnp.concatenate([strip_grad, theirs]),
            jnp.concatenate([theirs, strip_grad]),
        )
    return (strip_grad, probe_grad)


def solution(mesh):
    return jax.shard_map(
        shards,
        mesh=mesh,
        in_specs=(
            P(None, "scan", None),
            P("mode", None, None, None),
            P("scan", None, None),
            P("scan"),
            P("scan"),
            P("scan"),
        ),
        out_specs=(P(None, "scan", None), P("mode", None, None, None)),
        check_vma=False,
    )
```
